512 devices in a mesh: chol: 64 (over y, z_lo, x), pop: 8 (over z_hi, core).
Axes of the slice: x: 4, y: 4, z: 16 (z_hi: 4, z_lo: 4; z = z_hi * 4 + z_lo), core: 2. Of those that a mesh axis runs over, the one named last changes fastest.
Arguments:
- walkers: bfloat16 [32, 640, 160], P('pop', 'chol'), may hold values from -1 to 2
- chol_vectors: bfloat16 [320, 640, 640], P(None, 'chol'), may hold values from -8 to 8
- noise: float32 [2, 32, 320], P(None, 'pop'), may hold values from -5 to 5
- sources: int32 [32], P('pop'), may hold values from 0 to 31
Outputs:
- branched: bfloat16 [32, 640, 160], P('pop', 'chol')
- force_bias: float32 [2, 32, 320], P(None, 'pop', 'chol')
The draws below stay inside these ranges and needn't reach their ends.
Inputs may be any that keep to these rules, and one draw needn't show every extreme that they name: `sources`: a walker id over all populations.
All inputs are finite; a program needn't handle non-finite values.
Results may differ from the reference program's by a relative error of at most 0.015.
Values may be sent and summed in bfloat16 or wider, within the bound.
A program may use at most 64 MiB of HBM per device.

```python
import math
import jax
import jax.numpy as jnp
from jax import lax

NORB = 640
NOCC = 160
NCHOL = 320
STEPS = 2
ORDER = 4
NWALK = 32


def draw_walkers(key, part):
    key = jax.random.fold_in(key, 23)
    values = jnp.clip(jax.random.normal(key, (NWALK, NORB, NOCC), jnp.float32), -4.0, 4.0)
    row_ids = jnp.arange(NORB)[:, None]
    col_ids = jnp.arange(NOCC)[None, :]
    spread = jnp.where(row_ids < NOCC, 0.02, 0.03)
    unit = jnp.where(row_ids == col_ids, 1.0, 0.0)
    return (unit[None] + values * spread[None]).astype(jnp.bfloat16)


def draw_chol_vectors(key, part):
    key = jax.random.fold_in(key, 11)
    key_base, key_diag, key_rows = jax.random.split(key, 3)
    base = jnp.clip(jax.random.normal(key_base, (NCHOL, NORB, NORB), jnp.float32), -4.0, 4.0)
    unit = jnp.eye(NORB, dtype=jnp.float32)[None]
    symmetric = (base + jnp.swapaxes(base, 1, 2)) * 0.70710678 * (10.0 / math.sqrt(NORB * NCHOL)) * (1.0 - unit)
    diag_scale = jnp.clip(jax.random.normal(key_diag, (NCHOL, 1, 1), jnp.float32), -4.0, 4.0) * (0.3 / NOCC)
    row_factor = jax.random.uniform(key_rows, (1, NORB, 1), jnp.float32, 0.5, 1.5)
    return (symmetric + diag_scale * row_factor * unit).astype(jnp.bfloat16)


def set_ends(result, stream_key, low, largest):
    spot = [jax.random.randint(jax.random.fold_in(stream_key, axis), (), 0, length) for axis, length in enumerate(result.shape)]
    main_axis = result.shape.index(max(result.shape))
    beside = spot[:main_axis] + [(spot[main_axis] + 1) % result.shape[main_axis]] + spot[main_axis + 1:]
    return result.at[tuple(spot)].set(low).at[tuple(beside)].set(largest)


def level_of(own_key, extent, shards, least, high):
    factor_of, own = 1.0, jax.random.fold_in(own_key, 6)
    for axis_at, shards_of in shards:
        draws = jnp.exp(jax.random.uniform(jax.random.fold_in(own, axis_at), (shards_of,), jnp.float32, least / len(shards), high / len(shards)))
        factor_of = factor_of * jnp.repeat(draws, extent[axis_at] // shards_of).reshape([-1 if axis == axis_at else 1 for axis in range(len(extent))])
    return factor_of


def bell_draw(rng, extent, width, limit, shards=(), kind=jnp.bfloat16):
    values = jax.random.normal(rng, extent, jnp.float32) * width
    if len(shards) > 0:
        values = level_of(rng, extent, shards, -0.22, 0.18) * values
    return jnp.clip(values, min=-limit, max=limit).astype(kind)


def setup_inputs(seed: int = 0) -> dict:
    seeds = jax.random.split(jax.random.key(seed), 5)
    walkers = draw_walkers(jax.random.fold_in(seeds[4], 71), 0)
    chol_vectors = draw_chol_vectors(jax.random.fold_in(seeds[4], 71), 0)
    noise = bell_draw(seeds[2], (STEPS, NWALK, NCHOL), 1.0, 5.0, ((1, 8),), jnp.float32)
    sources = set_ends(jax.random.randint(seeds[3], (NWALK,), 0, NWALK), jax.random.fold_in(seeds[3], 1), 0, NWALK - 1).astype(jnp.int32)
    return dict(walkers=walkers, chol_vectors=chol_vectors, noise=noise, sources=sources)


SQRT_DT = 0.1

def solve_each(factor, target):
    return jax.scipy.linalg.cho_solve((factor, True), target)

def occupied_inverse(current):
    top_plain = current[:, :NOCC, :]
    gram = jnp.einsum('wai,waj->wij', top_plain.astype(jnp.float32), top_plain.astype(jnp.float32), preferred_element_type=jnp.float32)
    factor = jnp.linalg.cholesky(gram)
    top_rows = top_plain.astype(jnp.float32)
    return jax.vmap(solve_each)(factor, jnp.swapaxes(top_rows, 1, 2))

def reference(walkers, chol_vectors, noise, sources):
    flat_chol = chol_vectors.reshape(NCHOL, NORB * NORB)
    occ_chol = chol_vectors[:, :NOCC, :].reshape(NCHOL, NOCC * NORB)
    current = walkers
    biases = []
    for step_index in range(STEPS):
        phi = current.astype(jnp.float32)
        inverse = occupied_inverse(current)
        theta = jnp.einsum('wja,wab->wjb', phi, inverse, precision=lax.Precision.HIGHEST).astype(jnp.bfloat16)
        green = jnp.swapaxes(theta, 1, 2).reshape(NWALK, NOCC * NORB)
        bias_now = SQRT_DT * lax.dot_general(green.astype(jnp.float32), occ_chol.astype(jnp.float32), (((1,), (1,)), ((), ())), preferred_element_type=jnp.float32)
        biases.append(bias_now)
        field = (noise[step_index] - bias_now).astype(jnp.bfloat16)
        potential = (SQRT_DT * jnp.dot(field.astype(jnp.float32), flat_chol.astype(jnp.float32), preferred_element_type=jnp.float32)).reshape(NWALK, NORB, NORB).astype(jnp.bfloat16)
        total = phi
        term = current
        for order_index in range(1, ORDER + 1):
            product = jnp.einsum('wij,wjb->wib', potential.astype(jnp.float32), term.astype(jnp.float32))
            term = (-product / order_index).astype(jnp.bfloat16)
            total = total + term.astype(jnp.float32)
        current = total.astype(jnp.bfloat16)
    branched = current[sources]
    return (branched, jnp.stack(biases))
```

```python
import functools

import jax
import jax.numpy as jnp
from jax import lax
from jax.experimental import pallas as pl
from jax.experimental.pallas import tpu as pltpu
from jax.sharding import PartitionSpec as P

STEPS = 2
ORDER = 4
SQRT_DT = 0.1
MESH = pl.DeviceIdType.MESH
F32 = jnp.float32
BF16 = jnp.bfloat16
VMEM = pltpu.VMEM
ROWS = 10
PAD = 16
SIDE = 4
LIMIT = 48 * 1024 * 1024


def place():
    d = lax.axis_index("chol")
    return d // 16, (d // 4) % 4, d % 4


def chol_id(y, z, x):
    return {"chol": y * 16 + z * 4 + x}


def others(at):
    return [lax.rem(at + k, SIDE) for k in range(1, SIDE)]


def dot(a, b):
    return lax.dot_general(a, b, (((1,), (0,)), ((), ())), preferred_element_type=F32)


def dot_nt(a, b):
    return lax.dot_general(a, b, (((1,), (1,)), ((), ())), preferred_element_type=F32)


def split(a, parts):
    out = []
    for _ in range(parts):
        head = a.astype(BF16)
        out.append(head)
        a = a - head.astype(F32)
    return out


def greet(peers):
    barrier = pltpu.get_barrier_semaphore()
    for peer in peers:
        pl.semaphore_signal(barrier, inc=1, device_id=peer, device_id_type=MESH)
    pl.semaphore_wait(barrier, len(peers))


def push(src, dst, send, recv, peer):
    copy = pltpu.make_async_remote_copy(
        src_ref=src, dst_ref=dst, send_sem=send, recv_sem=recv, device_id=peer, device_id_type=MESH
    )
    copy.start()
    return copy


def spread(blocks, grid, sems, local_sem):
    send, recv = sems
    y, z, x = place()
    mine = pltpu.make_async_copy(blocks.at[z], grid.at[y, z, x], local_sem)
    mine.start()
    first = [
        push(blocks.at[w], grid.at[y, z, x], send.at[k], recv.at[k], chol_id(y, w, x))
        for k, w in enumerate(others(z))
    ]
    mine.wait()
    for copy in first:
        copy.wait()
    ys, xs = others(y), others(x)
    one, two = pl.ds(0, 2), pl.ds(2, 2)
    along_y = [
        push(grid.at[y, one, x], grid.at[y, one, x], send.at[3 + k], recv.at[3 + k], chol_id(b, z, x))
        for k, b in enumerate(ys)
    ]
    along_x = [
        push(grid.at[y, two, x], grid.at[y, two, x], send.at[6 + k], recv.at[6 + k], chol_id(y, z, b))
        for k, b in enumerate(xs)
    ]
    for copy in along_y:
        copy.wait()
    then_x = [
        push(grid.at[:, one, x], grid.at[:, one, x], send.at[9 + k], recv.at[9 + k], chol_id(y, z, b))
        for k, b in enumerate(xs)
    ]
    for copy in along_x:
        copy.wait()
    then_y = [
        push(grid.at[y, two, :], grid.at[y, two, :], send.at[12 + k], recv.at[12 + k], chol_id(b, z, x))
        for k, b in enumerate(ys)
    ]
    for copy in then_x + then_y:
        copy.wait()


def compact(grid, out, width):
    rows = lax.broadcasted_iota(jnp.int32, (8 * ROWS, 8 * PAD), 0)
    cols = lax.broadcasted_iota(jnp.int32, (8 * ROWS, 8 * PAD), 1)
    pick = (rows == (cols // PAD) * ROWS + cols % PAD) & (cols % PAD < ROWS)
    pick = jnp.where(pick, 1.0, 0.0).astype(BF16)
    for part in range(8):
        piece = grid[part // 2, 2 * (part % 2) : 2 * (part % 2) + 2].reshape(8 * PAD, grid.shape[-1])
        kept = dot(pick, piece).astype(BF16)
        out[8 * ROWS * part : 8 * ROWS * (part + 1), :] = kept[:, :width]


def cube_peers():
    y, z, x = place()
    return (
        [chol_id(y, b, x) for b in others(z)]
        + [chol_id(b, z, x) for b in others(y)]
        + [chol_id(y, z, b) for b in others(x)]
    )


def gather_kernel(blocks, phi, grid, send, recv, local_sem):
    greet(cube_peers())
    spread(blocks, grid, (send, recv), local_sem)
    compact(grid, phi, phi.shape[1])


def gather(blocks, occ):
    lanes = blocks.shape[2]
    return pl.pallas_call(
        gather_kernel,
        out_shape=jax.ShapeDtypeStruct((64 * ROWS, occ), BF16),
        in_specs=[pl.BlockSpec(memory_space=VMEM)],
        out_specs=pl.BlockSpec(memory_space=VMEM),
        scratch_shapes=[
            VMEM((SIDE, SIDE, SIDE, PAD, lanes), BF16),
            pltpu.SemaphoreType.DMA((15,)),
            pltpu.SemaphoreType.DMA((15,)),
            pltpu.SemaphoreType.DMA,
        ],
        compiler_params=pltpu.CompilerParams(collective_id=0, has_side_effects=True, vmem_limit_bytes=LIMIT),
        name="gather_walkers",
    )(blocks)


def theta_kernel(phi, out):
    orb, occ = phi.shape
    _, _, x = place()
    top = phi[:occ, :]
    rows = lax.broadcasted_iota(jnp.int32, (occ, occ), 0)
    cols = lax.broadcasted_iota(jnp.int32, (occ, occ), 1)
    eye = jnp.where(rows == cols, 1.0, 0.0).astype(F32)
    gram = dot_nt(top, top)
    scale = 1.0 / jnp.max(jnp.sum(jnp.abs(gram), axis=1, keepdims=True), axis=0, keepdims=True)
    start = top.astype(F32) * scale

    inv = 2.0 * start - dot((gram * (scale * scale)).astype(BF16), top)
    for _ in range(6):
        near = inv.astype(BF16)
        inv = 2.0 * inv - dot(dot_nt(near, top).astype(BF16), near)

    def miss_of(guess):
        return eye - sum(dot_nt(part, top) for part in split(guess, 3)[::-1])

    def size_of(miss):
        return jnp.sum(miss * miss)

    miss = miss_of(inv)
    size = size_of(miss)
    good = size < 0.5
    inv = jnp.where(good, inv, start)

    def more(state):
        count, size, _ = state
        return (count < 64) & jnp.logical_not(size < 1e-7)

    def refine(state):
        count, _, guess = state
        miss = miss_of(guess)
        m_hi, m_lo = split(miss, 2)
        g_hi, g_lo = split(guess, 2)
        guess = guess + (dot(m_lo, g_hi) + dot(m_hi, g_lo) + dot(m_hi, g_hi))
        return count + 1, size_of(miss), guess

    _, _, inv = lax.while_loop(more, refine, (0, jnp.float32(1.0), inv))

    sel_rows = lax.broadcasted_iota(jnp.int32, (SIDE * PAD, occ), 0)
    sel_cols = lax.broadcasted_iota(jnp.int32, (SIDE * PAD, occ), 1)
    r = sel_rows % PAD
    sel = (sel_cols == ((sel_rows // PAD) * SIDE + x) * ROWS + r) & (r < ROWS)
    sel = jnp.where(sel, 1.0, 0.0).astype(BF16)
    picked = [dot(sel, part).astype(BF16) for part in split(inv, 2)]
    theta = dot_nt(picked[1], phi[...]) + dot_nt(picked[0], phi[...])
    out[...] = theta.astype(BF16).reshape(SIDE, PAD, orb)


def theta_of(phi):
    orb, _ = phi.shape
    return pl.pallas_call(
        theta_kernel,
        out_shape=jax.ShapeDtypeStruct((SIDE, PAD, orb), BF16),
        in_specs=[pl.BlockSpec(memory_space=VMEM)],
        out_specs=pl.BlockSpec(memory_space=VMEM),
        compiler_params=pltpu.CompilerParams(vmem_limit_bytes=LIMIT),
        name="occupied_inverse_theta",
    )(phi)


def step_kernel(
    theta, chol_hbm, noise, phi, current, bias,
    chol, slab_theta, parts, total, blocks, grid, pot, send, recv, bias_send, bias_recv, local_sem, chol_sem,
):
    y, z, x = place()
    vecs, orb = chol.shape[1:]
    load = pltpu.make_async_copy(chol_hbm, chol, chol_sem)
    load.start()
    slab = z * SIDE + x

    barrier = pltpu.get_barrier_semaphore()

    @pl.when(y == 0)
    def _():
        plane = [lax.rem(slab + k, 16) for k in range(1, 16)]
        for peer in [{"chol": p} for p in plane] + [chol_id(b, z, x) for b in range(1, SIDE)]:
            pl.semaphore_signal(barrier, inc=1, device_id=peer, device_id_type=MESH)
        pl.semaphore_wait(barrier, 18)

        own = pltpu.make_async_copy(theta.at[z], slab_theta.at[z], local_sem)
        own.start()
        moves = [
            push(theta.at[b], slab_theta.at[z], send.at[k], recv.at[k], chol_id(0, b, x))
            for k, b in enumerate(others(z))
        ]
        own.wait()
        for move in moves:
            move.wait()
        load.wait()
        green = slab_theta[...].reshape(SIDE * PAD, orb)
        green_row = lax.broadcasted_iota(jnp.int32, green.shape, 0) % PAD

        def one_row(r, acc):
            return acc + dot_nt(jnp.where(green_row == r, green, jnp.zeros_like(green)), chol[r])

        acc = lax.fori_loop(0, ROWS, one_row, jnp.zeros((SIDE * PAD, vecs), F32))
        parts[slab] = jnp.sum(acc.reshape(SIDE, PAD, vecs), axis=1)
        moves = [
            push(parts.at[slab], parts.at[slab], bias_send.at[k], bias_recv.at[k], {"chol": p})
            for k, p in enumerate(plane)
        ]
        for move in moves:
            move.wait()
        total[...] = SQRT_DT * jnp.sum(parts[...], axis=0)
        moves = [
            push(total, total, bias_send.at[15 + k], bias_recv.at[15], chol_id(b + 1, z, x)) for k, b in enumerate(range(3))
        ]
        for move in moves:
            move.wait_send()

    @pl.when(y != 0)
    def _():
        for peer in cube_peers():
            pl.semaphore_signal(barrier, inc=1, device_id=peer, device_id_type=MESH)
        pl.semaphore_wait(barrier, 9)
        load.wait()
        pltpu.make_async_copy(total, total, bias_recv.at[15]).wait()

    bias[...] = total[...]
    field = (noise[...] - total[...]).astype(BF16).astype(F32)
    field = jnp.broadcast_to(field[:, None, :], (SIDE, PAD, vecs)).reshape(SIDE * PAD, vecs).astype(BF16)
    field_row = lax.broadcasted_iota(jnp.int32, field.shape, 0) % PAD

    def one_slab(r, acc):
        return acc + dot(jnp.where(field_row == r, field, jnp.zeros_like(field)), chol[r])

    acc = lax.fori_loop(0, ROWS, one_slab, jnp.zeros((SIDE * PAD, orb), F32))
    blocks[...] = (SQRT_DT * acc).astype(BF16).reshape(SIDE, PAD, orb)
    spread(blocks, grid, (send.at[pl.ds(3, 15)], recv.at[pl.ds(3, 15)]), local_sem)
    compact(grid, pot, orb)

    term = phi[...]
    sum_of = term.astype(F32)
    for order in range(1, ORDER + 1):
        term = (-dot(pot[...], term) / order).astype(BF16)
        sum_of = sum_of + term.astype(F32)
    current[...] = sum_of.astype(BF16)


def step(theta, chol, noise, phi):
    rows, vecs, orb = chol.shape
    occ = phi.shape[1]
    dma = pltpu.SemaphoreType.DMA
    vmem = pl.BlockSpec(memory_space=VMEM)
    return pl.pallas_call(
        step_kernel,
        out_shape=(
            jax.ShapeDtypeStruct((orb, occ), BF16),
            jax.ShapeDtypeStruct((SIDE, vecs), F32),
        ),
        in_specs=[vmem, pl.BlockSpec(memory_space=pl.ANY), vmem, vmem],
        out_specs=(vmem, vmem),
        scratch_shapes=[
            VMEM((rows, vecs, orb), BF16),
            VMEM((SIDE, PAD, orb), BF16),
            VMEM((16, SIDE, vecs), F32),
            VMEM((SIDE, vecs), F32),
            VMEM((SIDE, PAD, orb), BF16),
            VMEM((SIDE, SIDE, SIDE, PAD, orb), BF16),
            VMEM((orb, orb), BF16),
            dma((18,)),
            dma((18,)),
            dma((18,)),
            dma((16,)),
            dma,
            dma,
        ],
        compiler_params=pltpu.CompilerParams(collective_id=1, has_side_effects=True, vmem_limit_bytes=LIMIT),
        name="propagation_step",
    )(theta, chol, noise, phi)


def branch_kernel(sources, phi, out, blocks, everyone, send, recv, local_sem):
    y, z, x = place()
    pop = lax.axis_index("pop")
    pops = [lax.rem(pop + k, 8) for k in range(1, 8)]
    greet([chol_id(y, b, x) for b in others(z)] + [{"pop": p} for p in pops])
    orb, occ = phi.shape
    rows = lax.broadcasted_iota(jnp.int32, (SIDE * PAD, orb), 0)
    cols = lax.broadcasted_iota(jnp.int32, (SIDE * PAD, orb), 1)
    r = rows % PAD
    sel = (cols == (y * 16 + (rows // PAD) * SIDE + x) * ROWS + r) & (r < ROWS)
    picked = dot(jnp.where(sel, 1.0, 0.0).astype(BF16), phi[...]).astype(BF16)
    blocks[...] = picked.reshape(SIDE, PAD, occ)
    own = pltpu.make_async_copy(blocks.at[z], everyone.at[pop, z], local_sem)
    own.start()
    moves = [
        push(blocks.at[b], everyone.at[pop, z], send.at[k], recv.at[k], chol_id(y, b, x))
        for k, b in enumerate(others(z))
    ]
    own.wait()
    for move in moves:
        move.wait()
    moves = [
        push(everyone.at[pop], everyone.at[pop], send.at[3 + k], recv.at[3 + k], {"pop": p}) for k, p in enumerate(pops)
    ]
    for move in moves:
        move.wait()
    for slot in range(SIDE):
        source = sources[slot]
        out[slot] = everyone[source // SIDE, source % SIDE]


def branch(sources, phi):
    occ = phi.shape[1]
    dma = pltpu.SemaphoreType.DMA
    return pl.pallas_call(
        branch_kernel,
        out_shape=jax.ShapeDtypeStruct((SIDE, PAD, occ), BF16),
        in_specs=[pl.BlockSpec(memory_space=pltpu.SMEM), pl.BlockSpec(memory_space=VMEM)],
        out_specs=pl.BlockSpec(memory_space=VMEM),
        scratch_shapes=[
            VMEM((SIDE, PAD, occ), BF16),
            VMEM((8, SIDE, PAD, occ), BF16),
            dma((10,)),
            dma((10,)),
            dma,
        ],
        compiler_params=pltpu.CompilerParams(collective_id=2, has_side_effects=True, vmem_limit_bytes=LIMIT),
        name="branch_walkers",
    )(sources, phi)


def local(walkers, chol_vectors, noise, sources):
    _, row_count, occ = walkers.shape
    vec_count = chol_vectors.shape[0]
    chol = jnp.transpose(chol_vectors, (1, 0, 2))
    blocks = jnp.pad(walkers, ((0, 0), (0, PAD - row_count), (0, 256 - occ)))
    phi = gather(blocks, occ)
    biases = []
    for index in range(STEPS):
        phi, bias = step(theta_of(phi), chol, noise[index], phi)
        biases.append(bias)
    branched = branch(sources, phi)[:, :row_count, :]
    share = vec_count // lax.axis_size("chol")
    stacked = jnp.stack(biases)
    bias_share = lax.dynamic_slice_in_dim(stacked, lax.axis_index("chol") * share, share, 2)
    return branched, bias_share


def solution(mesh):
    return jax.shard_map(
        local,
        mesh=mesh,
        in_specs=(P("pop", "chol", None), P(None, "chol", None), P(None, "pop", None), P("pop")),
        out_specs=(P("pop", "chol", None), P(None, "pop", "chol")),
        check_vma=False,
    )
```

```python
import jax
import jax.numpy as jnp
from jax import lax
from jax.experimental import pallas as pl
from jax.experimental.pallas import tpu as pltpu
from jax.sharding import PartitionSpec as P

STEPS = 2
ORDER = 4
SQRT_DT = 0.1
MESH = pl.DeviceIdType.MESH
F32 = jnp.float32
BF16 = jnp.bfloat16
VMEM = pltpu.VMEM
ROWS = 10
PAD = 16
SIDE = 4
MAIN = 512
LANES = 128
FLAG = 15
NEWTON = ((0.05, 5), (0.001, 8))
REFINE = 2
MISS = 1e-3
LIMIT = 60 * 1024 * 1024


def dot(a, b):
    return lax.dot_general(a, b, (((1,), (0,)), ((), ())), preferred_element_type=F32)


def dot_nt(a, b):
    return lax.dot_general(a, b, (((1,), (1,)), ((), ())), preferred_element_type=F32)


def split(a):
    head = a.astype(BF16)
    return head, (a - head.astype(F32)).astype(BF16)


def index(shape, axis):
    return lax.broadcasted_iota(jnp.int32, shape, axis)


def one_hot(mask):
    return jnp.where(mask, 1.0, 0.0).astype(BF16)


def chol_id(y, z, x):
    return {"chol": y * 16 + z * 4 + x}


def others(at):
    return [lax.rem(at + k, SIDE) for k in range(1, SIDE)]


def remote(src, dst, send, recv, peer):
    return pltpu.make_async_remote_copy(
        src_ref=src, dst_ref=dst, send_sem=send, recv_sem=recv, device_id=peer, device_id_type=MESH
    )


def start(copies):
    for copy in copies:
        copy.start()


def received(copies):
    for copy in copies:
        copy.wait_recv()


def sent(copies):
    for copy in copies:
        copy.wait_send()


def spread(at, blocks, grid, send, recv, local_sem):
    y, z, x = at
    ys, xs = others(y), others(x)
    one, two = pl.ds(0, 2), pl.ds(2, 2)

    def along(spot, axis, base):
        peers = [chol_id(b, z, x) for b in ys] if axis == 0 else [chol_id(y, z, b) for b in xs]
        return [remote(grid.at[spot], grid.at[spot], send.at[base + k], recv.at[base + k], p) for k, p in enumerate(peers)]

    mine = pltpu.make_async_copy(blocks.at[z], grid.at[y, z, x], local_sem)
    first = [
        remote(blocks.at[w], grid.at[y, z, x], send.at[k], recv.at[k], chol_id(y, w, x)) for k, w in enumerate(others(z))
    ]
    start(first)
    mine.start()
    mine.wait()
    received(first)
    along_y = along((y, one, x), 0, 3)
    along_x = along((y, two, x), 1, 6)
    start(along_y + along_x)
    received(along_y)
    then_x = along((slice(None), one, x), 1, 9)
    start(then_x)
    received(along_x)
    then_y = along((y, two, slice(None)), 0, 12)
    start(then_y)
    sent(first + along_y + along_x)
    received(then_x + then_y)
    return then_x + then_y


def eight(grid, part):
    return grid[part // 2, 2 * (part % 2) : 2 * (part % 2) + 2].reshape(8 * PAD, grid.shape[-1])


def pick_rows():
    shape = (8 * ROWS, 8 * PAD)
    row, col = index(shape, 0), index(shape, 1)
    same = row // ROWS == col // PAD
    return row % ROWS, col % PAD, same


def compact(grid, out):
    row, col, same = pick_rows()
    pick = one_hot(same & (row == col))
    for part in range(8):
        kept = dot(pick, eight(grid, part)).astype(BF16)
        out[8 * ROWS * part : 8 * ROWS * (part + 1), :] = kept


def compact_packed(grid, out):
    row, col, same = pick_rows()
    pick = one_hot(same & (row == col))
    rest = [one_hot(same & (col == ROWS + row // 4) & (row % 4 == s)) for s in range(4)]
    for part in range(8):
        piece = eight(grid, part)
        rows = pl.ds(8 * ROWS * part, 8 * ROWS)
        out[rows, :MAIN] = dot(pick, piece).astype(BF16)
        tail = sum(dot(rest[s], piece[:, LANES * s : LANES * (s + 1)]) for s in range(4))
        out[rows, MAIN:] = tail.astype(BF16)


def theta_rows(phi, out, x, tuned, products):
    orb, occ = phi.shape
    top = phi[:occ, :]
    gram = dot_nt(top, top)
    scale = 0.999 / jnp.max(jnp.sum(jnp.abs(gram), axis=1, keepdims=True), axis=0, keepdims=True)
    inv, square = top.astype(F32) * scale, gram * scale
    least = tuned
    for turn in range(products):
        c = 2.0 / (1.0 + least)
        least = 1.0 - ((1.0 - least) / (1.0 + least)) ** 2
        near = inv.astype(BF16)
        if turn > 0:
            square = dot_nt(near, top)
        inv = (2.0 * c) * inv - (c * c) * dot(square.astype(BF16), near)
    eye = jnp.where(index((occ, occ), 0) == index((occ, occ), 1), 1.0, 0.0)
    for _ in range(REFINE):
        head, rest = split(inv)
        miss = eye - (dot_nt(rest, top) + dot_nt(head, top))
        inv = inv + dot(miss.astype(BF16), head)
    size = jnp.sum(jnp.sum(miss * miss, axis=1, keepdims=True), axis=0, keepdims=True)

    shape = (SIDE * PAD, occ)
    row, col = index(shape, 0), index(shape, 1)
    sel = one_hot((col == (row // PAD * SIDE + x) * ROWS + row % PAD) & (row % PAD < ROWS))
    head, rest = [dot(sel, part).astype(BF16) for part in split(inv)]
    theta = dot_nt(rest, phi[...]) + dot_nt(head, phi[...])
    out[...] = theta.astype(BF16).reshape(SIDE, PAD, orb)
    return jnp.where(size < MISS, 0.0, 1.0)


def bias_rows(green, chol):
    rows, vecs, _ = chol.shape
    row = index(green.shape, 0) % PAD
    acc = sum(dot_nt(jnp.where(row == r, green, jnp.zeros_like(green)), chol[r]) for r in range(rows))
    return jnp.sum(acc.reshape(SIDE, PAD, vecs), axis=1)


def potential_blocks(field, chol, blocks):
    rows, vecs, _ = chol.shape
    field = field.astype(BF16).astype(F32)
    field = jnp.broadcast_to(field[:, None, :], (SIDE, PAD, vecs)).reshape(SIDE * PAD, vecs).astype(BF16)
    row = index(field.shape, 0) % PAD
    none = jnp.zeros_like(field)
    main = sum(dot(jnp.where(row == r, field, none), chol[r, :, :MAIN]) for r in range(rows))
    for s in range(4):
        tail = sum(dot(jnp.where(row == ROWS + r // 4, field, none), chol[r, :, MAIN:]) for r in range(s, rows, 4))
        lanes = slice(LANES * s, LANES * (s + 1))
        blocks[:, :, lanes] = (SQRT_DT * (main[:, lanes] + tail)).astype(BF16).reshape(SIDE, PAD, LANES)


def pack_walker(phi, blocks, y, x, missed):
    orb, occ = phi.shape
    shape = (SIDE * PAD, orb)
    row, col = index(shape, 0), index(shape, 1)
    base, r = (y * 16 + row // PAD * SIDE + x) * ROWS, row % PAD
    whole = dot(one_hot((col == base + r) & (r < ROWS)), phi[:, :LANES])
    rest = occ - LANES
    copies = dot(phi[:, LANES:], one_hot(index((rest, LANES), 0) == index((rest, LANES), 1) % rest)).astype(BF16)
    lane = index((SIDE * PAD, LANES), 1) // rest
    for s in range(4):
        at = 4 * (r - ROWS) + s
        tail = dot(one_hot((col == base + at) & (at >= 0) & (at < ROWS)), copies)
        whole = whole + jnp.where(lane == s, tail, 0.0)
    whole = jnp.where(index(whole.shape, 0) % PAD == FLAG, missed, whole)
    blocks[...] = whole.astype(BF16).reshape(SIDE, PAD, LANES)


def kernel(
    walkers, chol_hbm, noise, sources, out, bias, missed_out,
    chol, first_grid, phi, theta, slab_theta, parts, total, blocks, grid, pot, packed, everyone,
    send0, recv0, send, recv, bias_send, bias_recv, last_send, last_recv, local_sem, chol_sem,
):
    d, pop = lax.axis_index("chol"), lax.axis_index("pop")
    y, z, x = at = d // 16, (d // 4) % 4, d % 4
    slab = z * SIDE + x
    hi, core = pop // 2, pop % 2
    load = pltpu.make_async_copy(chol_hbm, chol, chol_sem)
    load.start()

    ring = []
    for k in range(1, 16):
        place = lax.rem(hi * 4 + z + k, 16)
        ring.append((place // 4, place % 4))
    twin = {"pop": hi * 2 + 1 - core}
    ring_peers = [{"chol": y * 16 + b * 4 + x, "pop": h * 2 + core} for h, b in ring]
    plane = [{"chol": lax.rem(slab + k, 16)} for k in range(1, 16)]
    y_peers = [chol_id(b, z, x) for b in others(y)]
    x_peers = [chol_id(y, z, b) for b in others(x)]

    barrier = pltpu.get_barrier_semaphore()

    def greet(peers):
        for peer in peers:
            pl.semaphore_signal(barrier, inc=1, device_id=peer, device_id_type=MESH)

    greet(ring_peers + [twin] + y_peers + x_peers)

    @pl.when(y == 0)
    def _():
        greet([chol_id(0, b, c) for b in others(z) for c in others(x)])
        pl.semaphore_wait(barrier, 31)

    @pl.when(y != 0)
    def _():
        pl.semaphore_wait(barrier, 22)

    last = spread(at, walkers, first_grid, send0, recv0, local_sem)
    compact(first_grid, phi)
    sent(last)

    missed = jnp.zeros((1, 1), F32)
    for s in range(STEPS):
        tuned, products = NEWTON[s]
        missed = missed + theta_rows(phi, theta.at[s], x, tuned, products)

        to_slab = [
            remote(theta.at[s, b], slab_theta.at[s, z], send.at[s, k], recv.at[s, k], chol_id(0, b, x))
            for k, b in enumerate(others(z))
        ]
        to_plane = [
            remote(parts.at[s, slab], parts.at[s, slab], bias_send.at[s, k], bias_recv.at[s, k], p)
            for k, p in enumerate(plane)
        ]
        to_rows = [
            remote(total.at[s], total.at[s], bias_send.at[s, 15 + k], bias_recv.at[s, 15], chol_id(1 + k, z, x))
            for k in range(3)
        ]

        @pl.when(y == 0)
        def _():
            start(to_slab)
            own = pltpu.make_async_copy(theta.at[s, z], slab_theta.at[s, z], local_sem)
            own.start()
            own.wait()
            if s == 0:
                load.wait()
            received(to_slab)
            parts[s, slab] = bias_rows(slab_theta[s].reshape(SIDE * PAD, chol.shape[2]), chol)
            start(to_plane)
            received(to_plane)
            total[s] = SQRT_DT * jnp.sum(parts[s], axis=0)
            start(to_rows)

        @pl.when(y != 0)
        def _():
            if s == 0:
                load.wait()
            to_rows[0].wait_recv()

        bias[s] = total[s]
        potential_blocks(noise[s] - total[s], chol, blocks.at[s])

        @pl.when(y == 0)
        def _():
            sent(to_slab + to_plane + to_rows)

        last = spread(at, blocks.at[s], grid.at[s], send.at[s, pl.ds(3, 15)], recv.at[s, pl.ds(3, 15)], local_sem)
        compact_packed(grid.at[s], pot)
        sent(last)

        term = phi[...]
        sum_of = term.astype(F32)
        for order in range(1, ORDER + 1):
            term = (-dot(pot[...], term) / order).astype(BF16)
            sum_of = sum_of + term.astype(F32)
        phi[...] = sum_of.astype(BF16)

    pack_walker(phi, packed, y, x, missed)
    spot = everyone.at[hi, core, z]
    to_ring = [
        remote(packed.at[b], spot, last_send.at[k], last_recv.at[k], peer)
        for k, ((_, b), peer) in enumerate(zip(ring, ring_peers, strict=True))
    ]
    start(to_ring)
    own = pltpu.make_async_copy(packed.at[z], spot, local_sem)
    own.start()
    own.wait()
    received(to_ring)
    mine = everyone.at[:, core]
    to_twin = [remote(mine, mine, last_send.at[15], last_recv.at[15], twin)]
    start(to_twin)
    sent(to_ring)
    received(to_twin)

    chosen = []
    for slot in range(SIDE):
        source = sources[slot]
        chosen.append(everyone[source // 8, source // 4 % 2, source % 4])
    whole = jnp.concatenate(chosen, axis=0)
    out[:, :, :LANES] = whole.reshape(SIDE, PAD, LANES)
    rest = out.shape[2] - LANES
    shape = (SIDE * PAD, SIDE * PAD)
    row, col = index(shape, 0), index(shape, 1)
    r = row % PAD
    back = one_hot(index((LANES, rest), 0) % rest == index((LANES, rest), 1))
    lane = index((SIDE * PAD, LANES), 1) // rest
    tail = jnp.zeros((SIDE * PAD, LANES), F32)
    for s in range(4):
        pick = one_hot((row // PAD == col // PAD) & (col % PAD == ROWS + r // 4) & (r % 4 == s) & (r < ROWS))
        tail = tail + jnp.where(lane == s, dot(pick, whole), 0.0)
    out[:, :, LANES:] = dot(tail.astype(BF16), back).astype(BF16).reshape(SIDE, PAD, rest)
    flags = everyone[...].reshape(8 * SIDE, PAD, LANES).astype(F32)
    bad = jnp.where((index(flags.shape, 1) == FLAG) & jnp.logical_not(flags == 0.0), 1.0, 0.0)
    missed_out[...] = jnp.max(jnp.max(bad, axis=0), axis=0, keepdims=True)
    sent(to_twin)


def propagate(walkers, chol, noise, sources):
    rows, vecs, orb = chol.shape
    occ = walkers.shape[2]
    dma = pltpu.SemaphoreType.DMA
    vmem = pl.BlockSpec(memory_space=VMEM)
    return pl.pallas_call(
        kernel,
        out_shape=(
            jax.ShapeDtypeStruct((SIDE, PAD, occ), BF16),
            jax.ShapeDtypeStruct((STEPS, SIDE, vecs), F32),
            jax.ShapeDtypeStruct((1, LANES), F32),
        ),
        in_specs=[vmem, pl.BlockSpec(memory_space=pl.ANY), vmem, pl.BlockSpec(memory_space=pltpu.SMEM)],
        out_specs=(vmem, vmem, vmem),
        scratch_shapes=[
            VMEM((rows, vecs, orb), BF16),
            VMEM((SIDE, SIDE, SIDE, PAD, occ), BF16),
            VMEM((orb, occ), BF16),
            VMEM((STEPS, SIDE, PAD, orb), BF16),
            VMEM((STEPS, SIDE, PAD, orb), BF16),
            VMEM((STEPS, 16, SIDE, vecs), F32),
            VMEM((STEPS, SIDE, vecs), F32),
            VMEM((STEPS, SIDE, PAD, MAIN), BF16),
            VMEM((STEPS, SIDE, SIDE, SIDE, PAD, MAIN), BF16),
            VMEM((orb, orb), BF16),
            VMEM((SIDE, PAD, LANES), BF16),
            VMEM((SIDE, 2, SIDE, PAD, LANES), BF16),
            dma((15,)),
            dma((15,)),
            dma((STEPS, 18)),
            dma((STEPS, 18)),
            dma((STEPS, 18)),
            dma((STEPS, 16)),
            dma((16,)),
            dma((16,)),
            dma,
            dma,
        ],
        compiler_params=pltpu.CompilerParams(collective_id=0, has_side_effects=True, vmem_limit_bytes=LIMIT),
        name="propagate",
    )(walkers, chol, noise, sources)


def solve_each(factor, target):
    return jax.scipy.linalg.cho_solve((factor, True), target)


def by_cholesky(walkers, chol_vectors, noise, sources):
    walk_count, row_count, occ_count = walkers.shape
    vec_count, _, orb_count = chol_vectors.shape
    first_row = lax.axis_index("chol") * row_count
    flat_chol = chol_vectors.reshape(vec_count, row_count * orb_count)
    current = walkers
    biases = []
    for step_index in range(STEPS):
        gathered = lax.all_gather(current, "chol", axis=1, tiled=True)
        phi = gathered.astype(F32)
        top_plain = gathered[:, :occ_count, :]
        gram = jnp.einsum("wai,waj->wij", top_plain, top_plain, preferred_element_type=F32)
        factor = jnp.linalg.cholesky(gram)
        inverse = jax.vmap(solve_each)(factor, jnp.swapaxes(phi[:, :occ_count, :], 1, 2))
        inverse_wide = jnp.pad(inverse, ((0, 0), (0, 0), (0, orb_count - occ_count)))
        inverse_cols = lax.dynamic_slice_in_dim(inverse_wide, first_row, row_count, 2)
        theta_slab = jnp.einsum("wja,wai->wji", phi, inverse_cols, precision=lax.Precision.HIGHEST).astype(BF16)
        green = jnp.swapaxes(theta_slab, 1, 2).reshape(walk_count, row_count * orb_count)
        partial_bias = lax.dot_general(green, flat_chol, (((1,), (1,)), ((), ())), preferred_element_type=F32)
        bias_now = SQRT_DT * lax.psum(partial_bias, "chol")
        biases.append(bias_now)
        field = (noise[step_index] - bias_now).astype(BF16)
        potential = SQRT_DT * jnp.dot(field, flat_chol, preferred_element_type=F32)
        potential = potential.reshape(walk_count, row_count, orb_count).astype(BF16)
        total = current.astype(F32)
        term = current
        for order in range(1, ORDER + 1):
            whole = gathered if order == 1 else lax.all_gather(term, "chol", axis=1, tiled=True)
            product = jnp.einsum("wij,wjb->wib", potential, whole, preferred_element_type=F32)
            term = (-product / order).astype(BF16)
            total = total + term.astype(F32)
        current = total.astype(BF16)
    everyone = lax.all_gather(current, "pop", axis=0, tiled=True)
    return everyone[sources], jnp.stack(biases)


def local(walkers, chol_vectors, noise, sources):
    _, row_count, _ = walkers.shape
    vec_count = chol_vectors.shape[0]
    padded = jnp.pad(walkers, ((0, 0), (0, PAD - row_count), (0, 0)))
    branched, bias, missed = propagate(padded, jnp.transpose(chol_vectors, (1, 0, 2)), noise, sources)
    branched, bias = lax.cond(
        missed[0, 0] == 0.0,
        lambda: (branched[:, :row_count, :], bias),
        lambda: by_cholesky(walkers, chol_vectors, noise, sources),
    )
    share = vec_count // lax.axis_size("chol")
    bias_share = lax.dynamic_slice_in_dim(bias, lax.axis_index("chol") * share, share, 2)
    return branched, bias_share


def solution(mesh):
    return jax.shard_map(
        local,
        mesh=mesh,
        in_specs=(P("pop", "chol", None), P(None, "chol", None), P(None, "pop", None), P("pop")),
        out_specs=(P("pop", "chol", None), P(None, "pop", "chol")),
        check_vma=False,
    )
```

```python
import jax
import jax.numpy as jnp
from jax import lax
from jax.experimental import pallas as pl
from jax.experimental.pallas import tpu as pltpu
from jax.sharding import PartitionSpec as P

STEPS = 2
ORDER = 4
SQRT_DT = 0.1
MESH = pl.DeviceIdType.MESH
F32 = jnp.float32
BF16 = jnp.bfloat16
VMEM = pltpu.VMEM
ROWS = 10
PAD = 16
SIDE = 4
HALF = 256
LANES = 128
FLAGS = 384
FLAG = 15
NEWTON = ((0.05, 5), (0.001, 8))
REFINE = 2
MISS = 1e-3
LIMIT = 60 * 1024 * 1024


def dot(a, b):
    return lax.dot_general(a, b, (((1,), (0,)), ((), ())), preferred_element_type=F32)


def dot_nt(a, b):
    return lax.dot_general(a, b, (((1,), (1,)), ((), ())), preferred_element_type=F32)


def split(a):
    head = a.astype(BF16)
    return head, (a - head.astype(F32)).astype(BF16)


def index(shape, axis):
    return lax.broadcasted_iota(jnp.int32, shape, axis)


def one_hot(mask):
    return jnp.where(mask, 1.0, 0.0).astype(BF16)


def chol_id(y, z, x):
    return {"chol": y * 16 + z * 4 + x}


def others(at):
    return [lax.rem(at + k, SIDE) for k in range(1, SIDE)]


def remote(src, dst, send, recv, peer):
    return pltpu.make_async_remote_copy(
        src_ref=src, dst_ref=dst, send_sem=send, recv_sem=recv, device_id=peer, device_id_type=MESH
    )


def start(copies):
    for copy in copies:
        copy.start()


def received(copies):
    for copy in copies:
        copy.wait_recv()


def sent(copies):
    for copy in copies:
        copy.wait_send()


def inverse_of(top, tuned, products):
    occ = top.shape[0]
    gram = dot_nt(top, top)
    scale = 0.999 / jnp.max(jnp.sum(jnp.abs(gram), axis=1, keepdims=True), axis=0, keepdims=True)
    inv, square = top.astype(F32) * scale, gram * scale
    least = tuned
    for turn in range(products):
        c = 2.0 / (1.0 + least)
        least = 1.0 - ((1.0 - least) / (1.0 + least)) ** 2
        near = inv.astype(BF16)
        if turn > 0:
            square = dot_nt(near, top)
        inv = (2.0 * c) * inv - (c * c) * dot(square.astype(BF16), near)
    eye = jnp.where(index((occ, occ), 0) == index((occ, occ), 1), 1.0, 0.0)
    for _ in range(REFINE):
        head, rest = split(inv)
        miss = eye - (dot_nt(rest, top) + dot_nt(head, top))
        inv = inv + dot(miss.astype(BF16), head)
    return inv, jnp.sum(jnp.sum(miss * miss, axis=1, keepdims=True), axis=0, keepdims=True)


def theta_rows(inv, phi_t, x):
    occ, orb = phi_t.shape
    shape = (SIDE * PAD, occ)
    row, col = index(shape, 0), index(shape, 1)
    sel = one_hot((col == (row // PAD * SIDE + x) * ROWS + row % PAD) & (row % PAD < ROWS))
    head, rest = [dot(sel, part).astype(BF16) for part in split(inv)]
    theta = dot(rest, phi_t[...]) + dot(head, phi_t[...])
    return theta.astype(BF16).reshape(SIDE, PAD, orb)


def eight(grid, part):
    return grid[part // 2, 2 * (part % 2) : 2 * (part % 2) + 2].reshape(8 * PAD, grid.shape[-1])


def pick_rows():
    shape = (8 * ROWS, 8 * PAD)
    row, col = index(shape, 0), index(shape, 1)
    return row % ROWS, col % PAD, row // ROWS == col // PAD


def compact(grid, out, these):
    row, col, same = pick_rows()
    pick = one_hot(same & (row == col))
    for part in these:
        out[8 * ROWS * part : 8 * ROWS * (part + 1), :] = dot(pick, eight(grid, part)).astype(BF16)


def compact_packed(grid, out, c):
    row, col, same = pick_rows()
    pick = one_hot(same & (row == col))
    rest = [one_hot(same & (col == ROWS + row // 4) & (row % 4 == 2 * c + e)) for e in range(2)]
    for part in range(8):
        piece = eight(grid, part)
        rows = pl.ds(8 * ROWS * part, 8 * ROWS)
        out[rows, HALF * c : HALF * (c + 1)] = dot(pick, piece).astype(BF16)
        tail = sum(dot(rest[e], piece[:, LANES * e : LANES * (e + 1)]) for e in range(2))
        if c > 0:
            tail = tail + out[rows, 2 * HALF :].astype(F32)
        out[rows, 2 * HALF :] = tail.astype(BF16)


def bias_rows(green, chol):
    rows, vecs, _ = chol.shape
    row = index(green.shape, 0) % PAD
    acc = sum(dot_nt(jnp.where(row == r, green, jnp.zeros_like(green)), chol[r]) for r in range(rows))
    return jnp.sum(acc.reshape(SIDE, PAD, vecs), axis=1)


def potential_chunk(field, chol, c):
    rows, vecs, _ = chol.shape
    field = jnp.broadcast_to(field[:, None, :], (SIDE, PAD, vecs)).reshape(SIDE * PAD, vecs).astype(BF16)
    row = index(field.shape, 0) % PAD
    none = jnp.zeros_like(field)
    lanes = slice(HALF * c, HALF * (c + 1))
    main = sum(dot(jnp.where(row == r, field, none), chol[r, :, lanes]) for r in range(rows))
    tails = [
        sum(dot(jnp.where(row == ROWS + r // 4, field, none), chol[r, :, 2 * HALF :]) for r in range(2 * c + e, rows, 4))
        for e in range(2)
    ]
    whole = SQRT_DT * (main + jnp.concatenate(tails, axis=1))
    return whole.astype(BF16).reshape(SIDE, PAD, HALF)


def pack_walker(phi_t, blocks, y, x, missed):
    occ, orb = phi_t.shape
    shape = (SIDE * PAD, orb)
    row, col = index(shape, 0), index(shape, 1)
    base, r = (y * 16 + row // PAD * SIDE + x) * ROWS, row % PAD
    whole = dot_nt(one_hot((col == base + r) & (r < ROWS)), phi_t[:LANES, :])
    rest = occ - LANES
    copies = jnp.concatenate([phi_t[LANES:, :]] * 4, axis=0)
    lane = index((SIDE * PAD, LANES), 1) // rest
    for s in range(4):
        at = 4 * (r - ROWS) + s
        tail = dot_nt(one_hot((col == base + at) & (at >= 0) & (at < ROWS)), copies)
        whole = whole + jnp.where(lane == s, tail, 0.0)
    whole = jnp.where(index(whole.shape, 0) % PAD == FLAG, missed, whole)
    blocks[...] = whole.astype(BF16).reshape(SIDE, PAD, LANES)


def kernel(
    walkers, chol_hbm, noise, sources, out, bias, missed_out,
    chol, padded, first_grid, phi, phi_t, theta, slab_theta, parts, halves, blocks, grid, pot, packed, everyone,
    send0, recv0, send, recv, bias_send, bias_recv, last_send, last_recv, chol_sem,
):
    d, pop = lax.axis_index("chol"), lax.axis_index("pop")
    y, z, x = d // 16, (d // 4) % 4, d % 4
    slab, pair = z * SIDE + x, x // 2
    near, far = x + 1 - 2 * (x % 2), lax.rem(x + 2, SIDE)
    hi, core = pop // 2, pop % 2
    load = pltpu.make_async_copy(chol_hbm, chol, chol_sem)
    load.start()

    ys, zs, xs = others(y), others(z), others(x)
    ring = []
    for k in range(1, 16):
        place = lax.rem(hi * 4 + z + k, 16)
        ring.append((place // 4, place % 4))
    twin = {"pop": hi * 2 + 1 - core}
    ring_peers = [{"chol": y * 16 + b * 4 + x, "pop": h * 2 + core} for h, b in ring]
    z_peers = [chol_id(y, b, x) for b in zs]
    y_peers = [chol_id(b, z, x) for b in ys]
    x_peers = [chol_id(y, z, b) for b in xs]
    barrier = pltpu.get_barrier_semaphore()

    def greet(peers):
        for peer in peers:
            pl.semaphore_signal(barrier, inc=1, device_id=peer, device_id_type=MESH)

    greet(ring_peers + x_peers + y_peers + [twin])

    @pl.when(y == 0)
    def _():
        greet([chol_id(0, b, near) for b in zs] + [chol_id(b, z, far) for b in range(1, SIDE)])

    @pl.when(y != 0)
    def _():
        greet([chol_id(0, z, far)])

    padded[...] = jnp.zeros_like(padded)
    padded[:, :ROWS, :] = walkers[...]

    @pl.when(y == 0)
    def _():
        pl.semaphore_wait(barrier, 28)

    @pl.when(y != 0)
    def _():
        pl.semaphore_wait(barrier, 23)

    def pushes(ref, spot, peers, sems, base):
        return [remote(ref.at[spot], ref.at[spot], sems[0].at[base + k], sems[1].at[base + k], p) for k, p in enumerate(peers)]

    one, two = pl.ds(0, 2), pl.ds(2, 2)
    sems0 = send0, recv0
    first = [
        remote(padded.at[w], first_grid.at[y, z, x], send0.at[k], recv0.at[k], peer)
        for k, (w, peer) in enumerate(zip(zs, z_peers, strict=True))
    ]
    start(first)
    first_grid[y, z, x] = padded[z]
    received(first)
    along_y = pushes(first_grid, (y, one, x), y_peers, sems0, 3)
    along_x = pushes(first_grid, (y, two, x), x_peers, sems0, 6)
    then_y = pushes(first_grid, (y, two, slice(None)), y_peers, sems0, 9)
    start(along_y + along_x)

    @pl.when(y != 0)
    def _():
        then_x = pushes(first_grid, (slice(None), one, x), x_peers, sems0, 12)
        received(along_y)
        start(then_x)
        received(along_x)
        start(then_y)
        sent(first + along_y + along_x)
        received(then_x + then_y)
        compact(first_grid, phi, range(8))
        sent(then_x + then_y)

    for s in range(STEPS):
        to_slab = [
            remote(theta.at[s, b], slab_theta.at[s, z], send.at[s, k], recv.at[s, k], peer)
            for k, (b, peer) in enumerate(zip(zs, z_peers, strict=True))
        ]
        pairs = [(lax.rem(z + k // 2, SIDE), (x, near)[k % 2]) for k in range(1, 8)]
        to_pair = [
            remote(parts.at[s, slab], parts.at[s, slab], bias_send.at[s, k], bias_recv.at[s, k], chol_id(0, b, c))
            for k, (b, c) in enumerate(pairs)
        ]
        half = halves.at[s, pair]
        to_rows = [
            remote(half, half, bias_send.at[s, 7 + k], bias_recv.at[s, 7 + pair], peer)
            for k, peer in enumerate([chol_id(b, z, c) for c in (x, far) for b in range(SIDE)][1:])
        ]

        def half_arrives(which, s=s):
            pltpu.make_async_copy(halves.at[s, which], halves.at[s, which], bias_recv.at[s, 7 + which]).wait()

        @pl.when(y == 0)
        def _(s=s):
            if s == 0:
                early = pushes(first_grid, (0, one, x), x_peers, sems0, 15)
                then_x = pushes(first_grid, (pl.ds(1, 3), one, x), x_peers, sems0, 12)
                start(early)
                received(along_y)
                start(then_x)
                received(along_x)
                start(then_y)
                received(early)
                compact(first_grid, phi, range(2))
                inv, size = inverse_of(phi[: phi.shape[1], :], *NEWTON[s])
                received(then_x + then_y)
                compact(first_grid, phi, range(2, 8))
                phi_t[...] = phi[...].astype(F32).T.astype(BF16)
            else:
                top = phi_t[:, : phi_t.shape[0]].astype(F32).T.astype(BF16)
                inv, size = inverse_of(top, *NEWTON[s])
            theta[s] = theta_rows(inv, phi_t, x)
            start(to_slab)
            slab_theta[s, z] = theta[s, z]
            if s == 0:
                sent(first + along_y + along_x + early + then_x + then_y)
                load.wait()
            missed = jnp.where(size < MISS, 0.0, 1.0)
            mine = parts.at[s, slab]
            mine[...] = jnp.zeros(mine.shape, F32)
            flags = index((SIDE, LANES), 0) == z
            mine[:, FLAGS:] = jnp.where(flags, missed, 0.0)
            received(to_slab)
            mine[:, : chol.shape[1]] = bias_rows(slab_theta[s].reshape(SIDE * PAD, chol.shape[2]), chol)
            start(to_pair)
            received(to_pair)
            half[...] = sum(parts[s, SIDE * b + 2 * pair + e] for e in range(2) for b in range(SIDE))
            start(to_rows)
            half_arrives(1 - pair)

        @pl.when(y != 0)
        def _(s=s):
            if s == 0:
                phi_t[...] = phi[...].astype(F32).T.astype(BF16)
                load.wait()
            half_arrives(0)
            half_arrives(1)

        total = halves[s, 0] + halves[s, 1]
        flag = jnp.sum(jnp.where(index((SIDE, LANES), 0) == z, total[:, FLAGS:], 0.0), axis=0, keepdims=True)[:, :1]
        missed = flag if s == 0 else missed + flag
        total = SQRT_DT * total[:, : chol.shape[1]]
        field = (noise[s] - total).astype(BF16).astype(F32)

        sems = send.at[s, pl.ds(3, 30)], recv.at[s, pl.ds(3, 30)]
        firsts, alongs, thens = [], [], []
        for c in range(2):
            blocks[s, c] = potential_chunk(field, chol, c)
            firsts.append([
                remote(blocks.at[s, c, w], grid.at[s, c, y, z, x], sems[0].at[15 * c + k], sems[1].at[15 * c + k], peer)
                for k, (w, peer) in enumerate(zip(zs, z_peers, strict=True))
            ])
            start(firsts[c])
            grid[s, c, y, z, x] = blocks[s, c, z]
        share = one_hot(index((chol.shape[1], 8), 0) == d * bias.shape[2] + index((chol.shape[1], 8), 1)).astype(F32)
        bias[s] = jnp.dot(total, share, precision=lax.Precision.HIGHEST, preferred_element_type=F32)[:, : bias.shape[2]]
        for c in range(2):
            received(firsts[c])
            view = grid.at[s, c]
            alongs.append((
                pushes(view, (y, one, x), y_peers, sems, 15 * c + 3),
                pushes(view, (y, two, x), x_peers, sems, 15 * c + 6),
            ))
            start(alongs[c][0] + alongs[c][1])
        for c in range(2):
            view = grid.at[s, c]
            then_x = pushes(view, (slice(None), one, x), x_peers, sems, 15 * c + 9)
            then_y = pushes(view, (y, two, slice(None)), y_peers, sems, 15 * c + 12)
            received(alongs[c][0])
            start(then_x)
            received(alongs[c][1])
            start(then_y)
            thens.append(then_x + then_y)
        for c in range(2):
            received(thens[c])
            compact_packed(grid.at[s, c], pot, c)

        term = phi_t[...]
        sum_of = term.astype(F32)
        for order in range(1, ORDER + 1):
            term = (-dot_nt(term, pot[...]) / order).astype(BF16)
            sum_of = sum_of + term.astype(F32)
        phi_t[...] = sum_of.astype(BF16)
        for c in range(2):
            sent(firsts[c] + alongs[c][0] + alongs[c][1] + thens[c])

        @pl.when(y == 0)
        def _():
            sent(to_slab + to_pair + to_rows)

    pack_walker(phi_t, packed, y, x, missed)
    spot = everyone.at[hi, core, z]
    to_ring = [
        remote(packed.at[b], spot, last_send.at[k], last_recv.at[k], peer)
        for k, ((_, b), peer) in enumerate(zip(ring, ring_peers, strict=True))
    ]
    start(to_ring)
    everyone[hi, core, z] = packed[z]
    received(to_ring)
    mine = everyone.at[:, core]
    to_twin = [remote(mine, mine, last_send.at[15], last_recv.at[15], twin)]
    start(to_twin)
    sent(to_ring)
    received(to_twin)

    chosen = []
    for slot in range(SIDE):
        source = sources[slot]
        chosen.append(everyone[source // 8, source // 4 % 2, source % 4])
    whole = jnp.concatenate(chosen, axis=0)
    out[:, :, :LANES] = whole.reshape(SIDE, PAD, LANES)
    rest = out.shape[2] - LANES
    shape = (SIDE * PAD, SIDE * PAD)
    row, col = index(shape, 0), index(shape, 1)
    r = row % PAD
    back = one_hot(index((LANES, rest), 0) % rest == index((LANES, rest), 1))
    lane = index((SIDE * PAD, LANES), 1) // rest
    tail = jnp.zeros((SIDE * PAD, LANES), F32)
    for s in range(4):
        pick = one_hot((row // PAD == col // PAD) & (col % PAD == ROWS + r // 4) & (r % 4 == s) & (r < ROWS))
        tail = tail + jnp.where(lane == s, dot(pick, whole), 0.0)
    out[:, :, LANES:] = dot(tail.astype(BF16), back).astype(BF16).reshape(SIDE, PAD, rest)
    flags = everyone[...].reshape(8 * SIDE, PAD, LANES).astype(F32)
    bad = jnp.where((index(flags.shape, 1) == FLAG) & jnp.logical_not(flags == 0.0), 1.0, 0.0)
    missed_out[...] = jnp.max(jnp.max(bad, axis=0), axis=0, keepdims=True)
    sent(to_twin)


def propagate(walkers, chol, noise, sources):
    rows, vecs, orb = chol.shape
    occ = walkers.shape[2]
    dma = pltpu.SemaphoreType.DMA
    vmem = pl.BlockSpec(memory_space=VMEM)
    return pl.pallas_call(
        kernel,
        out_shape=(
            jax.ShapeDtypeStruct((SIDE, PAD, occ), BF16),
            jax.ShapeDtypeStruct((STEPS, SIDE, vecs // SIDE**3), F32),
            jax.ShapeDtypeStruct((1, LANES), F32),
        ),
        in_specs=[vmem, pl.BlockSpec(memory_space=pl.ANY), vmem, pl.BlockSpec(memory_space=pltpu.SMEM)],
        out_specs=(vmem, vmem, vmem),
        scratch_shapes=[
            VMEM((rows, vecs, orb), BF16),
            VMEM((SIDE, PAD, occ), BF16),
            VMEM((SIDE, SIDE, SIDE, PAD, occ), BF16),
            VMEM((orb, occ), BF16),
            VMEM((occ, orb), BF16),
            VMEM((STEPS, SIDE, PAD, orb), BF16),
            VMEM((STEPS, SIDE, PAD, orb), BF16),
            VMEM((STEPS, 16, SIDE, FLAGS + LANES), F32),
            VMEM((STEPS, 2, SIDE, FLAGS + LANES), F32),
            VMEM((STEPS, 2, SIDE, PAD, HALF), BF16),
            VMEM((STEPS, 2, SIDE, SIDE, SIDE, PAD, HALF), BF16),
            VMEM((orb, orb), BF16),
            VMEM((SIDE, PAD, LANES), BF16),
            VMEM((SIDE, 2, SIDE, PAD, LANES), BF16),
            dma((18,)),
            dma((18,)),
            dma((STEPS, 33)),
            dma((STEPS, 33)),
            dma((STEPS, 14)),
            dma((STEPS, 9)),
            dma((16,)),
            dma((16,)),
            dma,
        ],
        compiler_params=pltpu.CompilerParams(collective_id=0, has_side_effects=True, vmem_limit_bytes=LIMIT),
        name="propagate",
    )(walkers, chol, noise, sources)


def solve_each(factor, target):
    return jax.scipy.linalg.cho_solve((factor, True), target)


def by_cholesky(walkers, chol_vectors, noise, sources):
    walk_count, row_count, occ_count = walkers.shape
    vec_count, _, orb_count = chol_vectors.shape
    first_row = lax.axis_index("chol") * row_count
    flat_chol = chol_vectors.reshape(vec_count, row_count * orb_count)
    current = walkers
    biases = []
    for step_index in range(STEPS):
        gathered = lax.all_gather(current, "chol", axis=1, tiled=True)
        phi = gathered.astype(F32)
        top_plain = gathered[:, :occ_count, :]
        gram = jnp.einsum("wai,waj->wij", top_plain, top_plain, preferred_element_type=F32)
        factor = jnp.linalg.cholesky(gram)
        inverse = jax.vmap(solve_each)(factor, jnp.swapaxes(phi[:, :occ_count, :], 1, 2))
        inverse_wide = jnp.pad(inverse, ((0, 0), (0, 0), (0, orb_count - occ_count)))
        inverse_cols = lax.dynamic_slice_in_dim(inverse_wide, first_row, row_count, 2)
        theta_slab = jnp.einsum("wja,wai->wji", phi, inverse_cols, precision=lax.Precision.HIGHEST).astype(BF16)
        green = jnp.swapaxes(theta_slab, 1, 2).reshape(walk_count, row_count * orb_count)
        partial_bias = lax.dot_general(green, flat_chol, (((1,), (1,)), ((), ())), preferred_element_type=F32)
        bias_now = SQRT_DT * lax.psum(partial_bias, "chol")
        biases.append(bias_now)
        field = (noise[step_index] - bias_now).astype(BF16)
        potential = SQRT_DT * jnp.dot(field, flat_chol, preferred_element_type=F32)
        potential = potential.reshape(walk_count, row_count, orb_count).astype(BF16)
        total = current.astype(F32)
        term = current
        for order in range(1, ORDER + 1):
            whole = gathered if order == 1 else lax.all_gather(term, "chol", axis=1, tiled=True)
            product = jnp.einsum("wij,wjb->wib", potential, whole, preferred_element_type=F32)
            term = (-product / order).astype(BF16)
            total = total + term.astype(F32)
        current = total.astype(BF16)
    everyone = lax.all_gather(current, "pop", axis=0, tiled=True)
    return everyone[sources], jnp.stack(biases)


def local(walkers, chol_vectors, noise, sources):
    _, row_count, _ = walkers.shape
    vec_count = chol_vectors.shape[0]
    share = vec_count // lax.axis_size("chol")
    branched, bias, missed = propagate(walkers, jnp.transpose(chol_vectors, (1, 0, 2)), noise, sources)

    def by_share():
        branched, bias = by_cholesky(walkers, chol_vectors, noise, sources)
        return branched, lax.dynamic_slice_in_dim(bias, lax.axis_index("chol") * share, share, 2)

    return lax.cond(missed[0, 0] == 0.0, lambda: (branched[:, :row_count, :], bias), by_share)


def solution(mesh):
    return jax.shard_map(
        local,
        mesh=mesh,
        in_specs=(P("pop", "chol", None), P(None, "chol", None), P(None, "pop", None), P("pop")),
        out_specs=(P("pop", "chol", None), P(None, "pop", "chol")),
        check_vma=False,
    )
```

```python
import jax
import jax.numpy as jnp
from jax import lax
from jax.experimental import pallas as pl
from jax.experimental.pallas import tpu as pltpu
from jax.sharding import PartitionSpec as P

STEPS = 2
ORDER = 4
SQRT_DT = 0.1
MESH = pl.DeviceIdType.MESH
F32 = jnp.float32
BF16 = jnp.bfloat16
VMEM = pltpu.VMEM
ROWS = 10
PAD = 16
SIDE = 4
HALF = 256
LANES = 128
FLAGS = 384
FLAG = 15
NEWTON = ((0.05, 5), (0.001, 8))
REFINE = 2
MISS = 1e-3
LIMIT = 60 * 1024 * 1024


def dot(a, b):
    return lax.dot_general(a, b, (((1,), (0,)), ((), ())), preferred_element_type=F32)


def dot_nt(a, b):
    return lax.dot_general(a, b, (((1,), (1,)), ((), ())), preferred_element_type=F32)


def split(a):
    head = a.astype(BF16)
    return head, (a - head.astype(F32)).astype(BF16)


def index(shape, axis):
    return lax.broadcasted_iota(jnp.int32, shape, axis)


def one_hot(mask):
    return jnp.where(mask, 1.0, 0.0).astype(BF16)


def chol_id(y, z, x):
    return {"chol": y * 16 + z * 4 + x}


def others(at):
    return [lax.rem(at + k, SIDE) for k in range(1, SIDE)]


def remote(src, dst, send, recv, peer):
    return pltpu.make_async_remote_copy(
        src_ref=src, dst_ref=dst, send_sem=send, recv_sem=recv, device_id=peer, device_id_type=MESH
    )


def start(copies):
    for copy in copies:
        copy.start()


def received(copies):
    for copy in copies:
        copy.wait_recv()


def sent(copies):
    for copy in copies:
        copy.wait_send()


def inverse_of(top, tuned, products):
    occ = top.shape[0]
    gram = dot_nt(top, top)
    scale = 0.999 / jnp.max(jnp.sum(jnp.abs(gram), axis=1, keepdims=True), axis=0, keepdims=True)
    inv, square = top.astype(F32) * scale, gram * scale
    least = tuned
    for turn in range(products):
        c = 2.0 / (1.0 + least)
        least = 1.0 - ((1.0 - least) / (1.0 + least)) ** 2
        near = inv.astype(BF16)
        if turn > 0:
            square = dot_nt(near, top)
        inv = (2.0 * c) * inv - (c * c) * dot(square.astype(BF16), near)
    eye = jnp.where(index((occ, occ), 0) == index((occ, occ), 1), 1.0, 0.0)
    for _ in range(REFINE):
        head, rest = split(inv)
        miss = eye - (dot_nt(rest, top) + dot_nt(head, top))
        inv = inv + dot(miss.astype(BF16), head)
    return inv, jnp.sum(jnp.sum(miss * miss, axis=1, keepdims=True), axis=0, keepdims=True)


def theta_rows(inv, phi_t, x):
    occ, orb = phi_t.shape
    shape = (SIDE * PAD, occ)
    row, col = index(shape, 0), index(shape, 1)
    sel = one_hot((col == (row // PAD * SIDE + x) * ROWS + row % PAD) & (row % PAD < ROWS))
    head, rest = [dot(sel, part).astype(BF16) for part in split(inv)]
    theta = dot(rest, phi_t[...]) + dot(head, phi_t[...])
    return theta.astype(BF16).reshape(SIDE, PAD, orb)


def eight(block, part):
    y, z = part // 2, 2 * (part % 2)
    return jnp.concatenate([block(y, z + k // SIDE, k % SIDE) for k in range(8)], axis=0)


def pick_rows():
    shape = (8 * ROWS, 8 * PAD)
    row, col = index(shape, 0), index(shape, 1)
    return row % ROWS, col % PAD, row // ROWS == col // PAD


def compact(block, out, these):
    row, col, same = pick_rows()
    pick = one_hot(same & (row == col))
    for part in these:
        out[8 * ROWS * part : 8 * ROWS * (part + 1), :] = dot(pick, eight(block, part)).astype(BF16)


def compact_packed(block, out, c):
    row, col, same = pick_rows()
    pick = one_hot(same & (row == col))
    rest = [one_hot(same & (col == ROWS + row // 4) & (row % 4 == 2 * c + e)) for e in range(2)]
    for part in range(8):
        piece = eight(block, part)
        rows = pl.ds(8 * ROWS * part, 8 * ROWS)
        out[rows, HALF * c : HALF * (c + 1)] = dot(pick, piece).astype(BF16)
        tail = sum(dot(rest[e], piece[:, LANES * e : LANES * (e + 1)]) for e in range(2))
        if c > 0:
            tail = tail + out[rows, 2 * HALF :].astype(F32)
        out[rows, 2 * HALF :] = tail.astype(BF16)


def bias_rows(green, chol):
    rows, vecs, _ = chol.shape
    row = index(green.shape, 0) % PAD
    acc = sum(dot_nt(jnp.where(row == r, green, jnp.zeros_like(green)), chol[r]) for r in range(rows))
    return jnp.sum(acc.reshape(SIDE, PAD, vecs), axis=1)


def potential_chunk(field, chol, c):
    rows, vecs, _ = chol.shape
    field = jnp.broadcast_to(field[:, None, :], (SIDE, PAD, vecs)).reshape(SIDE * PAD, vecs).astype(BF16)
    row = index(field.shape, 0) % PAD
    none = jnp.zeros_like(field)
    lanes = slice(HALF * c, HALF * (c + 1))
    main = sum(dot(jnp.where(row == r, field, none), chol[r, :, lanes]) for r in range(rows))
    tails = [
        sum(dot(jnp.where(row == ROWS + r // 4, field, none), chol[r, :, 2 * HALF :]) for r in range(2 * c + e, rows, 4))
        for e in range(2)
    ]
    whole = SQRT_DT * (main + jnp.concatenate(tails, axis=1))
    return whole.astype(BF16).reshape(SIDE, PAD, HALF)


def pack_walker(phi_t, blocks, y, x, missed):
    occ, orb = phi_t.shape
    shape = (SIDE * PAD, orb)
    row, col = index(shape, 0), index(shape, 1)
    base, r = (y * 16 + row // PAD * SIDE + x) * ROWS, row % PAD
    whole = dot_nt(one_hot((col == base + r) & (r < ROWS)), phi_t[:LANES, :])
    rest = occ - LANES
    copies = jnp.concatenate([phi_t[LANES:, :]] * 4, axis=0)
    lane = index((SIDE * PAD, LANES), 1) // rest
    for s in range(4):
        at = 4 * (r - ROWS) + s
        tail = dot_nt(one_hot((col == base + at) & (at >= 0) & (at < ROWS)), copies)
        whole = whole + jnp.where(lane == s, tail, 0.0)
    whole = jnp.where(index(whole.shape, 0) % PAD == FLAG, missed, whole)
    blocks[...] = whole.astype(BF16).reshape(SIDE, PAD, LANES)


def kernel(
    walkers, chol_hbm, noise, sources, out, bias, missed_out,
    chol, padded, first_grid, phi, phi_t, theta, slab_theta, parts, halves, blocks, grid, pot, packed, everyone,
    send0, recv0, send, recv, bias_send, bias_recv, last_send, last_recv, chol_sem,
):
    d, pop = lax.axis_index("chol"), lax.axis_index("pop")
    y, z, x = d // 16, (d // 4) % 4, d % 4
    slab, pair = z * SIDE + x, x // 2
    near, far = x + 1 - 2 * (x % 2), lax.rem(x + 2, SIDE)
    hi, core = pop // 2, pop % 2
    load = pltpu.make_async_copy(chol_hbm, chol, chol_sem)
    load.start()

    ys, zs, xs = others(y), others(z), others(x)
    ring = []
    for k in range(1, 16):
        place = lax.rem(hi * 4 + z + k, 16)
        ring.append((place // 4, place % 4))
    twin = {"pop": hi * 2 + 1 - core}
    ring_peers = [{"chol": y * 16 + b * 4 + x, "pop": h * 2 + core} for h, b in ring]
    z_peers = [chol_id(y, b, x) for b in zs]
    y_peers = [chol_id(b, z, x) for b in ys]
    x_peers = [chol_id(y, z, b) for b in xs]
    barrier = pltpu.get_barrier_semaphore()

    def greet(peers):
        for peer in peers:
            pl.semaphore_signal(barrier, inc=1, device_id=peer, device_id_type=MESH)

    greet(ring_peers + x_peers + y_peers + [twin])

    @pl.when(y == 0)
    def _():
        greet([chol_id(0, b, near) for b in zs] + [chol_id(b, z, far) for b in range(1, SIDE)])

    @pl.when(y != 0)
    def _():
        greet([chol_id(0, z, far)])

    padded[...] = jnp.zeros_like(padded)
    padded[:, :ROWS, :] = jnp.swapaxes(walkers[...].astype(F32), 0, 1).astype(BF16)

    @pl.when(y == 0)
    def _():
        pl.semaphore_wait(barrier, 28)

    @pl.when(y != 0)
    def _():
        pl.semaphore_wait(barrier, 23)

    def pushes(ref, peers, sems, base):
        return [remote(ref, ref, sems[0].at[base + k], sems[1].at[base + k], p) for k, p in enumerate(peers)]

    sems0 = send0, recv0
    upper = z // 2
    spot = first_grid.at[upper, x + upper * (y - x), y + upper * (x - y), z % 2]
    first = [
        remote(padded.at[w], spot, send0.at[k], recv0.at[k], peer)
        for k, (w, peer) in enumerate(zip(zs, z_peers, strict=True))
    ]
    start(first)
    spot[...] = padded[z]
    received(first)
    along_y = pushes(first_grid.at[0, x, y], y_peers, sems0, 3)
    along_x = pushes(first_grid.at[1, y, x], x_peers, sems0, 6)
    then_y = pushes(first_grid.at[1, y], y_peers, sems0, 9)
    start(along_y + along_x)

    def first_block(b, c, e):
        return first_grid[0, e, b, c] if c < 2 else first_grid[1, b, e, c - 2]

    @pl.when(y != 0)
    def _():
        then_x = pushes(first_grid.at[0, x], x_peers, sems0, 12)
        received(along_y)
        start(then_x)
        received(along_x)
        start(then_y)
        sent(first + along_y + along_x)
        received(then_x + then_y)
        compact(first_block, phi, range(8))
        phi_t[...] = phi[...].astype(F32).T.astype(BF16)
        sent(then_x + then_y)

    drain = []
    for s in range(STEPS):
        to_slab = [
            remote(theta.at[s, b], slab_theta.at[s, z], send.at[s, k], recv.at[s, k], peer)
            for k, (b, peer) in enumerate(zip(zs, z_peers, strict=True))
        ]
        pairs = [(lax.rem(z + k // 2, SIDE), (x, near)[k % 2]) for k in range(1, 8)]
        to_pair = [
            remote(parts.at[s, slab], parts.at[s, slab], bias_send.at[s, k], bias_recv.at[s, k], chol_id(0, b, c))
            for k, (b, c) in enumerate(pairs)
        ]
        half = halves.at[s, pair]
        to_rows = [
            remote(half, half, bias_send.at[s, 7 + k], bias_recv.at[s, 7 + pair], peer)
            for k, peer in enumerate([chol_id(b, z, c) for c in (x, far) for b in range(SIDE)][1:])
        ]

        def half_arrives(which, s=s):
            pltpu.make_async_copy(halves.at[s, which], halves.at[s, which], bias_recv.at[s, 7 + which]).wait()

        @pl.when(y == 0)
        def _(s=s, drain=drain, led=led if s else []):
            if s == 0:
                early = pushes(first_grid.at[0, x, 0], x_peers, sems0, 15)
                then_x = pushes(first_grid.at[0, x, pl.ds(1, 3)], x_peers, sems0, 12)
                start(early)
                received(along_y)
                start(then_x)
                received(along_x)
                start(then_y)
                received(early)
                compact(first_block, phi, range(2))
                inv, size = inverse_of(phi[: phi.shape[1], :], *NEWTON[s])
                received(then_x + then_y)
                compact(first_block, phi, range(2, 8))
                phi_t[...] = phi[...].astype(F32).T.astype(BF16)
            else:
                top = phi_t[:, : phi_t.shape[0]].astype(F32).T.astype(BF16)
                inv, size = inverse_of(top, *NEWTON[s])
            theta[s] = theta_rows(inv, phi_t, x)
            start(to_slab)
            slab_theta[s, z] = theta[s, z]
            if s == 0:
                sent(first + along_y + along_x + early + then_x + then_y)
                load.wait()
            sent(drain + led)
            missed = jnp.where(size < MISS, 0.0, 1.0)
            mine = parts.at[s, slab]
            mine[...] = jnp.zeros(mine.shape, F32)
            flags = index((SIDE, LANES), 0) == z
            mine[:, FLAGS:] = jnp.where(flags, missed, 0.0)
            received(to_slab)
            mine[:, : chol.shape[1]] = bias_rows(slab_theta[s].reshape(SIDE * PAD, chol.shape[2]), chol)
            start(to_pair)
            received(to_pair)
            half[...] = sum(parts[s, SIDE * b + 2 * pair + e] for e in range(2) for b in range(SIDE))
            start(to_rows)
            half_arrives(1 - pair)

        @pl.when(y != 0)
        def _(s=s, drain=drain):
            sent(drain)
            if s == 0:
                load.wait()
            half_arrives(0)
            half_arrives(1)

        total = halves[s, 0] + halves[s, 1]
        flag = jnp.sum(jnp.where(index((SIDE, LANES), 0) == z, total[:, FLAGS:], 0.0), axis=0, keepdims=True)[:, :1]
        missed = flag if s == 0 else missed + flag
        total = SQRT_DT * total[:, : chol.shape[1]]
        field = (noise[s] - total).astype(BF16).astype(F32)

        sems = send.at[s, pl.ds(3, 18)], recv.at[s, pl.ds(3, 18)]
        firsts, alongs, thens = [], [], []
        for c, (u, v) in enumerate([(x, y), (y, x)]):
            blocks[s, c] = potential_chunk(field, chol, c)
            spot = grid.at[s, c, u, v, z]
            firsts.append([
                remote(blocks.at[s, c, w], spot, sems[0].at[9 * c + k], sems[1].at[9 * c + k], peer)
                for k, (w, peer) in enumerate(zip(zs, z_peers, strict=True))
            ])
            start(firsts[c])
            spot[...] = blocks[s, c, z]
        for c, (u, v, peers) in enumerate([(x, y, y_peers), (y, x, x_peers)]):
            received(firsts[c])
            alongs.append(pushes(grid.at[s, c, u, v], peers, sems, 9 * c + 3))
            start(alongs[c])
        for c, (u, peers) in enumerate([(x, x_peers), (y, y_peers)]):
            received(alongs[c])
            thens.append(pushes(grid.at[s, c, u], peers, sems, 9 * c + 6))
            start(thens[c])
        share = one_hot(index((chol.shape[1], 8), 0) == d * bias.shape[2] + index((chol.shape[1], 8), 1)).astype(F32)
        bias[s] = jnp.dot(total, share, precision=lax.Precision.HIGHEST, preferred_element_type=F32)[:, : bias.shape[2]]
        received(thens[0])
        compact_packed(lambda b, c, e, s=s: grid[s, 0, e, b, c], pot, 0)
        received(thens[1])
        compact_packed(lambda b, c, e, s=s: grid[s, 1, b, e, c], pot, 1)

        term = phi_t[...]
        sum_of = term.astype(F32)
        for order in range(1, ORDER + 1):
            term = (-dot_nt(term, pot[...]) / order).astype(BF16)
            sum_of = sum_of + term.astype(F32)
        phi_t[...] = sum_of.astype(BF16)
        drain = sum(firsts + alongs + thens, [])
        led = to_slab + to_pair + to_rows

    pack_walker(phi_t, packed, y, x, missed)
    spot = everyone.at[hi, core, z]
    to_ring = [
        remote(packed.at[b], spot, last_send.at[k], last_recv.at[k], peer)
        for k, ((_, b), peer) in enumerate(zip(ring, ring_peers, strict=True))
    ]
    start(to_ring)
    everyone[hi, core, z] = packed[z]
    sent(drain)

    @pl.when(y == 0)
    def _():
        sent(led)

    received(to_ring)
    mine = everyone.at[:, core]
    to_twin = [remote(mine, mine, last_send.at[15], last_recv.at[15], twin)]
    start(to_twin)
    sent(to_ring)
    received(to_twin)

    chosen = []
    for slot in range(SIDE):
        source = sources[slot]
        chosen.append(everyone[source // 8, source // 4 % 2, source % 4])
    whole = jnp.concatenate(chosen, axis=0)
    rest = out.shape[2] - LANES
    shape = (SIDE * PAD, SIDE * PAD)
    row, col = index(shape, 0), index(shape, 1)
    r = row % PAD
    back = one_hot(index((LANES, rest), 0) % rest == index((LANES, rest), 1))
    lane = index((SIDE * PAD, LANES), 1) // rest
    tail = jnp.zeros((SIDE * PAD, LANES), F32)
    for s in range(4):
        pick = one_hot((row // PAD == col // PAD) & (col % PAD == ROWS + r // 4) & (r % 4 == s) & (r < ROWS))
        tail = tail + jnp.where(lane == s, dot(pick, whole), 0.0)
    tail = dot(tail.astype(BF16), back)
    whole = jnp.concatenate([whole.astype(F32), tail], axis=1).reshape(SIDE, PAD, LANES + rest)
    out[...] = jnp.swapaxes(whole[:, :ROWS, :], 0, 1).astype(BF16)
    flags = everyone[...].reshape(8 * SIDE, PAD, LANES).astype(F32)
    bad = jnp.where((index(flags.shape, 1) == FLAG) & jnp.logical_not(flags == 0.0), 1.0, 0.0)
    missed_out[...] = jnp.max(jnp.max(bad, axis=0), axis=0, keepdims=True)
    sent(to_twin)


def propagate(walkers, chol, noise, sources):
    rows, vecs, orb = chol.shape
    occ = walkers.shape[2]
    dma = pltpu.SemaphoreType.DMA
    vmem = pl.BlockSpec(memory_space=VMEM)
    return pl.pallas_call(
        kernel,
        out_shape=(
            jax.ShapeDtypeStruct((rows, SIDE, occ), BF16),
            jax.ShapeDtypeStruct((STEPS, SIDE, vecs // SIDE**3), F32),
            jax.ShapeDtypeStruct((1, LANES), F32),
        ),
        in_specs=[vmem, pl.BlockSpec(memory_space=pl.ANY), vmem, pl.BlockSpec(memory_space=pltpu.SMEM)],
        out_specs=(vmem, vmem, vmem),
        scratch_shapes=[
            VMEM((rows, vecs, orb), BF16),
            VMEM((SIDE, PAD, occ), BF16),
            VMEM((2, SIDE, SIDE, 2, PAD, occ), BF16),
            VMEM((orb, occ), BF16),
            VMEM((occ, orb), BF16),
            VMEM((STEPS, SIDE, PAD, orb), BF16),
            VMEM((STEPS, SIDE, PAD, orb), BF16),
            VMEM((STEPS, 16, SIDE, FLAGS + LANES), F32),
            VMEM((STEPS, 2, SIDE, FLAGS + LANES), F32),
            VMEM((STEPS, 2, SIDE, PAD, HALF), BF16),
            VMEM((STEPS, 2, SIDE, SIDE, SIDE, PAD, HALF), BF16),
            VMEM((orb, orb), BF16),
            VMEM((SIDE, PAD, LANES), BF16),
            VMEM((SIDE, 2, SIDE, PAD, LANES), BF16),
            dma((18,)),
            dma((18,)),
            dma((STEPS, 21)),
            dma((STEPS, 21)),
            dma((STEPS, 14)),
            dma((STEPS, 9)),
            dma((16,)),
            dma((16,)),
            dma,
        ],
        compiler_params=pltpu.CompilerParams(collective_id=0, has_side_effects=True, vmem_limit_bytes=LIMIT),
        name="propagate",
    )(walkers, chol, noise, sources)


def solve_each(factor, target):
    return jax.scipy.linalg.cho_solve((factor, True), target)


def by_cholesky(walkers, chol_vectors, noise, sources):
    walk_count, row_count, occ_count = walkers.shape
    vec_count, _, orb_count = chol_vectors.shape
    first_row = lax.axis_index("chol") * row_count
    flat_chol = chol_vectors.reshape(vec_count, row_count * orb_count)
    current = walkers
    biases = []
    for step_index in range(STEPS):
        gathered = lax.all_gather(current, "chol", axis=1, tiled=True)
        phi = gathered.astype(F32)
        top_plain = gathered[:, :occ_count, :]
        gram = jnp.einsum("wai,waj->wij", top_plain, top_plain, preferred_element_type=F32)
        factor = jnp.linalg.cholesky(gram)
        inverse = jax.vmap(solve_each)(factor, jnp.swapaxes(phi[:, :occ_count, :], 1, 2))
        inverse_wide = jnp.pad(inverse, ((0, 0), (0, 0), (0, orb_count - occ_count)))
        inverse_cols = lax.dynamic_slice_in_dim(inverse_wide, first_row, row_count, 2)
        theta_slab = jnp.einsum("wja,wai->wji", phi, inverse_cols, precision=lax.Precision.HIGHEST).astype(BF16)
        green = jnp.swapaxes(theta_slab, 1, 2).reshape(walk_count, row_count * orb_count)
        partial_bias = lax.dot_general(green, flat_chol, (((1,), (1,)), ((), ())), preferred_element_type=F32)
        bias_now = SQRT_DT * lax.psum(partial_bias, "chol")
        biases.append(bias_now)
        field = (noise[step_index] - bias_now).astype(BF16)
        potential = SQRT_DT * jnp.dot(field, flat_chol, preferred_element_type=F32)
        potential = potential.reshape(walk_count, row_count, orb_count).astype(BF16)
        total = current.astype(F32)
        term = current
        for order in range(1, ORDER + 1):
            whole = gathered if order == 1 else lax.all_gather(term, "chol", axis=1, tiled=True)
            product = jnp.einsum("wij,wjb->wib", potential, whole, preferred_element_type=F32)
            term = (-product / order).astype(BF16)
            total = total + term.astype(F32)
        current = total.astype(BF16)
    everyone = lax.all_gather(current, "pop", axis=0, tiled=True)
    return everyone[sources], jnp.stack(biases)


def local(walkers, chol_vectors, noise, sources):
    vec_count = chol_vectors.shape[0]
    share = vec_count // lax.axis_size("chol")
    branched, bias, missed = propagate(
        jnp.transpose(walkers, (1, 0, 2)), jnp.transpose(chol_vectors, (1, 0, 2)), noise, sources
    )

    def by_share():
        branched, bias = by_cholesky(walkers, chol_vectors, noise, sources)
        return branched, lax.dynamic_slice_in_dim(bias, lax.axis_index("chol") * share, share, 2)

    return lax.cond(missed[0, 0] == 0.0, lambda: (jnp.transpose(branched, (1, 0, 2)), bias), by_share)


def solution(mesh):
    return jax.shard_map(
        local,
        mesh=mesh,
        in_specs=(P("pop", "chol", None), P(None, "chol", None), P(None, "pop", None), P("pop")),
        out_specs=(P("pop", "chol", None), P(None, "pop", "chol")),
        check_vma=False,
    )
```

```python
import jax
import jax.numpy as jnp
from jax import lax
from jax.experimental import pallas as pl
from jax.experimental.pallas import tpu as pltpu
from jax.sharding import PartitionSpec as P

STEPS = 2
ORDER = 4
SQRT_DT = 0.1
MESH = pl.DeviceIdType.MESH
F32 = jnp.float32
BF16 = jnp.bfloat16
VMEM = pltpu.VMEM
ROWS = 10
PAD = 16
SIDE = 4
HALF = 256
LANES = 128
FLAGS = 384
FLAG = 15
NEWTON = ((0.05, 5), (0.001, 7))
REFINE = 2
MISS = 1e-3
LIMIT = 60 * 1024 * 1024


def dot(a, b):
    return lax.dot_general(a, b, (((1,), (0,)), ((), ())), preferred_element_type=F32)


def dot_nt(a, b):
    return lax.dot_general(a, b, (((1,), (1,)), ((), ())), preferred_element_type=F32)


def split(a):
    head = a.astype(BF16)
    return head, (a - head.astype(F32)).astype(BF16)


def index(shape, axis):
    return lax.broadcasted_iota(jnp.int32, shape, axis)


def one_hot(mask):
    return jnp.where(mask, 1.0, 0.0).astype(BF16)


def chol_id(y, z, x):
    return {"chol": y * 16 + z * 4 + x}


def others(at):
    return [lax.rem(at + k, SIDE) for k in range(1, SIDE)]


def remote(src, dst, send, recv, peer):
    return pltpu.make_async_remote_copy(
        src_ref=src, dst_ref=dst, send_sem=send, recv_sem=recv, device_id=peer, device_id_type=MESH
    )


def start(copies):
    for copy in copies:
        copy.start()


def received(copies):
    for copy in copies:
        copy.wait_recv()


def sent(copies):
    for copy in copies:
        copy.wait_send()


def inverse_of(top, tuned, products):
    occ = top.shape[0]
    gram = dot_nt(top, top)
    scale = 0.999 / jnp.max(jnp.sum(jnp.abs(gram), axis=1, keepdims=True), axis=0, keepdims=True)
    inv, square = top.astype(F32) * scale, gram * scale
    least = tuned
    for turn in range(products):
        c = 2.0 / (1.0 + least)
        least = 1.0 - ((1.0 - least) / (1.0 + least)) ** 2
        near = inv.astype(BF16)
        if turn > 0:
            square = dot_nt(near, top)
        inv = (2.0 * c) * inv - (c * c) * dot(square.astype(BF16), near)
    eye = jnp.where(index((occ, occ), 0) == index((occ, occ), 1), 1.0, 0.0)
    for _ in range(REFINE):
        head, rest = split(inv)
        miss = eye - (dot_nt(rest, top) + dot_nt(head, top))
        inv = inv + dot(miss.astype(BF16), head)
    return inv, jnp.sum(jnp.sum(miss * miss, axis=1, keepdims=True), axis=0, keepdims=True)


def theta_rows(inv, phi_t, x):
    occ, orb = phi_t.shape
    shape = (SIDE * PAD, occ)
    row, col = index(shape, 0), index(shape, 1)
    sel = one_hot((col == (row // PAD * SIDE + x) * ROWS + row % PAD) & (row % PAD < ROWS))
    head, rest = [dot(sel, part).astype(BF16) for part in split(inv)]
    theta = dot(rest, phi_t[...]) + dot(head, phi_t[...])
    return theta.astype(BF16).reshape(SIDE, PAD, orb)


def eight(block, part):
    y, z = part // 2, 2 * (part % 2)
    return jnp.concatenate([block(y, z + k // SIDE, k % SIDE) for k in range(8)], axis=0)


def pick_rows():
    shape = (8 * ROWS, 8 * PAD)
    row, col = index(shape, 0), index(shape, 1)
    return row % ROWS, col % PAD, row // ROWS == col // PAD


def compact(block, out, these):
    row, col, same = pick_rows()
    pick = one_hot(same & (row == col))
    for part in these:
        out[8 * ROWS * part : 8 * ROWS * (part + 1), :] = dot(pick, eight(block, part)).astype(BF16)


def compact_packed(block, out, c):
    row, col, same = pick_rows()
    pick = one_hot(same & (row == col))
    rest = [one_hot(same & (col == ROWS + row // 4) & (row % 4 == 2 * c + e)) for e in range(2)]
    for part in range(8):
        piece = eight(block, part)
        rows = pl.ds(8 * ROWS * part, 8 * ROWS)
        out[rows, HALF * c : HALF * (c + 1)] = dot(pick, piece).astype(BF16)
        tail = sum(dot(rest[e], piece[:, LANES * e : LANES * (e + 1)]) for e in range(2))
        if c > 0:
            tail = tail + out[rows, 2 * HALF :].astype(F32)
        out[rows, 2 * HALF :] = tail.astype(BF16)


def bias_rows(green, chol):
    rows, vecs, _ = chol.shape
    row = index(green.shape, 0) % PAD
    acc = sum(dot_nt(jnp.where(row == r, green, jnp.zeros_like(green)), chol[r]) for r in range(rows))
    return jnp.sum(acc.reshape(SIDE, PAD, vecs), axis=1)


def potential_chunk(field, chol, c):
    rows, vecs, _ = chol.shape
    field = jnp.broadcast_to(field[:, None, :], (SIDE, PAD, vecs)).reshape(SIDE * PAD, vecs).astype(BF16)
    row = index(field.shape, 0) % PAD
    none = jnp.zeros_like(field)
    lanes = slice(HALF * c, HALF * (c + 1))
    main = sum(dot(jnp.where(row == r, field, none), chol[r, :, lanes]) for r in range(rows))
    tails = [
        sum(dot(jnp.where(row == ROWS + r // 4, field, none), chol[r, :, 2 * HALF :]) for r in range(2 * c + e, rows, 4))
        for e in range(2)
    ]
    whole = SQRT_DT * (main + jnp.concatenate(tails, axis=1))
    return whole.astype(BF16).reshape(SIDE, PAD, HALF)


def pack_picks(picks, y, x):
    shape = picks.shape[1:]
    row, col = index(shape, 0), index(shape, 1)
    base, r = (y * 16 + row // PAD * SIDE + x) * ROWS, row % PAD
    picks[0] = one_hot((col == base + r) & (r < ROWS))
    for s in range(4):
        at = 4 * (r - ROWS) + s
        picks[1 + s] = one_hot((col == base + at) & (at >= 0) & (at < ROWS))


def pack_walker(phi_t, picks, blocks, missed):
    occ, _ = phi_t.shape
    rest = occ - LANES
    whole = dot_nt(picks[0], phi_t[:LANES, :])
    copies = jnp.concatenate([phi_t[LANES:, :]] * 4, axis=0)
    lane = index((SIDE * PAD, LANES), 1) // rest
    for s in range(4):
        whole = whole + jnp.where(lane == s, dot_nt(picks[1 + s], copies), 0.0)
    whole = jnp.where(index(whole.shape, 0) % PAD == FLAG, missed, whole)
    blocks[...] = whole.astype(BF16).reshape(SIDE, PAD, LANES)


def kernel(
    walkers, chol_hbm, noise, sources, out, bias, missed_out,
    chol, padded, first_grid, phi, phi_t, theta, slab_theta, parts, halves, blocks, grid, pot, picks, packed, everyone,
    send0, recv0, send, recv, bias_send, bias_recv, last_send, last_recv, chol_sem, ready,
):
    d, pop = lax.axis_index("chol"), lax.axis_index("pop")
    y, z, x = d // 16, (d // 4) % 4, d % 4
    slab, pair = z * SIDE + x, x // 2
    near, far = x + 1 - 2 * (x % 2), lax.rem(x + 2, SIDE)
    hi, core = pop // 2, pop % 2
    load = pltpu.make_async_copy(chol_hbm, chol, chol_sem)
    load.start()

    ys, zs, xs = others(y), others(z), others(x)
    ring = []
    for k in range(1, 16):
        place = lax.rem(hi * 4 + z + k, 16)
        ring.append((place // 4, place % 4))
    twin = {"pop": hi * 2 + 1 - core}
    ring_peers = [{"chol": y * 16 + b * 4 + x, "pop": h * 2 + core} for h, b in ring]
    z_peers = [chol_id(y, b, x) for b in zs]
    y_peers = [chol_id(b, z, x) for b in ys]
    x_peers = [chol_id(y, z, b) for b in xs]
    barrier = pltpu.get_barrier_semaphore()

    def greet(peers):
        for peer in peers:
            pl.semaphore_signal(barrier, inc=1, device_id=peer, device_id_type=MESH)

    hi_peers = [{"pop": lax.rem(hi + k, 4) * 2 + core} for k in range(1, 4)]
    lines = z_peers + x_peers + y_peers + hi_peers + [twin]
    greet(lines)
    padded[...] = jnp.zeros_like(padded)
    padded[:, :ROWS, :] = jnp.swapaxes(walkers[...].astype(F32), 0, 1).astype(BF16)

    pl.semaphore_wait(barrier, len(lines))

    def pushes(ref, peers, sems, base):
        return [remote(ref, ref, sems[0].at[base + k], sems[1].at[base + k], p) for k, p in enumerate(peers)]

    sems0 = send0, recv0
    upper = z // 2
    spot = first_grid.at[upper, x + upper * (y - x), y + upper * (x - y), z % 2]
    first = [
        remote(padded.at[w], spot, send0.at[k], recv0.at[k], peer)
        for k, (w, peer) in enumerate(zip(zs, z_peers, strict=True))
    ]
    start(first)
    spot[...] = padded[z]
    received(first)
    along_y = pushes(first_grid.at[0, x, y], y_peers, sems0, 3)
    along_x = pushes(first_grid.at[1, y, x], x_peers, sems0, 6)
    then_y = pushes(first_grid.at[1, y], y_peers, sems0, 9)
    start(along_y + along_x)
    for peer in hi_peers:
        pl.semaphore_signal(ready, inc=1, device_id=peer, device_id_type=MESH)

    def first_block(b, c, e):
        return first_grid[0, e, b, c] if c < 2 else first_grid[1, b, e, c - 2]

    @pl.when(y != 0)
    def _():
        then_x = pushes(first_grid.at[0, x], x_peers, sems0, 12)
        received(along_y)
        start(then_x)
        received(along_x)
        start(then_y)
        sent(first + along_y + along_x)
        received(then_x + then_y)
        compact(first_block, phi, range(8))
        phi_t[...] = phi[...].astype(F32).T.astype(BF16)
        sent(then_x + then_y)

    drain = []
    for s in range(STEPS):
        to_slab = [
            remote(theta.at[s, b], slab_theta.at[s, z], send.at[s, k], recv.at[s, k], peer)
            for k, (b, peer) in enumerate(zip(zs, z_peers, strict=True))
        ]
        pairs = [(lax.rem(z + k // 2, SIDE), (x, near)[k % 2]) for k in range(1, 8)]
        to_pair = [
            remote(parts.at[s, slab], parts.at[s, slab], bias_send.at[s, k], bias_recv.at[s, k], chol_id(0, b, c))
            for k, (b, c) in enumerate(pairs)
        ]
        half = halves.at[s, pair]
        to_rows = [
            remote(half, half, bias_send.at[s, 7 + k], bias_recv.at[s, 7 + pair], peer)
            for k, peer in enumerate([chol_id(b, z, c) for c in (x, far) for b in range(SIDE)][1:])
        ]

        def half_arrives(which, s=s):
            pltpu.make_async_copy(halves.at[s, which], halves.at[s, which], bias_recv.at[s, 7 + which]).wait()

        @pl.when(y == 0)
        def _(s=s, drain=drain, led=led if s else []):
            if s == 0:
                early = pushes(first_grid.at[0, x, 0], x_peers, sems0, 15)
                then_x = pushes(first_grid.at[0, x, pl.ds(1, 3)], x_peers, sems0, 12)
                start(early)
                received(along_y)
                start(then_x)
                received(along_x)
                start(then_y)
                received(early)
                compact(first_block, phi, range(2))
                inv, size = inverse_of(phi[: phi.shape[1], :], *NEWTON[s])
                received(then_x + then_y)
                compact(first_block, phi, range(2, 8))
                phi_t[...] = phi[...].astype(F32).T.astype(BF16)
            else:
                top = phi_t[:, : phi_t.shape[0]].astype(F32).T.astype(BF16)
                inv, size = inverse_of(top, *NEWTON[s])
            theta[s] = theta_rows(inv, phi_t, x)
            start(to_slab)
            slab_theta[s, z] = theta[s, z]
            if s == 0:
                sent(first + along_y + along_x + early + then_x + then_y)
                load.wait()
                pack_picks(picks, y, x)
            sent(drain + led)
            missed = jnp.where(size < MISS, 0.0, 1.0)
            mine = parts.at[s, slab]
            mine[...] = jnp.zeros(mine.shape, F32)
            flags = index((SIDE, LANES), 0) == z
            mine[:, FLAGS:] = jnp.where(flags, missed, 0.0)
            received(to_slab)
            mine[:, : chol.shape[1]] = bias_rows(slab_theta[s].reshape(SIDE * PAD, chol.shape[2]), chol)
            start(to_pair)
            received(to_pair)
            half[...] = sum(parts[s, SIDE * b + 2 * pair + e] for e in range(2) for b in range(SIDE))
            start(to_rows)
            half_arrives(1 - pair)

        @pl.when(y != 0)
        def _(s=s, drain=drain):
            sent(drain)
            if s == 0:
                load.wait()
                pack_picks(picks, y, x)
            half_arrives(0)
            half_arrives(1)

        total = halves[s, 0] + halves[s, 1]
        flag = jnp.sum(jnp.where(index((SIDE, LANES), 0) == z, total[:, FLAGS:], 0.0), axis=0, keepdims=True)[:, :1]
        missed = flag if s == 0 else missed + flag
        total = SQRT_DT * total[:, : chol.shape[1]]
        field = (noise[s] - total).astype(BF16).astype(F32)

        sems = send.at[s, pl.ds(3, 18)], recv.at[s, pl.ds(3, 18)]
        firsts, alongs, thens = [], [], []
        for c, (u, v) in enumerate([(x, y), (y, x)]):
            blocks[s, c] = potential_chunk(field, chol, c)
            spot = grid.at[s, c, u, v, z]
            firsts.append([
                remote(blocks.at[s, c, w], spot, sems[0].at[9 * c + k], sems[1].at[9 * c + k], peer)
                for k, (w, peer) in enumerate(zip(zs, z_peers, strict=True))
            ])
            start(firsts[c])
            spot[...] = blocks[s, c, z]
        for c, (u, v, peers) in enumerate([(x, y, y_peers), (y, x, x_peers)]):
            received(firsts[c])
            alongs.append(pushes(grid.at[s, c, u, v], peers, sems, 9 * c + 3))
            start(alongs[c])
        for c, (u, peers) in enumerate([(x, x_peers), (y, y_peers)]):
            received(alongs[c])
            thens.append(pushes(grid.at[s, c, u], peers, sems, 9 * c + 6))
            start(thens[c])
        share = one_hot(index((chol.shape[1], 8), 0) == d * bias.shape[2] + index((chol.shape[1], 8), 1)).astype(F32)
        bias[s] = jnp.dot(total, share, precision=lax.Precision.HIGHEST, preferred_element_type=F32)[:, : bias.shape[2]]
        received(thens[0])
        compact_packed(lambda b, c, e, s=s: grid[s, 0, e, b, c], pot, 0)
        received(thens[1])
        compact_packed(lambda b, c, e, s=s: grid[s, 1, b, e, c], pot, 1)

        term = phi_t[...]
        sum_of = term.astype(F32)
        for order in range(1, ORDER + 1):
            term = (-dot_nt(term, pot[...]) / order).astype(BF16)
            sum_of = sum_of + term.astype(F32)
        phi_t[...] = sum_of.astype(BF16)
        drain = sum(firsts + alongs + thens, [])
        led = to_slab + to_pair + to_rows

    pl.semaphore_wait(ready, len(hi_peers))
    pack_walker(phi_t, picks, packed, missed)
    spot = everyone.at[hi, core, z]
    to_ring = [
        remote(packed.at[b], spot, last_send.at[k], last_recv.at[k], peer)
        for k, ((_, b), peer) in enumerate(zip(ring, ring_peers, strict=True))
    ]
    start(to_ring)
    everyone[hi, core, z] = packed[z]
    sent(drain)

    @pl.when(y == 0)
    def _():
        sent(led)

    received(to_ring)
    mine = everyone.at[:, core]
    to_twin = [remote(mine, mine, last_send.at[15], last_recv.at[15], twin)]
    start(to_twin)
    sent(to_ring)
    received(to_twin)

    chosen = []
    for slot in range(SIDE):
        source = sources[slot]
        chosen.append(everyone[source // 8, source // 4 % 2, source % 4])
    whole = jnp.concatenate(chosen, axis=0)
    rest = out.shape[2] - LANES
    shape = (SIDE * PAD, SIDE * PAD)
    row, col = index(shape, 0), index(shape, 1)
    r = row % PAD
    back = one_hot(index((LANES, rest), 0) % rest == index((LANES, rest), 1))
    lane = index((SIDE * PAD, LANES), 1) // rest
    tail = jnp.zeros((SIDE * PAD, LANES), F32)
    for s in range(4):
        pick = one_hot((row // PAD == col // PAD) & (col % PAD == ROWS + r // 4) & (r % 4 == s) & (r < ROWS))
        tail = tail + jnp.where(lane == s, dot(pick, whole), 0.0)
    tail = dot(tail.astype(BF16), back)
    whole = jnp.concatenate([whole.astype(F32), tail], axis=1).reshape(SIDE, PAD, LANES + rest)
    out[...] = jnp.swapaxes(whole[:, :ROWS, :], 0, 1).astype(BF16)
    flags = everyone[...].reshape(8 * SIDE, PAD, LANES).astype(F32)
    bad = jnp.where((index(flags.shape, 1) == FLAG) & jnp.logical_not(flags == 0.0), 1.0, 0.0)
    missed_out[...] = jnp.max(jnp.max(bad, axis=0), axis=0, keepdims=True)
    sent(to_twin)


def propagate(walkers, chol, noise, sources):
    rows, vecs, orb = chol.shape
    occ = walkers.shape[2]
    dma = pltpu.SemaphoreType.DMA
    vmem = pl.BlockSpec(memory_space=VMEM)
    return pl.pallas_call(
        kernel,
        out_shape=(
            jax.ShapeDtypeStruct((rows, SIDE, occ), BF16),
            jax.ShapeDtypeStruct((STEPS, SIDE, vecs // SIDE**3), F32),
            jax.ShapeDtypeStruct((1, LANES), F32),
        ),
        in_specs=[vmem, pl.BlockSpec(memory_space=pl.ANY), vmem, pl.BlockSpec(memory_space=pltpu.SMEM)],
        out_specs=(vmem, vmem, vmem),
        scratch_shapes=[
            VMEM((rows, vecs, orb), BF16),
            VMEM((SIDE, PAD, occ), BF16),
            VMEM((2, SIDE, SIDE, 2, PAD, occ), BF16),
            VMEM((orb, occ), BF16),
            VMEM((occ, orb), BF16),
            VMEM((STEPS, SIDE, PAD, orb), BF16),
            VMEM((STEPS, SIDE, PAD, orb), BF16),
            VMEM((STEPS, 16, SIDE, FLAGS + LANES), F32),
            VMEM((STEPS, 2, SIDE, FLAGS + LANES), F32),
            VMEM((STEPS, 2, SIDE, PAD, HALF), BF16),
            VMEM((STEPS, 2, SIDE, SIDE, SIDE, PAD, HALF), BF16),
            VMEM((orb, orb), BF16),
            VMEM((5, SIDE * PAD, orb), BF16),
            VMEM((SIDE, PAD, LANES), BF16),
            VMEM((SIDE, 2, SIDE, PAD, LANES), BF16),
            dma((18,)),
            dma((18,)),
            dma((STEPS, 21)),
            dma((STEPS, 21)),
            dma((STEPS, 14)),
            dma((STEPS, 9)),
            dma((16,)),
            dma((16,)),
            dma,
            pltpu.SemaphoreType.REGULAR,
        ],
        compiler_params=pltpu.CompilerParams(collective_id=0, has_side_effects=True, vmem_limit_bytes=LIMIT),
        name="propagate",
    )(walkers, chol, noise, sources)


def solve_each(factor, target):
    return jax.scipy.linalg.cho_solve((factor, True), target)


def by_cholesky(walkers, chol_vectors, noise, sources):
    walk_count, row_count, occ_count = walkers.shape
    vec_count, _, orb_count = chol_vectors.shape
    first_row = lax.axis_index("chol") * row_count
    flat_chol = chol_vectors.reshape(vec_count, row_count * orb_count)
    current = walkers
    biases = []
    for step_index in range(STEPS):
        gathered = lax.all_gather(current, "chol", axis=1, tiled=True)
        phi = gathered.astype(F32)
        top_plain = gathered[:, :occ_count, :]
        gram = jnp.einsum("wai,waj->wij", top_plain, top_plain, preferred_element_type=F32)
        factor = jnp.linalg.cholesky(gram)
        inverse = jax.vmap(solve_each)(factor, jnp.swapaxes(phi[:, :occ_count, :], 1, 2))
        inverse_wide = jnp.pad(inverse, ((0, 0), (0, 0), (0, orb_count - occ_count)))
        inverse_cols = lax.dynamic_slice_in_dim(inverse_wide, first_row, row_count, 2)
        theta_slab = jnp.einsum("wja,wai->wji", phi, inverse_cols, precision=lax.Precision.HIGHEST).astype(BF16)
        green = jnp.swapaxes(theta_slab, 1, 2).reshape(walk_count, row_count * orb_count)
        partial_bias = lax.dot_general(green, flat_chol, (((1,), (1,)), ((), ())), preferred_element_type=F32)
        bias_now = SQRT_DT * lax.psum(partial_bias, "chol")
        biases.append(bias_now)
        field = (noise[step_index] - bias_now).astype(BF16)
        potential = SQRT_DT * jnp.dot(field, flat_chol, preferred_element_type=F32)
        potential = potential.reshape(walk_count, row_count, orb_count).astype(BF16)
        total = current.astype(F32)
        term = current
        for order in range(1, ORDER + 1):
            whole = gathered if order == 1 else lax.all_gather(term, "chol", axis=1, tiled=True)
            product = jnp.einsum("wij,wjb->wib", potential, whole, preferred_element_type=F32)
            term = (-product / order).astype(BF16)
            total = total + term.astype(F32)
        current = total.astype(BF16)
    everyone = lax.all_gather(current, "pop", axis=0, tiled=True)
    return everyone[sources], jnp.stack(biases)


def local(walkers, chol_vectors, noise, sources):
    vec_count = chol_vectors.shape[0]
    share = vec_count // lax.axis_size("chol")
    branched, bias, missed = propagate(
        jnp.transpose(walkers, (1, 0, 2)), jnp.transpose(chol_vectors, (1, 0, 2)), noise, sources
    )

    def by_share():
        branched, bias = by_cholesky(walkers, chol_vectors, noise, sources)
        return branched, lax.dynamic_slice_in_dim(bias, lax.axis_index("chol") * share, share, 2)

    return lax.cond(missed[0, 0] == 0.0, lambda: (jnp.transpose(branched, (1, 0, 2)), bias), by_share)


def solution(mesh):
    return jax.shard_map(
        local,
        mesh=mesh,
        in_specs=(P("pop", "chol", None), P(None, "chol", None), P(None, "pop", None), P("pop")),
        out_specs=(P("pop", "chol", None), P(None, "pop", "chol")),
        check_vma=False,
    )
```

```python
import jax
import jax.numpy as jnp
from jax import lax
from jax.experimental import pallas as pl
from jax.experimental.pallas import tpu as pltpu
from jax.sharding import PartitionSpec as P

STEPS = 2
ORDER = 4
SQRT_DT = 0.1
MESH = pl.DeviceIdType.MESH
F32 = jnp.float32
BF16 = jnp.bfloat16
VMEM = pltpu.VMEM
ROWS = 10
PAD = 16
SIDE = 4
HALF = 256
LANES = 128
FLAGS = 384
FLAG = 15
NEWTON = ((0.05, 5), (0.001, 7))
REFINE = 2
MISS = 1e-3
LIMIT = 60 * 1024 * 1024


def dot(a, b):
    return lax.dot_general(a, b, (((1,), (0,)), ((), ())), preferred_element_type=F32)


def dot_nt(a, b):
    return lax.dot_general(a, b, (((1,), (1,)), ((), ())), preferred_element_type=F32)


def split(a):
    head = a.astype(BF16)
    return head, (a - head.astype(F32)).astype(BF16)


def index(shape, axis):
    return lax.broadcasted_iota(jnp.int32, shape, axis)


def one_hot(mask):
    return jnp.where(mask, 1.0, 0.0).astype(BF16)


def chol_id(y, z, x):
    return {"chol": y * 16 + z * 4 + x}


def others(at):
    return [lax.rem(at + k, SIDE) for k in range(1, SIDE)]


def remote(src, dst, send, recv, peer):
    return pltpu.make_async_remote_copy(
        src_ref=src, dst_ref=dst, send_sem=send, recv_sem=recv, device_id=peer, device_id_type=MESH
    )


def start(copies):
    for copy in copies:
        copy.start()


def received(copies):
    for copy in copies:
        copy.wait_recv()


def sent(copies):
    for copy in copies:
        copy.wait_send()


def inverse_of(top, tuned, products):
    occ = top.shape[0]
    gram = dot_nt(top, top)
    scale = 0.999 / jnp.max(jnp.sum(jnp.abs(gram), axis=1, keepdims=True), axis=0, keepdims=True)
    inv, square = top.astype(F32) * scale, gram * scale
    least = tuned
    for turn in range(products):
        c = 2.0 / (1.0 + least)
        least = 1.0 - ((1.0 - least) / (1.0 + least)) ** 2
        near = inv.astype(BF16)
        if turn > 0:
            square = dot_nt(near, top)
        inv = (2.0 * c) * inv - (c * c) * dot(square.astype(BF16), near)
    eye = jnp.where(index((occ, occ), 0) == index((occ, occ), 1), 1.0, 0.0)
    for _ in range(REFINE):
        head, rest = split(inv)
        miss = eye - (dot_nt(rest, top) + dot_nt(head, top))
        inv = inv + dot(miss.astype(BF16), head)
    return inv, jnp.sum(jnp.sum(miss * miss, axis=1, keepdims=True), axis=0, keepdims=True)


def theta_rows(inv, phi_t, x):
    occ, orb = phi_t.shape
    shape = (SIDE * PAD, occ)
    row, col = index(shape, 0), index(shape, 1)
    sel = one_hot((col == (row // PAD * SIDE + x) * ROWS + row % PAD) & (row % PAD < ROWS))
    head, rest = [dot(sel, part).astype(BF16) for part in split(inv)]
    theta = dot(rest, phi_t[...]) + dot(head, phi_t[...])
    return theta.astype(BF16).reshape(SIDE, PAD, orb)


def eight(block, part):
    y, z = part // 2, 2 * (part % 2)
    return jnp.concatenate([block(y, z + k // SIDE, k % SIDE) for k in range(8)], axis=0)


def pick_rows():
    shape = (8 * ROWS, 8 * PAD)
    row, col = index(shape, 0), index(shape, 1)
    return row % ROWS, col % PAD, row // ROWS == col // PAD


def compact(block, out, these):
    row, col, same = pick_rows()
    pick = one_hot(same & (row == col))
    for part in these:
        out[8 * ROWS * part : 8 * ROWS * (part + 1), :] = dot(pick, eight(block, part)).astype(BF16)


def compact_packed(block, out, c):
    row, col, same = pick_rows()
    pick = one_hot(same & (row == col))
    rest = [one_hot(same & (col == ROWS + row // 4) & (row % 4 == 2 * c + e)) for e in range(2)]
    for part in range(8):
        piece = eight(block, part)
        rows = pl.ds(8 * ROWS * part, 8 * ROWS)
        out[rows, HALF * c : HALF * (c + 1)] = dot(pick, piece).astype(BF16)
        tail = sum(dot(rest[e], piece[:, LANES * e : LANES * (e + 1)]) for e in range(2))
        if c > 0:
            tail = tail + out[rows, 2 * HALF :].astype(F32)
        out[rows, 2 * HALF :] = tail.astype(BF16)


def bias_rows(green, chol):
    rows, vecs, _ = chol.shape
    row = index(green.shape, 0) % PAD
    acc = sum(dot_nt(jnp.where(row == r, green, jnp.zeros_like(green)), chol[r]) for r in range(rows))
    return jnp.sum(acc.reshape(SIDE, PAD, vecs), axis=1)


def potential_chunk(field, chol, c):
    rows, vecs, _ = chol.shape
    field = jnp.broadcast_to(field[:, None, :], (SIDE, PAD, vecs)).reshape(SIDE * PAD, vecs).astype(BF16)
    row = index(field.shape, 0) % PAD
    none = jnp.zeros_like(field)
    lanes = slice(HALF * c, HALF * (c + 1))
    main = sum(dot(jnp.where(row == r, field, none), chol[r, :, lanes]) for r in range(rows))
    tails = [
        sum(dot(jnp.where(row == ROWS + r // 4, field, none), chol[r, :, 2 * HALF :]) for r in range(2 * c + e, rows, 4))
        for e in range(2)
    ]
    whole = SQRT_DT * (main + jnp.concatenate(tails, axis=1))
    return whole.astype(BF16).reshape(SIDE, PAD, HALF)


def pack_picks(picks, y, x):
    shape = picks.shape[1:]
    row, col = index(shape, 0), index(shape, 1)
    base, r = (y * 16 + row // PAD * SIDE + x) * ROWS, row % PAD
    picks[0] = one_hot((col == base + r) & (r < ROWS))
    for s in range(4):
        at = 4 * (r - ROWS) + s
        picks[1 + s] = one_hot((col == base + at) & (at >= 0) & (at < ROWS))


def pack_walker(phi_t, picks, blocks, missed):
    occ, _ = phi_t.shape
    rest = occ - LANES
    whole = dot_nt(picks[0], phi_t[:LANES, :])
    copies = jnp.concatenate([phi_t[LANES:, :]] * 4, axis=0)
    lane = index((SIDE * PAD, LANES), 1) // rest
    for s in range(4):
        whole = whole + jnp.where(lane == s, dot_nt(picks[1 + s], copies), 0.0)
    whole = jnp.where(index(whole.shape, 0) % PAD == FLAG, missed, whole)
    blocks[...] = whole.astype(BF16).reshape(SIDE, PAD, LANES)


def kernel(
    walkers, chol_hbm, noise, sources, out, bias, missed_out,
    chol, padded, first_grid, phi, phi_t, theta, slab_theta, parts, sums, blocks, grid, pot, picks, packed, everyone,
    send0, recv0, send, recv, bias_send, bias_recv, last_send, last_recv, chol_sem, ready,
):
    d, pop = lax.axis_index("chol"), lax.axis_index("pop")
    y, z, x = d // 16, (d // 4) % 4, d % 4
    hi, core = pop // 2, pop % 2
    load = pltpu.make_async_copy(chol_hbm, chol, chol_sem)
    load.start()

    ys, zs, xs = others(y), others(z), others(x)
    ring = []
    for k in range(1, 16):
        place = lax.rem(hi * 4 + z + k, 16)
        ring.append((place // 4, place % 4))
    twin = {"pop": hi * 2 + 1 - core}
    ring_peers = [{"chol": y * 16 + b * 4 + x, "pop": h * 2 + core} for h, b in ring]
    z_peers = [chol_id(y, b, x) for b in zs]
    y_peers = [chol_id(b, z, x) for b in ys]
    x_peers = [chol_id(y, z, b) for b in xs]
    barrier = pltpu.get_barrier_semaphore()

    def greet(peers):
        for peer in peers:
            pl.semaphore_signal(barrier, inc=1, device_id=peer, device_id_type=MESH)

    hi_peers = [{"pop": lax.rem(hi + k, 4) * 2 + core} for k in range(1, 4)]
    lines = z_peers + x_peers + y_peers + hi_peers + [twin]
    greet(lines)
    padded[...] = jnp.zeros_like(padded)
    padded[:, :ROWS, :] = jnp.swapaxes(walkers[...].astype(F32), 0, 1).astype(BF16)

    pl.semaphore_wait(barrier, len(lines))

    def pushes(ref, peers, sems, base):
        return [remote(ref, ref, sems[0].at[base + k], sems[1].at[base + k], p) for k, p in enumerate(peers)]

    sems0 = send0, recv0
    upper = z // 2
    spot = first_grid.at[upper, x + upper * (y - x), y + upper * (x - y), z % 2]
    first = [
        remote(padded.at[w], spot, send0.at[k], recv0.at[k], peer)
        for k, (w, peer) in enumerate(zip(zs, z_peers, strict=True))
    ]
    start(first)
    spot[...] = padded[z]
    received(first)
    along_y = pushes(first_grid.at[0, x, y], y_peers, sems0, 3)
    along_x = pushes(first_grid.at[1, y, x], x_peers, sems0, 6)
    then_y = pushes(first_grid.at[1, y], y_peers, sems0, 9)
    start(along_y + along_x)
    for peer in hi_peers:
        pl.semaphore_signal(ready, inc=1, device_id=peer, device_id_type=MESH)

    def first_block(b, c, e):
        return first_grid[0, e, b, c] if c < 2 else first_grid[1, b, e, c - 2]

    @pl.when(y != 0)
    def _():
        then_x = pushes(first_grid.at[0, x], x_peers, sems0, 12)
        received(along_y)
        start(then_x)
        received(along_x)
        start(then_y)
        sent(first + along_y + along_x)
        received(then_x + then_y)
        compact(first_block, phi, range(8))
        phi_t[...] = phi[...].astype(F32).T.astype(BF16)
        sent(then_x + then_y)

    drain = []
    for s in range(STEPS):
        to_slab = [
            remote(theta.at[s, b], slab_theta.at[s, z], send.at[s, k], recv.at[s, k], peer)
            for k, (b, peer) in enumerate(zip(zs, z_peers, strict=True))
        ]
        spots = [(k // SIDE, lax.rem(z + k % SIDE, SIDE)) for k in range(1, 16)]
        to_sums = [
            remote(parts.at[s, z], parts.at[s, z], bias_send.at[s, k], bias_recv.at[s, z], chol_id(b, c, x))
            for k, (b, c) in enumerate(spots)
        ]
        to_x = [
            remote(sums.at[s, x], sums.at[s, x], bias_send.at[s, 15 + k], bias_recv.at[s, 4 + k], peer)
            for k, peer in enumerate(x_peers)
        ]

        def part_arrives(which, s=s):
            pltpu.make_async_copy(parts.at[s, which], parts.at[s, which], bias_recv.at[s, which]).wait()

        @pl.when(y == 0)
        def _(s=s, drain=drain, led=led if s else []):
            if s == 0:
                early = pushes(first_grid.at[0, x, 0], x_peers, sems0, 15)
                then_x = pushes(first_grid.at[0, x, pl.ds(1, 3)], x_peers, sems0, 12)
                start(early)
                received(along_y)
                start(then_x)
                received(along_x)
                start(then_y)
                received(early)
                compact(first_block, phi, range(2))
                inv, size = inverse_of(phi[: phi.shape[1], :], *NEWTON[s])
                received(then_x + then_y)
                compact(first_block, phi, range(2, 8))
                phi_t[...] = phi[...].astype(F32).T.astype(BF16)
            else:
                top = phi_t[:, : phi_t.shape[0]].astype(F32).T.astype(BF16)
                inv, size = inverse_of(top, *NEWTON[s])
            theta[s] = theta_rows(inv, phi_t, x)
            start(to_slab)
            slab_theta[s, z] = theta[s, z]
            if s == 0:
                sent(first + along_y + along_x + early + then_x + then_y)
                load.wait()
                pack_picks(picks, y, x)
            sent(drain + led)
            missed = jnp.where(size < MISS, 0.0, 1.0)
            mine = parts.at[s, z]
            mine[...] = jnp.zeros(mine.shape, F32)
            flags = index((SIDE, LANES), 0) == z
            mine[:, FLAGS:] = jnp.where(flags, missed, 0.0)
            received(to_slab)
            mine[:, : chol.shape[1]] = bias_rows(slab_theta[s].reshape(SIDE * PAD, chol.shape[2]), chol)
            start(to_sums)
            for which in zs:
                part_arrives(which)

        @pl.when(y != 0)
        def _(s=s, drain=drain):
            sent(drain)
            if s == 0:
                load.wait()
                pack_picks(picks, y, x)
            for which in range(SIDE):
                part_arrives(which)

        sums[s, x] = sum(parts[s, which] for which in range(SIDE))
        start(to_x)
        received(to_x)
        total = sum(sums[s, which] for which in range(SIDE))
        flag = jnp.sum(jnp.where(index((SIDE, LANES), 0) == z, total[:, FLAGS:], 0.0), axis=0, keepdims=True)[:, :1]
        missed = flag if s == 0 else missed + flag
        total = SQRT_DT * total[:, : chol.shape[1]]
        field = (noise[s] - total).astype(BF16).astype(F32)

        sems = send.at[s, pl.ds(3, 18)], recv.at[s, pl.ds(3, 18)]
        firsts, alongs, thens = [], [], []
        for c, (u, v) in enumerate([(x, y), (y, x)]):
            blocks[s, c] = potential_chunk(field, chol, c)
            spot = grid.at[s, c, u, v, z]
            firsts.append([
                remote(blocks.at[s, c, w], spot, sems[0].at[9 * c + k], sems[1].at[9 * c + k], peer)
                for k, (w, peer) in enumerate(zip(zs, z_peers, strict=True))
            ])
            start(firsts[c])
            spot[...] = blocks[s, c, z]
        for c, (u, v, peers) in enumerate([(x, y, y_peers), (y, x, x_peers)]):
            received(firsts[c])
            alongs.append(pushes(grid.at[s, c, u, v], peers, sems, 9 * c + 3))
            start(alongs[c])
        for c, (u, peers) in enumerate([(x, x_peers), (y, y_peers)]):
            received(alongs[c])
            thens.append(pushes(grid.at[s, c, u], peers, sems, 9 * c + 6))
            start(thens[c])
        share = one_hot(index((chol.shape[1], 8), 0) == d * bias.shape[2] + index((chol.shape[1], 8), 1)).astype(F32)
        bias[s] = jnp.dot(total, share, precision=lax.Precision.HIGHEST, preferred_element_type=F32)[:, : bias.shape[2]]
        received(thens[0])
        compact_packed(lambda b, c, e, s=s: grid[s, 0, e, b, c], pot, 0)
        received(thens[1])
        compact_packed(lambda b, c, e, s=s: grid[s, 1, b, e, c], pot, 1)

        term = phi_t[...]
        sum_of = term.astype(F32)
        for order in range(1, ORDER + 1):
            term = (-dot_nt(term, pot[...]) / order).astype(BF16)
            sum_of = sum_of + term.astype(F32)
        phi_t[...] = sum_of.astype(BF16)
        drain = sum(firsts + alongs + thens, to_x)
        led = to_slab + to_sums

    pl.semaphore_wait(ready, len(hi_peers))
    pack_walker(phi_t, picks, packed, missed)
    spot = everyone.at[hi, core, z]
    to_ring = [
        remote(packed.at[b], spot, last_send.at[k], last_recv.at[k], peer)
        for k, ((_, b), peer) in enumerate(zip(ring, ring_peers, strict=True))
    ]
    start(to_ring)
    everyone[hi, core, z] = packed[z]
    sent(drain)

    @pl.when(y == 0)
    def _():
        sent(led)

    received(to_ring)
    mine = everyone.at[:, core]
    to_twin = [remote(mine, mine, last_send.at[15], last_recv.at[15], twin)]
    start(to_twin)
    sent(to_ring)
    received(to_twin)

    chosen = []
    for slot in range(SIDE):
        source = sources[slot]
        chosen.append(everyone[source // 8, source // 4 % 2, source % 4])
    whole = jnp.concatenate(chosen, axis=0)
    rest = out.shape[2] - LANES
    shape = (SIDE * PAD, SIDE * PAD)
    row, col = index(shape, 0), index(shape, 1)
    r = row % PAD
    back = one_hot(index((LANES, rest), 0) % rest == index((LANES, rest), 1))
    lane = index((SIDE * PAD, LANES), 1) // rest
    tail = jnp.zeros((SIDE * PAD, LANES), F32)
    for s in range(4):
        pick = one_hot((row // PAD == col // PAD) & (col % PAD == ROWS + r // 4) & (r % 4 == s) & (r < ROWS))
        tail = tail + jnp.where(lane == s, dot(pick, whole), 0.0)
    tail = dot(tail.astype(BF16), back)
    whole = jnp.concatenate([whole.astype(F32), tail], axis=1).reshape(SIDE, PAD, LANES + rest)
    out[...] = jnp.swapaxes(whole[:, :ROWS, :], 0, 1).astype(BF16)
    flags = everyone[...].reshape(8 * SIDE, PAD, LANES).astype(F32)
    bad = jnp.where((index(flags.shape, 1) == FLAG) & jnp.logical_not(flags == 0.0), 1.0, 0.0)
    missed_out[...] = jnp.max(jnp.max(bad, axis=0), axis=0, keepdims=True)
    sent(to_twin)


def propagate(walkers, chol, noise, sources):
    rows, vecs, orb = chol.shape
    occ = walkers.shape[2]
    dma = pltpu.SemaphoreType.DMA
    vmem = pl.BlockSpec(memory_space=VMEM)
    return pl.pallas_call(
        kernel,
        out_shape=(
            jax.ShapeDtypeStruct((rows, SIDE, occ), BF16),
            jax.ShapeDtypeStruct((STEPS, SIDE, vecs // SIDE**3), F32),
            jax.ShapeDtypeStruct((1, LANES), F32),
        ),
        in_specs=[vmem, pl.BlockSpec(memory_space=pl.ANY), vmem, pl.BlockSpec(memory_space=pltpu.SMEM)],
        out_specs=(vmem, vmem, vmem),
        scratch_shapes=[
            VMEM((rows, vecs, orb), BF16),
            VMEM((SIDE, PAD, occ), BF16),
            VMEM((2, SIDE, SIDE, 2, PAD, occ), BF16),
            VMEM((orb, occ), BF16),
            VMEM((occ, orb), BF16),
            VMEM((STEPS, SIDE, PAD, orb), BF16),
            VMEM((STEPS, SIDE, PAD, orb), BF16),
            VMEM((STEPS, SIDE, SIDE, FLAGS + LANES), F32),
            VMEM((STEPS, SIDE, SIDE, FLAGS + LANES), F32),
            VMEM((STEPS, 2, SIDE, PAD, HALF), BF16),
            VMEM((STEPS, 2, SIDE, SIDE, SIDE, PAD, HALF), BF16),
            VMEM((orb, orb), BF16),
            VMEM((5, SIDE * PAD, orb), BF16),
            VMEM((SIDE, PAD, LANES), BF16),
            VMEM((SIDE, 2, SIDE, PAD, LANES), BF16),
            dma((18,)),
            dma((18,)),
            dma((STEPS, 21)),
            dma((STEPS, 21)),
            dma((STEPS, 18)),
            dma((STEPS, 7)),
            dma((16,)),
            dma((16,)),
            dma,
            pltpu.SemaphoreType.REGULAR,
        ],
        compiler_params=pltpu.CompilerParams(collective_id=0, has_side_effects=True, vmem_limit_bytes=LIMIT),
        name="propagate",
    )(walkers, chol, noise, sources)


def solve_each(factor, target):
    return jax.scipy.linalg.cho_solve((factor, True), target)


def by_cholesky(walkers, chol_vectors, noise, sources):
    walk_count, row_count, occ_count = walkers.shape
    vec_count, _, orb_count = chol_vectors.shape
    first_row = lax.axis_index("chol") * row_count
    flat_chol = chol_vectors.reshape(vec_count, row_count * orb_count)
    current = walkers
    biases = []
    for step_index in range(STEPS):
        gathered = lax.all_gather(current, "chol", axis=1, tiled=True)
        phi = gathered.astype(F32)
        top_plain = gathered[:, :occ_count, :]
        gram = jnp.einsum("wai,waj->wij", top_plain, top_plain, preferred_element_type=F32)
        factor = jnp.linalg.cholesky(gram)
        inverse = jax.vmap(solve_each)(factor, jnp.swapaxes(phi[:, :occ_count, :], 1, 2))
        inverse_wide = jnp.pad(inverse, ((0, 0), (0, 0), (0, orb_count - occ_count)))
        inverse_cols = lax.dynamic_slice_in_dim(inverse_wide, first_row, row_count, 2)
        theta_slab = jnp.einsum("wja,wai->wji", phi, inverse_cols, precision=lax.Precision.HIGHEST).astype(BF16)
        green = jnp.swapaxes(theta_slab, 1, 2).reshape(walk_count, row_count * orb_count)
        partial_bias = lax.dot_general(green, flat_chol, (((1,), (1,)), ((), ())), preferred_element_type=F32)
        bias_now = SQRT_DT * lax.psum(partial_bias, "chol")
        biases.append(bias_now)
        field = (noise[step_index] - bias_now).astype(BF16)
        potential = SQRT_DT * jnp.dot(field, flat_chol, preferred_element_type=F32)
        potential = potential.reshape(walk_count, row_count, orb_count).astype(BF16)
        total = current.astype(F32)
        term = current
        for order in range(1, ORDER + 1):
            whole = gathered if order == 1 else lax.all_gather(term, "chol", axis=1, tiled=True)
            product = jnp.einsum("wij,wjb->wib", potential, whole, preferred_element_type=F32)
            term = (-product / order).astype(BF16)
            total = total + term.astype(F32)
        current = total.astype(BF16)
    everyone = lax.all_gather(current, "pop", axis=0, tiled=True)
    return everyone[sources], jnp.stack(biases)


def local(walkers, chol_vectors, noise, sources):
    vec_count = chol_vectors.shape[0]
    share = vec_count // lax.axis_size("chol")
    branched, bias, missed = propagate(
        jnp.transpose(walkers, (1, 0, 2)), jnp.transpose(chol_vectors, (1, 0, 2)), noise, sources
    )

    def by_share():
        branched, bias = by_cholesky(walkers, chol_vectors, noise, sources)
        return branched, lax.dynamic_slice_in_dim(bias, lax.axis_index("chol") * share, share, 2)

    return lax.cond(missed[0, 0] == 0.0, lambda: (jnp.transpose(branched, (1, 0, 2)), bias), by_share)


def solution(mesh):
    return jax.shard_map(
        local,
        mesh=mesh,
        in_specs=(P("pop", "chol", None), P(None, "chol", None), P(None, "pop", None), P("pop")),
        out_specs=(P("pop", "chol", None), P(None, "pop", "chol")),
        check_vma=False,
    )
```

```python
import jax
import jax.numpy as jnp
from jax import lax
from jax.experimental import pallas as pl
from jax.experimental.pallas import tpu as pltpu
from jax.sharding import PartitionSpec as P

STEPS = 2
ORDER = 4
SQRT_DT = 0.1
MESH = pl.DeviceIdType.MESH
F32 = jnp.float32
BF16 = jnp.bfloat16
VMEM = pltpu.VMEM
ROWS = 10
PAD = 16
SIDE = 4
HALF = 256
LANES = 128
VIRT = 128
WINDOW = 256
FLAGS = 384
FLAG = 15
NEWTON = ((0.05, 5), (0.001, 7))
REFINE = 2
MISS = 1e-3
LIMIT = 60 * 1024 * 1024


def dot(a, b):
    return lax.dot_general(a, b, (((1,), (0,)), ((), ())), preferred_element_type=F32)


def dot_nt(a, b):
    return lax.dot_general(a, b, (((1,), (1,)), ((), ())), preferred_element_type=F32)


def split(a):
    head = a.astype(BF16)
    return head, (a - head.astype(F32)).astype(BF16)


def index(shape, axis):
    return lax.broadcasted_iota(jnp.int32, shape, axis)


def one_hot(mask):
    return jnp.where(mask, 1.0, 0.0).astype(BF16)


def chol_id(y, z, x):
    return {"chol": y * 16 + z * 4 + x}


def others(at):
    return [lax.rem(at + k, SIDE) for k in range(1, SIDE)]


def remote(src, dst, send, recv, peer):
    return pltpu.make_async_remote_copy(
        src_ref=src, dst_ref=dst, send_sem=send, recv_sem=recv, device_id=peer, device_id_type=MESH
    )


def start(copies):
    for copy in copies:
        copy.start()


def received(copies):
    for copy in copies:
        copy.wait_recv()


def sent(copies):
    for copy in copies:
        copy.wait_send()


def inverse_of(top, tuned, products):
    occ = top.shape[0]
    gram = dot_nt(top, top)
    scale = 0.999 / jnp.max(jnp.sum(jnp.abs(gram), axis=1, keepdims=True), axis=0, keepdims=True)
    inv, square = top.astype(F32) * scale, gram * scale
    least = tuned
    for turn in range(products):
        c = 2.0 / (1.0 + least)
        least = 1.0 - ((1.0 - least) / (1.0 + least)) ** 2
        near = inv.astype(BF16)
        if turn > 0:
            square = dot_nt(near, top)
        inv = (2.0 * c) * inv - (c * c) * dot(square.astype(BF16), near)
    eye = jnp.where(index((occ, occ), 0) == index((occ, occ), 1), 1.0, 0.0)
    for _ in range(REFINE):
        head, rest = split(inv)
        miss = eye - (dot_nt(rest, top) + dot_nt(head, top))
        inv = inv + dot(miss.astype(BF16), head)
    return inv, jnp.sum(jnp.sum(miss * miss, axis=1, keepdims=True), axis=0, keepdims=True)


def theta_rows(inv, phi_t, x):
    occ, orb = phi_t.shape
    shape = (SIDE * PAD, occ)
    row, col = index(shape, 0), index(shape, 1)
    sel = one_hot((col == (row // PAD * SIDE + x) * ROWS + row % PAD) & (row % PAD < ROWS))
    head, rest = [dot(sel, part).astype(BF16) for part in split(inv)]
    theta = dot(rest, phi_t[:, VIRT:]) + dot(head, phi_t[:, VIRT:])
    theta = jnp.where(index(theta.shape, 1) >= occ - VIRT, theta, 0.0)
    return theta.astype(BF16).reshape(SIDE, PAD, orb - VIRT)


def eight(block, part):
    y, z = part // 2, 2 * (part % 2)
    return jnp.concatenate([block(y, z + k // SIDE, k % SIDE) for k in range(8)], axis=0)


def pick_rows():
    shape = (8 * ROWS, 8 * PAD)
    row, col = index(shape, 0), index(shape, 1)
    return row % ROWS, col % PAD, row // ROWS == col // PAD


def compact(block, out, these):
    row, col, same = pick_rows()
    pick = one_hot(same & (row == col))
    for part in these:
        out[8 * ROWS * part : 8 * ROWS * (part + 1), :] = dot(pick, eight(block, part)).astype(BF16)


def compact_packed(block, out, c):
    row, col, same = pick_rows()
    pick = one_hot(same & (row == col))
    rest = [one_hot(same & (col == ROWS + row // 4) & (row % 4 == 2 * c + e)) for e in range(2)]
    for part in range(8):
        piece = eight(block, part)
        rows = pl.ds(8 * ROWS * part, 8 * ROWS)
        out[rows, HALF * c : HALF * (c + 1)] = dot(pick, piece).astype(BF16)
        tail = sum(dot(rest[e], piece[:, LANES * e : LANES * (e + 1)]) for e in range(2))
        if c > 0:
            tail = tail + out[rows, 2 * HALF :].astype(F32)
        out[rows, 2 * HALF :] = tail.astype(BF16)


def diagonal(chol, slab):
    rows = chol.shape[0]
    shape = (PAD, WINDOW)
    row, col = index(shape, 0), index(shape, 1)
    acc = sum(dot_nt(one_hot((row == r) & (col == slab * ROWS + r)), chol[r, :, :WINDOW]) for r in range(rows))
    return jnp.sum(acc, axis=0, keepdims=True)


def bias_rows(green, chol):
    rows, vecs, _ = chol.shape
    row = index(green.shape, 0) % PAD
    acc = sum(dot_nt(jnp.where(row == r, green, jnp.zeros_like(green)), chol[r, :, VIRT:]) for r in range(rows))
    return jnp.sum(acc.reshape(SIDE, PAD, vecs), axis=1)


def potential_chunk(field, chol, c):
    rows, vecs, _ = chol.shape
    field = jnp.broadcast_to(field[:, None, :], (SIDE, PAD, vecs)).reshape(SIDE * PAD, vecs).astype(BF16)
    row = index(field.shape, 0) % PAD
    none = jnp.zeros_like(field)
    lanes = slice(HALF * c, HALF * (c + 1))
    main = sum(dot(jnp.where(row == r, field, none), chol[r, :, lanes]) for r in range(rows))
    tails = [
        sum(dot(jnp.where(row == ROWS + r // 4, field, none), chol[r, :, 2 * HALF :]) for r in range(2 * c + e, rows, 4))
        for e in range(2)
    ]
    whole = SQRT_DT * (main + jnp.concatenate(tails, axis=1))
    return whole.astype(BF16).reshape(SIDE, PAD, HALF)


def pack_picks(picks, y, x):
    shape = picks.shape[1:]
    row, col = index(shape, 0), index(shape, 1)
    base, r = (y * 16 + row // PAD * SIDE + x) * ROWS - LANES * y, row % PAD
    picks[0] = one_hot((col == base + r) & (r < ROWS))
    for s in range(4):
        at = 4 * (r - ROWS) + s
        picks[1 + s] = one_hot((col == base + at) & (at >= 0) & (at < ROWS))


def pack_walker(phi_t, picks, blocks, y, missed):
    occ, _ = phi_t.shape
    rest = occ - LANES
    window = pl.ds(pl.multiple_of(LANES * y, LANES), WINDOW)
    whole = dot_nt(picks[0], phi_t[:LANES, window])
    copies = jnp.concatenate([phi_t[LANES:, window]] * 4, axis=0)
    lane = index((SIDE * PAD, LANES), 1) // rest
    for s in range(4):
        whole = whole + jnp.where(lane == s, dot_nt(picks[1 + s], copies), 0.0)
    whole = jnp.where(index(whole.shape, 0) % PAD == FLAG, missed, whole)
    blocks[...] = whole.astype(BF16).reshape(SIDE, PAD, LANES)


def kernel(
    walkers, chol_hbm, noise, sources, out, bias, missed_out,
    chol, padded, first_grid, phi, phi_t, theta, slab_theta, trace, parts, sums, blocks, grid, pot, picks, packed, everyone,
    send0, recv0, send, recv, bias_send, bias_recv, last_send, last_recv, chol_sem, ready,
):
    d, pop = lax.axis_index("chol"), lax.axis_index("pop")
    y, z, x = d // 16, (d // 4) % 4, d % 4
    hi, core = pop // 2, pop % 2
    load = pltpu.make_async_copy(chol_hbm, chol, chol_sem)
    load.start()

    ys, zs, xs = others(y), others(z), others(x)
    ring = []
    for k in range(1, 16):
        place = lax.rem(hi * 4 + z + k, 16)
        ring.append((place // 4, place % 4))
    twin = {"pop": hi * 2 + 1 - core}
    ring_peers = [{"chol": y * 16 + b * 4 + x, "pop": h * 2 + core} for h, b in ring]
    z_peers = [chol_id(y, b, x) for b in zs]
    y_peers = [chol_id(b, z, x) for b in ys]
    x_peers = [chol_id(y, z, b) for b in xs]
    barrier = pltpu.get_barrier_semaphore()

    def greet(peers):
        for peer in peers:
            pl.semaphore_signal(barrier, inc=1, device_id=peer, device_id_type=MESH)

    hi_peers = [{"pop": lax.rem(hi + k, 4) * 2 + core} for k in range(1, 4)]
    lines = z_peers + x_peers + y_peers + hi_peers + [twin]
    greet(lines)
    padded[...] = jnp.zeros_like(padded)
    padded[:, :ROWS, :] = jnp.swapaxes(walkers[...].astype(F32), 0, 1).astype(BF16)

    pl.semaphore_wait(barrier, len(lines))

    def pushes(ref, peers, sems, base):
        return [remote(ref, ref, sems[0].at[base + k], sems[1].at[base + k], p) for k, p in enumerate(peers)]

    sems0 = send0, recv0
    upper = z // 2
    spot = first_grid.at[upper, x + upper * (y - x), y + upper * (x - y), z % 2]
    first = [
        remote(padded.at[w], spot, send0.at[k], recv0.at[k], peer)
        for k, (w, peer) in enumerate(zip(zs, z_peers, strict=True))
    ]
    start(first)
    spot[...] = padded[z]
    received(first)
    along_y = pushes(first_grid.at[0, x, y], y_peers, sems0, 3)
    along_x = pushes(first_grid.at[1, y, x], x_peers, sems0, 6)
    then_y = pushes(first_grid.at[1, y], y_peers, sems0, 9)
    start(along_y + along_x)
    for peer in hi_peers:
        pl.semaphore_signal(ready, inc=1, device_id=peer, device_id_type=MESH)

    def first_block(b, c, e):
        return first_grid[0, e, b, c] if c < 2 else first_grid[1, b, e, c - 2]

    @pl.when(y != 0)
    def _():
        then_x = pushes(first_grid.at[0, x], x_peers, sems0, 12)
        received(along_y)
        start(then_x)
        received(along_x)
        start(then_y)
        sent(first + along_y + along_x)
        received(then_x + then_y)
        compact(first_block, phi, range(8))
        phi_t[...] = phi[...].astype(F32).T.astype(BF16)
        sent(then_x + then_y)

    drain = []
    for s in range(STEPS):
        to_slab = [
            remote(theta.at[s, b], slab_theta.at[s, z], send.at[s, k], recv.at[s, k], peer)
            for k, (b, peer) in enumerate(zip(zs, z_peers, strict=True))
        ]
        spots = [(k // SIDE, lax.rem(z + k % SIDE, SIDE)) for k in range(1, 16)]
        to_sums = [
            remote(parts.at[s, z], parts.at[s, z], bias_send.at[s, k], bias_recv.at[s, z], chol_id(b, c, x))
            for k, (b, c) in enumerate(spots)
        ]
        to_x = [
            remote(sums.at[s, x], sums.at[s, x], bias_send.at[s, 15 + k], bias_recv.at[s, 4 + k], peer)
            for k, peer in enumerate(x_peers)
        ]

        def part_arrives(which, s=s):
            pltpu.make_async_copy(parts.at[s, which], parts.at[s, which], bias_recv.at[s, which]).wait()

        @pl.when(y == 0)
        def _(s=s, drain=drain, led=led if s else []):
            if s == 0:
                early = pushes(first_grid.at[0, x, 0], x_peers, sems0, 15)
                then_x = pushes(first_grid.at[0, x, pl.ds(1, 3)], x_peers, sems0, 12)
                start(early)
                received(along_y)
                start(then_x)
                received(along_x)
                start(then_y)
                load.wait()
                trace[...] = diagonal(chol, z * SIDE + x)
                received(early)
                compact(first_block, phi, range(2))
                inv, size = inverse_of(phi[: phi.shape[1], :], *NEWTON[s])
                received(then_x + then_y)
                compact(first_block, phi, range(2, 8))
                phi_t[...] = phi[...].astype(F32).T.astype(BF16)
            else:
                top = phi_t[:, : phi_t.shape[0]].astype(F32).T.astype(BF16)
                inv, size = inverse_of(top, *NEWTON[s])
            theta[s] = theta_rows(inv, phi_t, x)
            start(to_slab)
            slab_theta[s, z] = theta[s, z]
            if s == 0:
                sent(first + along_y + along_x + early + then_x + then_y)
                pack_picks(picks, y, x)
            sent(drain + led)
            missed = jnp.where(size < MISS, 0.0, 1.0)
            mine = parts.at[s, z]
            mine[...] = jnp.zeros(mine.shape, F32)
            flags = index((SIDE, LANES), 0) == z
            mine[:, FLAGS:] = jnp.where(flags, missed, 0.0)
            received(to_slab)
            mine[:, : chol.shape[1]] = trace[...] + bias_rows(slab_theta[s].reshape(SIDE * PAD, chol.shape[2] - VIRT), chol)
            start(to_sums)
            for which in zs:
                part_arrives(which)

        @pl.when(y != 0)
        def _(s=s, drain=drain):
            sent(drain)
            if s == 0:
                load.wait()
                pack_picks(picks, y, x)
            for which in range(SIDE):
                part_arrives(which)

        sums[s, x] = sum(parts[s, which] for which in range(SIDE))
        start(to_x)
        received(to_x)
        total = sum(sums[s, which] for which in range(SIDE))
        flag = jnp.sum(jnp.where(index((SIDE, LANES), 0) == z, total[:, FLAGS:], 0.0), axis=0, keepdims=True)[:, :1]
        missed = flag if s == 0 else missed + flag
        total = SQRT_DT * total[:, : chol.shape[1]]
        field = (noise[s] - total).astype(BF16).astype(F32)

        sems = send.at[s, pl.ds(3, 18)], recv.at[s, pl.ds(3, 18)]
        firsts, alongs, thens = [], [], []
        for c, (u, v) in enumerate([(x, y), (y, x)]):
            blocks[s, c] = potential_chunk(field, chol, c)
            spot = grid.at[s, c, u, v, z]
            firsts.append([
                remote(blocks.at[s, c, w], spot, sems[0].at[9 * c + k], sems[1].at[9 * c + k], peer)
                for k, (w, peer) in enumerate(zip(zs, z_peers, strict=True))
            ])
            start(firsts[c])
            spot[...] = blocks[s, c, z]
        for c, (u, v, peers) in enumerate([(x, y, y_peers), (y, x, x_peers)]):
            received(firsts[c])
            alongs.append(pushes(grid.at[s, c, u, v], peers, sems, 9 * c + 3))
            start(alongs[c])
        for c, (u, peers) in enumerate([(x, x_peers), (y, y_peers)]):
            received(alongs[c])
            thens.append(pushes(grid.at[s, c, u], peers, sems, 9 * c + 6))
            start(thens[c])
        share = one_hot(index((chol.shape[1], 8), 0) == d * bias.shape[2] + index((chol.shape[1], 8), 1)).astype(F32)
        bias[s] = jnp.dot(total, share, precision=lax.Precision.HIGHEST, preferred_element_type=F32)[:, : bias.shape[2]]
        received(thens[0])
        compact_packed(lambda b, c, e, s=s: grid[s, 0, e, b, c], pot, 0)
        received(thens[1])
        compact_packed(lambda b, c, e, s=s: grid[s, 1, b, e, c], pot, 1)

        term = phi_t[...]
        sum_of = term.astype(F32)
        for order in range(1, ORDER + 1):
            term = (-dot_nt(term, pot[...]) / order).astype(BF16)
            sum_of = sum_of + term.astype(F32)
        phi_t[...] = sum_of.astype(BF16)
        drain = sum(firsts + alongs + thens, to_x)
        led = to_slab + to_sums

    pl.semaphore_wait(ready, len(hi_peers))
    pack_walker(phi_t, picks, packed, y, missed)
    spot = everyone.at[hi, core, z]
    to_ring = [
        remote(packed.at[b], spot, last_send.at[k], last_recv.at[k], peer)
        for k, ((_, b), peer) in enumerate(zip(ring, ring_peers, strict=True))
    ]
    start(to_ring)
    everyone[hi, core, z] = packed[z]
    sent(drain)

    @pl.when(y == 0)
    def _():
        sent(led)

    received(to_ring)
    mine = everyone.at[:, core]
    to_twin = [remote(mine, mine, last_send.at[15], last_recv.at[15], twin)]
    start(to_twin)
    sent(to_ring)
    received(to_twin)

    chosen = []
    for slot in range(SIDE):
        source = sources[slot]
        chosen.append(everyone[source // 8, source // 4 % 2, source % 4])
    whole = jnp.concatenate(chosen, axis=0)
    rest = out.shape[2] - LANES
    shape = (SIDE * PAD, SIDE * PAD)
    row, col = index(shape, 0), index(shape, 1)
    r = row % PAD
    back = one_hot(index((LANES, rest), 0) % rest == index((LANES, rest), 1))
    lane = index((SIDE * PAD, LANES), 1) // rest
    tail = jnp.zeros((SIDE * PAD, LANES), F32)
    for s in range(4):
        pick = one_hot((row // PAD == col // PAD) & (col % PAD == ROWS + r // 4) & (r % 4 == s) & (r < ROWS))
        tail = tail + jnp.where(lane == s, dot(pick, whole), 0.0)
    tail = dot(tail.astype(BF16), back)
    whole = jnp.concatenate([whole.astype(F32), tail], axis=1).reshape(SIDE, PAD, LANES + rest)
    out[...] = jnp.swapaxes(whole[:, :ROWS, :], 0, 1).astype(BF16)
    flags = everyone[...].reshape(8 * SIDE, PAD, LANES).astype(F32)
    bad = jnp.where((index(flags.shape, 1) == FLAG) & jnp.logical_not(flags == 0.0), 1.0, 0.0)
    missed_out[...] = jnp.max(jnp.max(bad, axis=0), axis=0, keepdims=True)
    sent(to_twin)


def propagate(walkers, chol, noise, sources):
    rows, vecs, orb = chol.shape
    occ = walkers.shape[2]
    dma = pltpu.SemaphoreType.DMA
    vmem = pl.BlockSpec(memory_space=VMEM)
    return pl.pallas_call(
        kernel,
        out_shape=(
            jax.ShapeDtypeStruct((rows, SIDE, occ), BF16),
            jax.ShapeDtypeStruct((STEPS, SIDE, vecs // SIDE**3), F32),
            jax.ShapeDtypeStruct((1, LANES), F32),
        ),
        in_specs=[vmem, pl.BlockSpec(memory_space=pl.ANY), vmem, pl.BlockSpec(memory_space=pltpu.SMEM)],
        out_specs=(vmem, vmem, vmem),
        scratch_shapes=[
            VMEM((rows, vecs, orb), BF16),
            VMEM((SIDE, PAD, occ), BF16),
            VMEM((2, SIDE, SIDE, 2, PAD, occ), BF16),
            VMEM((orb, occ), BF16),
            VMEM((occ, orb), BF16),
            VMEM((STEPS, SIDE, PAD, orb - VIRT), BF16),
            VMEM((STEPS, SIDE, PAD, orb - VIRT), BF16),
            VMEM((1, vecs), F32),
            VMEM((STEPS, SIDE, SIDE, FLAGS + LANES), F32),
            VMEM((STEPS, SIDE, SIDE, FLAGS + LANES), F32),
            VMEM((STEPS, 2, SIDE, PAD, HALF), BF16),
            VMEM((STEPS, 2, SIDE, SIDE, SIDE, PAD, HALF), BF16),
            VMEM((orb, orb), BF16),
            VMEM((5, SIDE * PAD, WINDOW), BF16),
            VMEM((SIDE, PAD, LANES), BF16),
            VMEM((SIDE, 2, SIDE, PAD, LANES), BF16),
            dma((18,)),
            dma((18,)),
            dma((STEPS, 21)),
            dma((STEPS, 21)),
            dma((STEPS, 18)),
            dma((STEPS, 7)),
            dma((16,)),
            dma((16,)),
            dma,
            pltpu.SemaphoreType.REGULAR,
        ],
        compiler_params=pltpu.CompilerParams(collective_id=0, has_side_effects=True, vmem_limit_bytes=LIMIT),
        name="propagate",
    )(walkers, chol, noise, sources)


def solve_each(factor, target):
    return jax.scipy.linalg.cho_solve((factor, True), target)


def by_cholesky(walkers, chol_vectors, noise, sources):
    walk_count, row_count, occ_count = walkers.shape
    vec_count, _, orb_count = chol_vectors.shape
    first_row = lax.axis_index("chol") * row_count
    flat_chol = chol_vectors.reshape(vec_count, row_count * orb_count)
    current = walkers
    biases = []
    for step_index in range(STEPS):
        gathered = lax.all_gather(current, "chol", axis=1, tiled=True)
        phi = gathered.astype(F32)
        top_plain = gathered[:, :occ_count, :]
        gram = jnp.einsum("wai,waj->wij", top_plain, top_plain, preferred_element_type=F32)
        factor = jnp.linalg.cholesky(gram)
        inverse = jax.vmap(solve_each)(factor, jnp.swapaxes(phi[:, :occ_count, :], 1, 2))
        inverse_wide = jnp.pad(inverse, ((0, 0), (0, 0), (0, orb_count - occ_count)))
        inverse_cols = lax.dynamic_slice_in_dim(inverse_wide, first_row, row_count, 2)
        theta_slab = jnp.einsum("wja,wai->wji", phi, inverse_cols, precision=lax.Precision.HIGHEST).astype(BF16)
        green = jnp.swapaxes(theta_slab, 1, 2).reshape(walk_count, row_count * orb_count)
        partial_bias = lax.dot_general(green, flat_chol, (((1,), (1,)), ((), ())), preferred_element_type=F32)
        bias_now = SQRT_DT * lax.psum(partial_bias, "chol")
        biases.append(bias_now)
        field = (noise[step_index] - bias_now).astype(BF16)
        potential = SQRT_DT * jnp.dot(field, flat_chol, preferred_element_type=F32)
        potential = potential.reshape(walk_count, row_count, orb_count).astype(BF16)
        total = current.astype(F32)
        term = current
        for order in range(1, ORDER + 1):
            whole = gathered if order == 1 else lax.all_gather(term, "chol", axis=1, tiled=True)
            product = jnp.einsum("wij,wjb->wib", potential, whole, preferred_element_type=F32)
            term = (-product / order).astype(BF16)
            total = total + term.astype(F32)
        current = total.astype(BF16)
    everyone = lax.all_gather(current, "pop", axis=0, tiled=True)
    return everyone[sources], jnp.stack(biases)


def local(walkers, chol_vectors, noise, sources):
    vec_count = chol_vectors.shape[0]
    share = vec_count // lax.axis_size("chol")
    branched, bias, missed = propagate(
        jnp.transpose(walkers, (1, 0, 2)), jnp.transpose(chol_vectors, (1, 0, 2)), noise, sources
    )

    def by_share():
        branched, bias = by_cholesky(walkers, chol_vectors, noise, sources)
        return branched, lax.dynamic_slice_in_dim(bias, lax.axis_index("chol") * share, share, 2)

    return lax.cond(missed[0, 0] == 0.0, lambda: (jnp.transpose(branched, (1, 0, 2)), bias), by_share)


def solution(mesh):
    return jax.shard_map(
        local,
        mesh=mesh,
        in_specs=(P("pop", "chol", None), P(None, "chol", None), P(None, "pop", None), P("pop")),
        out_specs=(P("pop", "chol", None), P(None, "pop", "chol")),
        check_vma=False,
    )
```

```python
import jax
import jax.numpy as jnp
from jax import lax
from jax.experimental import pallas as pl
from jax.experimental.pallas import tpu as pltpu
from jax.sharding import PartitionSpec as P

STEPS = 2
ORDER = 4
SQRT_DT = 0.1
MESH = pl.DeviceIdType.MESH
F32 = jnp.float32
BF16 = jnp.bfloat16
VMEM = pltpu.VMEM
ROWS = 10
PAD = 16
SIDE = 4
HALF = 256
LANES = 128
VIRT = 128
WINDOW = 256
FLAGS = 384
FLAG = 15
NEWTON = ((0.05, 5), (0.001, 7))
REFINE = 2
MISS = 1e-3
LIMIT = 60 * 1024 * 1024


def dot(a, b):
    return lax.dot_general(a, b, (((1,), (0,)), ((), ())), preferred_element_type=F32)


def dot_nt(a, b):
    return lax.dot_general(a, b, (((1,), (1,)), ((), ())), preferred_element_type=F32)


def split(a):
    head = a.astype(BF16)
    return head, (a - head.astype(F32)).astype(BF16)


def index(shape, axis):
    return lax.broadcasted_iota(jnp.int32, shape, axis)


def one_hot(mask):
    return jnp.where(mask, 1.0, 0.0).astype(BF16)


def chol_id(y, z, x):
    return {"chol": y * 16 + z * 4 + x}


def others(at):
    return [lax.rem(at + k, SIDE) for k in (2, 1, 3)]


def remote(src, dst, send, recv, peer):
    return pltpu.make_async_remote_copy(
        src_ref=src, dst_ref=dst, send_sem=send, recv_sem=recv, device_id=peer, device_id_type=MESH
    )


def start(copies):
    for copy in copies:
        copy.start()


def received(copies):
    for copy in copies:
        copy.wait_recv()


def sent(copies):
    for copy in copies:
        copy.wait_send()


def inverse_of(top, tuned, products):
    occ = top.shape[0]
    gram = dot_nt(top, top)
    scale = 0.999 / jnp.max(jnp.sum(jnp.abs(gram), axis=1, keepdims=True), axis=0, keepdims=True)
    inv, square = top.astype(F32) * scale, gram * scale
    least = tuned
    for turn in range(products):
        c = 2.0 / (1.0 + least)
        least = 1.0 - ((1.0 - least) / (1.0 + least)) ** 2
        near = inv.astype(BF16)
        if turn > 0:
            square = dot_nt(near, top)
        inv = (2.0 * c) * inv - (c * c) * dot(square.astype(BF16), near)
    eye = jnp.where(index((occ, occ), 0) == index((occ, occ), 1), 1.0, 0.0)
    for _ in range(REFINE):
        head, rest = split(inv)
        miss = eye - (dot_nt(rest, top) + dot_nt(head, top))
        inv = inv + dot(miss.astype(BF16), head)
    return inv, jnp.sum(jnp.sum(miss * miss, axis=1, keepdims=True), axis=0, keepdims=True)


def theta_rows(inv, phi_t, x):
    occ, orb = phi_t.shape
    shape = (SIDE * PAD, occ)
    row, col = index(shape, 0), index(shape, 1)
    sel = one_hot((col == (row // PAD * SIDE + x) * ROWS + row % PAD) & (row % PAD < ROWS))
    head, rest = [dot(sel, part).astype(BF16) for part in split(inv)]
    theta = dot(rest, phi_t[:, VIRT:]) + dot(head, phi_t[:, VIRT:])
    theta = jnp.where(index(theta.shape, 1) >= occ - VIRT, theta, 0.0)
    return theta.astype(BF16).reshape(SIDE, PAD, orb - VIRT)


def eight(block, part):
    y, z = part // 2, 2 * (part % 2)
    return jnp.concatenate([block(y, z + k // SIDE, k % SIDE) for k in range(8)], axis=0)


def pick_rows():
    shape = (8 * ROWS, 8 * PAD)
    row, col = index(shape, 0), index(shape, 1)
    return row % ROWS, col % PAD, row // ROWS == col // PAD


def compact(block, out, these):
    row, col, same = pick_rows()
    pick = one_hot(same & (row == col))
    for part in these:
        out[8 * ROWS * part : 8 * ROWS * (part + 1), :] = dot(pick, eight(block, part)).astype(BF16)


def compact_packed(block, out, c):
    row, col, same = pick_rows()
    pick = one_hot(same & (row == col))
    rest = [one_hot(same & (col == ROWS + row // 4) & (row % 4 == 2 * c + e)) for e in range(2)]
    for part in range(8):
        piece = eight(block, part)
        rows = pl.ds(8 * ROWS * part, 8 * ROWS)
        out[rows, HALF * c : HALF * (c + 1)] = dot(pick, piece).astype(BF16)
        tail = sum(dot(rest[e], piece[:, LANES * e : LANES * (e + 1)]) for e in range(2))
        if c > 0:
            tail = tail + out[rows, 2 * HALF :].astype(F32)
        out[rows, 2 * HALF :] = tail.astype(BF16)


def diagonal(chol, slab):
    rows = chol.shape[0]
    shape = (PAD, WINDOW)
    row, col = index(shape, 0), index(shape, 1)
    acc = sum(dot_nt(one_hot((row == r) & (col == slab * ROWS + r)), chol[r, :, :WINDOW]) for r in range(rows))
    return jnp.sum(acc, axis=0, keepdims=True)


def bias_rows(green, chol):
    rows, vecs, _ = chol.shape
    row = index(green.shape, 0) % PAD
    acc = sum(dot_nt(jnp.where(row == r, green, jnp.zeros_like(green)), chol[r, :, VIRT:]) for r in range(rows))
    return jnp.sum(acc.reshape(SIDE, PAD, vecs), axis=1)


def potential_chunk(field, chol, c):
    rows, vecs, _ = chol.shape
    field = jnp.broadcast_to(field[:, None, :], (SIDE, PAD, vecs)).reshape(SIDE * PAD, vecs).astype(BF16)
    row = index(field.shape, 0) % PAD
    none = jnp.zeros_like(field)
    lanes = slice(HALF * c, HALF * (c + 1))
    main = sum(dot(jnp.where(row == r, field, none), chol[r, :, lanes]) for r in range(rows))
    tails = [
        sum(dot(jnp.where(row == ROWS + r // 4, field, none), chol[r, :, 2 * HALF :]) for r in range(2 * c + e, rows, 4))
        for e in range(2)
    ]
    whole = SQRT_DT * (main + jnp.concatenate(tails, axis=1))
    return whole.astype(BF16).reshape(SIDE, PAD, HALF)


def pack_picks(picks, y, x):
    shape = picks.shape[1:]
    row, col = index(shape, 0), index(shape, 1)
    base, r = (y * 16 + row // PAD * SIDE + x) * ROWS - LANES * y, row % PAD
    picks[0] = one_hot((col == base + r) & (r < ROWS))
    for s in range(4):
        at = 4 * (r - ROWS) + s
        picks[1 + s] = one_hot((col == base + at) & (at >= 0) & (at < ROWS))


def pack_walker(phi_t, picks, blocks, y, missed):
    occ, _ = phi_t.shape
    rest = occ - LANES
    window = pl.ds(pl.multiple_of(LANES * y, LANES), WINDOW)
    whole = dot_nt(picks[0], phi_t[:LANES, window])
    copies = jnp.concatenate([phi_t[LANES:, window]] * 4, axis=0)
    lane = index((SIDE * PAD, LANES), 1) // rest
    for s in range(4):
        whole = whole + jnp.where(lane == s, dot_nt(picks[1 + s], copies), 0.0)
    whole = jnp.where(index(whole.shape, 0) % PAD == FLAG, missed, whole)
    blocks[...] = whole.astype(BF16).reshape(SIDE, PAD, LANES)


def kernel(
    walkers, chol_hbm, noise, sources, out, bias, missed_out,
    chol, padded, first_grid, phi, phi_t, theta, slab_theta, trace, parts, sums, blocks, grid, pot, picks, packed, everyone,
    send0, recv0, send, recv, bias_send, bias_recv, last_send, last_recv, chol_sem, ready,
):
    d, pop = lax.axis_index("chol"), lax.axis_index("pop")
    y, z, x = d // 16, (d // 4) % 4, d % 4
    hi, core = pop // 2, pop % 2
    load = pltpu.make_async_copy(chol_hbm, chol, chol_sem)
    load.start()

    ys, zs, xs = others(y), others(z), others(x)
    ring = []
    for k in sorted(range(1, 16), key=lambda k: abs(k - 8)):
        place = lax.rem(hi * 4 + z + k, 16)
        ring.append((place // 4, place % 4))
    twin = {"pop": hi * 2 + 1 - core}
    ring_peers = [{"chol": y * 16 + b * 4 + x, "pop": h * 2 + core} for h, b in ring]
    z_peers = [chol_id(y, b, x) for b in zs]
    y_peers = [chol_id(b, z, x) for b in ys]
    x_peers = [chol_id(y, z, b) for b in xs]
    barrier = pltpu.get_barrier_semaphore()

    def greet(peers):
        for peer in peers:
            pl.semaphore_signal(barrier, inc=1, device_id=peer, device_id_type=MESH)

    hi_peers = [{"pop": lax.rem(hi + k, 4) * 2 + core} for k in range(1, 4)]
    lines = z_peers + x_peers + y_peers + hi_peers + [twin]
    greet(lines)
    padded[...] = jnp.zeros_like(padded)
    padded[:, :ROWS, :] = jnp.swapaxes(walkers[...].astype(F32), 0, 1).astype(BF16)

    pl.semaphore_wait(barrier, len(lines))

    def pushes(ref, peers, sems, base):
        return [remote(ref, ref, sems[0].at[base + k], sems[1].at[base + k], p) for k, p in enumerate(peers)]

    sems0 = send0, recv0
    upper = z // 2
    spot = first_grid.at[upper, x + upper * (y - x), y + upper * (x - y), z % 2]
    first = [
        remote(padded.at[w], spot, send0.at[k], recv0.at[k], peer)
        for k, (w, peer) in enumerate(zip(zs, z_peers, strict=True))
    ]
    start(first)
    spot[...] = padded[z]
    received(first)
    along_y = pushes(first_grid.at[0, x, y], y_peers, sems0, 3)
    along_x = pushes(first_grid.at[1, y, x], x_peers, sems0, 6)
    then_y = pushes(first_grid.at[1, y], y_peers, sems0, 9)
    start(along_y + along_x)
    for peer in hi_peers:
        pl.semaphore_signal(ready, inc=1, device_id=peer, device_id_type=MESH)

    def first_block(b, c, e):
        return first_grid[0, e, b, c] if c < 2 else first_grid[1, b, e, c - 2]

    @pl.when(y != 0)
    def _():
        then_x = pushes(first_grid.at[0, x], x_peers, sems0, 12)
        received(along_y)
        start(then_x)
        received(along_x)
        start(then_y)
        sent(first + along_y + along_x)
        received(then_x + then_y)
        compact(first_block, phi, range(8))
        phi_t[...] = phi[...].astype(F32).T.astype(BF16)
        sent(then_x + then_y)

    drain = []
    for s in range(STEPS):
        to_slab = [
            remote(theta.at[s, b], slab_theta.at[s, z], send.at[s, k], recv.at[s, k], peer)
            for k, (b, peer) in enumerate(zip(zs, z_peers, strict=True))
        ]
        spots = [(k // SIDE, lax.rem(z + k % SIDE, SIDE)) for k in (10, 9, 11, 8, 6, 14, 5, 7, 13, 15, 4, 12, 2, 1, 3)]
        to_sums = [
            remote(parts.at[s, z], parts.at[s, z], bias_send.at[s, k], bias_recv.at[s, z], chol_id(b, c, x))
            for k, (b, c) in enumerate(spots)
        ]
        to_x = [
            remote(sums.at[s, x], sums.at[s, x], bias_send.at[s, 15 + k], bias_recv.at[s, 4 + k], peer)
            for k, peer in enumerate(x_peers)
        ]

        def part_arrives(which, s=s):
            pltpu.make_async_copy(parts.at[s, which], parts.at[s, which], bias_recv.at[s, which]).wait()

        @pl.when(y == 0)
        def _(s=s, drain=drain, led=led if s else []):
            if s == 0:
                early = pushes(first_grid.at[0, x, 0], x_peers, sems0, 15)
                then_x = pushes(first_grid.at[0, x, pl.ds(1, 3)], x_peers, sems0, 12)
                start(early)
                received(along_y)
                start(then_x)
                received(along_x)
                start(then_y)
                load.wait()
                trace[...] = diagonal(chol, z * SIDE + x)
                received(early)
                compact(first_block, phi, range(2))
                inv, size = inverse_of(phi[: phi.shape[1], :], *NEWTON[s])
                received(then_x + then_y)
                compact(first_block, phi, range(2, 8))
                phi_t[...] = phi[...].astype(F32).T.astype(BF16)
            else:
                top = phi_t[:, : phi_t.shape[0]].astype(F32).T.astype(BF16)
                inv, size = inverse_of(top, *NEWTON[s])
            theta[s] = theta_rows(inv, phi_t, x)
            start(to_slab)
            slab_theta[s, z] = theta[s, z]
            if s == 0:
                sent(first + along_y + along_x + early + then_x + then_y)
                pack_picks(picks, y, x)
            sent(drain + led)
            missed = jnp.where(size < MISS, 0.0, 1.0)
            mine = parts.at[s, z]
            mine[...] = jnp.zeros(mine.shape, F32)
            flags = index((SIDE, LANES), 0) == z
            mine[:, FLAGS:] = jnp.where(flags, missed, 0.0)
            received(to_slab)
            mine[:, : chol.shape[1]] = trace[...] + bias_rows(slab_theta[s].reshape(SIDE * PAD, chol.shape[2] - VIRT), chol)
            start(to_sums)
            for which in zs:
                part_arrives(which)

        @pl.when(y != 0)
        def _(s=s, drain=drain):
            sent(drain)
            if s == 0:
                load.wait()
                pack_picks(picks, y, x)
            for which in range(SIDE):
                part_arrives(which)

        sums[s, x] = sum(parts[s, which] for which in range(SIDE))
        start(to_x)
        received(to_x)
        total = sum(sums[s, which] for which in range(SIDE))
        flag = jnp.sum(jnp.where(index((SIDE, LANES), 0) == z, total[:, FLAGS:], 0.0), axis=0, keepdims=True)[:, :1]
        missed = flag if s == 0 else missed + flag
        total = SQRT_DT * total[:, : chol.shape[1]]
        field = (noise[s] - total).astype(BF16).astype(F32)

        sems = send.at[s, pl.ds(3, 18)], recv.at[s, pl.ds(3, 18)]
        firsts, alongs, thens = [], [], []
        for c, (u, v) in enumerate([(x, y), (y, x)]):
            blocks[s, c] = potential_chunk(field, chol, c)
            spot = grid.at[s, c, u, v, z]
            firsts.append([
                remote(blocks.at[s, c, w], spot, sems[0].at[9 * c + k], sems[1].at[9 * c + k], peer)
                for k, (w, peer) in enumerate(zip(zs, z_peers, strict=True))
            ])
            start(firsts[c])
            spot[...] = blocks[s, c, z]
        for c, (u, v, peers) in enumerate([(x, y, y_peers), (y, x, x_peers)]):
            received(firsts[c])
            alongs.append(pushes(grid.at[s, c, u, v], peers, sems, 9 * c + 3))
            start(alongs[c])
        for c, (u, peers) in enumerate([(x, x_peers), (y, y_peers)]):
            received(alongs[c])
            thens.append(pushes(grid.at[s, c, u], peers, sems, 9 * c + 6))
            start(thens[c])
        share = one_hot(index((chol.shape[1], 8), 0) == d * bias.shape[2] + index((chol.shape[1], 8), 1)).astype(F32)
        bias[s] = jnp.dot(total, share, precision=lax.Precision.HIGHEST, preferred_element_type=F32)[:, : bias.shape[2]]
        received(thens[0])
        compact_packed(lambda b, c, e, s=s: grid[s, 0, e, b, c], pot, 0)
        received(thens[1])
        compact_packed(lambda b, c, e, s=s: grid[s, 1, b, e, c], pot, 1)

        term = phi_t[...]
        sum_of = term.astype(F32)
        for order in range(1, ORDER + 1):
            term = (-dot_nt(term, pot[...]) / order).astype(BF16)
            sum_of = sum_of + term.astype(F32)
        phi_t[...] = sum_of.astype(BF16)
        drain = sum(firsts + alongs + thens, to_x)
        led = to_slab + to_sums

    pl.semaphore_wait(ready, len(hi_peers))
    pack_walker(phi_t, picks, packed, y, missed)
    spot = everyone.at[hi, core, z]
    to_ring = [
        remote(packed.at[b], spot, last_send.at[k], last_recv.at[k], peer)
        for k, ((_, b), peer) in enumerate(zip(ring, ring_peers, strict=True))
    ]
    start(to_ring)
    everyone[hi, core, z] = packed[z]
    sent(drain)

    @pl.when(y == 0)
    def _():
        sent(led)

    received(to_ring)
    mine = everyone.at[:, core]
    to_twin = [remote(mine, mine, last_send.at[15], last_recv.at[15], twin)]
    start(to_twin)
    sent(to_ring)
    received(to_twin)

    chosen = []
    for slot in range(SIDE):
        source = sources[slot]
        chosen.append(everyone[source // 8, source // 4 % 2, source % 4])
    whole = jnp.concatenate(chosen, axis=0)
    rest = out.shape[2] - LANES
    shape = (SIDE * PAD, SIDE * PAD)
    row, col = index(shape, 0), index(shape, 1)
    r = row % PAD
    back = one_hot(index((LANES, rest), 0) % rest == index((LANES, rest), 1))
    lane = index((SIDE * PAD, LANES), 1) // rest
    tail = jnp.zeros((SIDE * PAD, LANES), F32)
    for s in range(4):
        pick = one_hot((row // PAD == col // PAD) & (col % PAD == ROWS + r // 4) & (r % 4 == s) & (r < ROWS))
        tail = tail + jnp.where(lane == s, dot(pick, whole), 0.0)
    tail = dot(tail.astype(BF16), back)
    whole = jnp.concatenate([whole.astype(F32), tail], axis=1).reshape(SIDE, PAD, LANES + rest)
    out[...] = jnp.swapaxes(whole[:, :ROWS, :], 0, 1).astype(BF16)
    flags = everyone[...].reshape(8 * SIDE, PAD, LANES).astype(F32)
    bad = jnp.where((index(flags.shape, 1) == FLAG) & jnp.logical_not(flags == 0.0), 1.0, 0.0)
    missed_out[...] = jnp.max(jnp.max(bad, axis=0), axis=0, keepdims=True)
    sent(to_twin)


def propagate(walkers, chol, noise, sources):
    rows, vecs, orb = chol.shape
    occ = walkers.shape[2]
    dma = pltpu.SemaphoreType.DMA
    vmem = pl.BlockSpec(memory_space=VMEM)
    return pl.pallas_call(
        kernel,
        out_shape=(
            jax.ShapeDtypeStruct((rows, SIDE, occ), BF16),
            jax.ShapeDtypeStruct((STEPS, SIDE, vecs // SIDE**3), F32),
            jax.ShapeDtypeStruct((1, LANES), F32),
        ),
        in_specs=[vmem, pl.BlockSpec(memory_space=pl.ANY), vmem, pl.BlockSpec(memory_space=pltpu.SMEM)],
        out_specs=(vmem, vmem, vmem),
        scratch_shapes=[
            VMEM((rows, vecs, orb), BF16),
            VMEM((SIDE, PAD, occ), BF16),
            VMEM((2, SIDE, SIDE, 2, PAD, occ), BF16),
            VMEM((orb, occ), BF16),
            VMEM((occ, orb), BF16),
            VMEM((STEPS, SIDE, PAD, orb - VIRT), BF16),
            VMEM((STEPS, SIDE, PAD, orb - VIRT), BF16),
            VMEM((1, vecs), F32),
            VMEM((STEPS, SIDE, SIDE, FLAGS + LANES), F32),
            VMEM((STEPS, SIDE, SIDE, FLAGS + LANES), F32),
            VMEM((STEPS, 2, SIDE, PAD, HALF), BF16),
            VMEM((STEPS, 2, SIDE, SIDE, SIDE, PAD, HALF), BF16),
            VMEM((orb, orb), BF16),
            VMEM((5, SIDE * PAD, WINDOW), BF16),
            VMEM((SIDE, PAD, LANES), BF16),
            VMEM((SIDE, 2, SIDE, PAD, LANES), BF16),
            dma((18,)),
            dma((18,)),
            dma((STEPS, 21)),
            dma((STEPS, 21)),
            dma((STEPS, 18)),
            dma((STEPS, 7)),
            dma((16,)),
            dma((16,)),
            dma,
            pltpu.SemaphoreType.REGULAR,
        ],
        compiler_params=pltpu.CompilerParams(collective_id=0, has_side_effects=True, vmem_limit_bytes=LIMIT),
        name="propagate",
    )(walkers, chol, noise, sources)


def solve_each(factor, target):
    return jax.scipy.linalg.cho_solve((factor, True), target)


def by_cholesky(walkers, chol_vectors, noise, sources):
    walk_count, row_count, occ_count = walkers.shape
    vec_count, _, orb_count = chol_vectors.shape
    first_row = lax.axis_index("chol") * row_count
    flat_chol = chol_vectors.reshape(vec_count, row_count * orb_count)
    current = walkers
    biases = []
    for step_index in range(STEPS):
        gathered = lax.all_gather(current, "chol", axis=1, tiled=True)
        phi = gathered.astype(F32)
        top_plain = gathered[:, :occ_count, :]
        gram = jnp.einsum("wai,waj->wij", top_plain, top_plain, preferred_element_type=F32)
        factor = jnp.linalg.cholesky(gram)
        inverse = jax.vmap(solve_each)(factor, jnp.swapaxes(phi[:, :occ_count, :], 1, 2))
        inverse_wide = jnp.pad(inverse, ((0, 0), (0, 0), (0, orb_count - occ_count)))
        inverse_cols = lax.dynamic_slice_in_dim(inverse_wide, first_row, row_count, 2)
        theta_slab = jnp.einsum("wja,wai->wji", phi, inverse_cols, precision=lax.Precision.HIGHEST).astype(BF16)
        green = jnp.swapaxes(theta_slab, 1, 2).reshape(walk_count, row_count * orb_count)
        partial_bias = lax.dot_general(green, flat_chol, (((1,), (1,)), ((), ())), preferred_element_type=F32)
        bias_now = SQRT_DT * lax.psum(partial_bias, "chol")
        biases.append(bias_now)
        field = (noise[step_index] - bias_now).astype(BF16)
        potential = SQRT_DT * jnp.dot(field, flat_chol, preferred_element_type=F32)
        potential = potential.reshape(walk_count, row_count, orb_count).astype(BF16)
        total = current.astype(F32)
        term = current
        for order in range(1, ORDER + 1):
            whole = gathered if order == 1 else lax.all_gather(term, "chol", axis=1, tiled=True)
            product = jnp.einsum("wij,wjb->wib", potential, whole, preferred_element_type=F32)
            term = (-product / order).astype(BF16)
            total = total + term.astype(F32)
        current = total.astype(BF16)
    everyone = lax.all_gather(current, "pop", axis=0, tiled=True)
    return everyone[sources], jnp.stack(biases)


def local(walkers, chol_vectors, noise, sources):
    vec_count = chol_vectors.shape[0]
    share = vec_count // lax.axis_size("chol")
    branched, bias, missed = propagate(
        jnp.transpose(walkers, (1, 0, 2)), jnp.transpose(chol_vectors, (1, 0, 2)), noise, sources
    )

    def by_share():
        branched, bias = by_cholesky(walkers, chol_vectors, noise, sources)
        return branched, lax.dynamic_slice_in_dim(bias, lax.axis_index("chol") * share, share, 2)

    return lax.cond(missed[0, 0] == 0.0, lambda: (jnp.transpose(branched, (1, 0, 2)), bias), by_share)


def solution(mesh):
    return jax.shard_map(
        local,
        mesh=mesh,
        in_specs=(P("pop", "chol", None), P(None, "chol", None), P(None, "pop", None), P("pop")),
        out_specs=(P("pop", "chol", None), P(None, "pop", "chol")),
        check_vma=False,
    )
```

```python
import jax
import jax.numpy as jnp
from jax import lax
from jax.experimental import pallas as pl
from jax.experimental.pallas import tpu as pltpu
from jax.sharding import PartitionSpec as P

STEPS = 2
ORDER = 4
SQRT_DT = 0.1
MESH = pl.DeviceIdType.MESH
F32 = jnp.float32
BF16 = jnp.bfloat16
VMEM = pltpu.VMEM
ROWS = 10
PAD = 16
SIDE = 4
HALF = 256
LANES = 128
VIRT = 128
WINDOW = 256
FLAGS = 384
FLAG = 15
NEWTON = ((0.05, 5), (0.001, 7))
REFINE = 2
MISS = 1e-3
LIMIT = 60 * 1024 * 1024


def dot(a, b):
    return lax.dot_general(a, b, (((1,), (0,)), ((), ())), preferred_element_type=F32)


def dot_nt(a, b):
    return lax.dot_general(a, b, (((1,), (1,)), ((), ())), preferred_element_type=F32)


def split(a):
    head = a.astype(BF16)
    return head, (a - head.astype(F32)).astype(BF16)


def index(shape, axis):
    return lax.broadcasted_iota(jnp.int32, shape, axis)


def one_hot(mask):
    return jnp.where(mask, 1.0, 0.0).astype(BF16)


def chol_id(y, z, x):
    return {"chol": y * 16 + z * 4 + x}


def others(at):
    return [lax.rem(at + k, SIDE) for k in (2, 1, 3)]


def remote(src, dst, send, recv, peer):
    return pltpu.make_async_remote_copy(
        src_ref=src, dst_ref=dst, send_sem=send, recv_sem=recv, device_id=peer, device_id_type=MESH
    )


def start(copies):
    for copy in copies:
        copy.start()


def received(copies):
    for copy in copies:
        copy.wait_recv()


def sent(copies):
    for copy in copies:
        copy.wait_send()


def inverse_of(top, tuned, products):
    occ = top.shape[0]
    gram = dot_nt(top, top)
    scale = 0.999 / jnp.max(jnp.sum(jnp.abs(gram), axis=1, keepdims=True), axis=0, keepdims=True)
    inv, square = top.astype(F32) * scale, gram * scale
    least = tuned
    for turn in range(products):
        c = 2.0 / (1.0 + least)
        least = 1.0 - ((1.0 - least) / (1.0 + least)) ** 2
        near = inv.astype(BF16)
        if turn > 0:
            square = dot_nt(near, top)
        inv = (2.0 * c) * inv - (c * c) * dot(square.astype(BF16), near)
    eye = jnp.where(index((occ, occ), 0) == index((occ, occ), 1), 1.0, 0.0)
    for _ in range(REFINE):
        head, rest = split(inv)
        miss = eye - (dot_nt(rest, top) + dot_nt(head, top))
        inv = inv + dot(miss.astype(BF16), head)
    return inv, jnp.sum(jnp.sum(miss * miss, axis=1, keepdims=True), axis=0, keepdims=True)


def theta_rows(inv, phi_t, x):
    occ, orb = phi_t.shape
    shape = (SIDE * PAD, occ)
    row, col = index(shape, 0), index(shape, 1)
    sel = one_hot((col == (row // PAD * SIDE + x) * ROWS + row % PAD) & (row % PAD < ROWS))
    head, rest = [dot(sel, part).astype(BF16) for part in split(inv)]
    theta = dot(rest, phi_t[:, VIRT:]) + dot(head, phi_t[:, VIRT:])
    theta = jnp.where(index(theta.shape, 1) >= occ - VIRT, theta, 0.0)
    return theta.astype(BF16).reshape(SIDE, PAD, orb - VIRT)


def eight(block, part):
    y, z = part // 2, 2 * (part % 2)
    return jnp.concatenate([block(y, z + k // SIDE, k % SIDE) for k in range(8)], axis=0)


def pick_rows():
    shape = (8 * ROWS, 8 * PAD)
    row, col = index(shape, 0), index(shape, 1)
    return row % ROWS, col % PAD, row // ROWS == col // PAD


def compact(block, out, these):
    row, col, same = pick_rows()
    pick = one_hot(same & (row == col))
    for part in these:
        out[8 * ROWS * part : 8 * ROWS * (part + 1), :] = dot(pick, eight(block, part)).astype(BF16)


def compact_packed(block, out, c):
    row, col, same = pick_rows()
    pick = one_hot(same & (row == col))
    rest = [one_hot(same & (col == ROWS + row // 4) & (row % 4 == 2 * c + e)) for e in range(2)]
    for part in range(8):
        piece = eight(block, part)
        rows = pl.ds(8 * ROWS * part, 8 * ROWS)
        out[rows, HALF * c : HALF * (c + 1)] = dot(pick, piece).astype(BF16)
        tail = sum(dot(rest[e], piece[:, LANES * e : LANES * (e + 1)]) for e in range(2))
        if c > 0:
            tail = tail + out[rows, 2 * HALF :].astype(F32)
        out[rows, 2 * HALF :] = tail.astype(BF16)


def diagonal(chol, slab):
    rows = chol.shape[0]
    shape = (PAD, WINDOW)
    row, col = index(shape, 0), index(shape, 1)
    acc = sum(dot_nt(one_hot((row == r) & (col == slab * ROWS + r)), chol[r, :, :WINDOW]) for r in range(rows))
    return jnp.sum(acc, axis=0, keepdims=True)


def bias_rows(green, chol):
    rows, vecs, _ = chol.shape
    row = index(green.shape, 0) % PAD
    acc = sum(dot_nt(jnp.where(row == r, green, jnp.zeros_like(green)), chol[r, :, VIRT:]) for r in range(rows))
    return jnp.sum(acc.reshape(SIDE, PAD, vecs), axis=1)


def potential_chunk(field, chol, c):
    rows, vecs, _ = chol.shape
    field = jnp.broadcast_to(field[:, None, :], (SIDE, PAD, vecs)).reshape(SIDE * PAD, vecs).astype(BF16)
    row = index(field.shape, 0) % PAD
    none = jnp.zeros_like(field)
    lanes = slice(HALF * c, HALF * (c + 1))
    main = sum(dot(jnp.where(row == r, field, none), chol[r, :, lanes]) for r in range(rows))
    tails = [
        sum(dot(jnp.where(row == ROWS + r // 4, field, none), chol[r, :, 2 * HALF :]) for r in range(2 * c + e, rows, 4))
        for e in range(2)
    ]
    whole = SQRT_DT * (main + jnp.concatenate(tails, axis=1))
    return whole.astype(BF16).reshape(SIDE, PAD, HALF)


def pack_picks(picks, y, x):
    shape = picks.shape[1:]
    row, col = index(shape, 0), index(shape, 1)
    base, r = (y * 16 + row // PAD * SIDE + x) * ROWS - LANES * y, row % PAD
    picks[0] = one_hot((col == base + r) & (r < ROWS))
    for s in range(4):
        at = 4 * (r - ROWS) + s
        picks[1 + s] = one_hot((col == base + at) & (at >= 0) & (at < ROWS))


def pack_walker(phi_t, picks, blocks, y, missed):
    occ, _ = phi_t.shape
    rest = occ - LANES
    window = pl.ds(pl.multiple_of(LANES * y, LANES), WINDOW)
    whole = dot_nt(picks[0], phi_t[:LANES, window])
    copies = jnp.concatenate([phi_t[LANES:, window]] * 4, axis=0)
    lane = index((SIDE * PAD, LANES), 1) // rest
    for s in range(4):
        whole = whole + jnp.where(lane == s, dot_nt(picks[1 + s], copies), 0.0)
    whole = jnp.where(index(whole.shape, 0) % PAD == FLAG, missed, whole)
    blocks[...] = whole.astype(BF16).reshape(SIDE, PAD, LANES)


def kernel(
    walkers, chol_hbm, noise, sources, out, bias, missed_out,
    chol, padded, first_grid, phi, phi_t, theta, slab_theta, trace, parts, sums, blocks, grid, pot, picks, packed, everyone,
    send0, recv0, recv_z0, send, recv, recv_z, bias_send, bias_recv, last_send, last_recv, chol_sem, ready,
):
    d, pop = lax.axis_index("chol"), lax.axis_index("pop")
    y, z, x = d // 16, (d // 4) % 4, d % 4
    hi, core = pop // 2, pop % 2
    load = pltpu.make_async_copy(chol_hbm, chol, chol_sem)
    load.start()

    ys, xs = others(y), others(x)
    zs = [3 * (1 - z // 2), lax.rem(2 + 3 * z, 5)]
    zs.append(6 - z - zs[0] - zs[1])
    ring = []
    for k in sorted(range(1, 16), key=lambda k: abs(k - 8)):
        place = lax.rem(hi * 4 + z + k, 16)
        ring.append((place // 4, place % 4))
    twin = {"pop": hi * 2 + 1 - core}
    ring_peers = [{"chol": y * 16 + b * 4 + x, "pop": h * 2 + core} for h, b in ring]
    z_peers = [chol_id(y, b, x) for b in zs]
    y_peers = [chol_id(b, z, x) for b in ys]
    x_peers = [chol_id(y, z, b) for b in xs]
    barrier = pltpu.get_barrier_semaphore()

    def greet(peers):
        for peer in peers:
            pl.semaphore_signal(barrier, inc=1, device_id=peer, device_id_type=MESH)

    hi_peers = [{"pop": b * 2 + core} for b in others(hi)]
    lines = hi_peers + z_peers + x_peers + y_peers + [twin]
    greet(lines)
    padded[...] = jnp.zeros_like(padded)
    padded[:, :ROWS, :] = jnp.swapaxes(walkers[...].astype(F32), 0, 1).astype(BF16)

    pl.semaphore_wait(barrier, len(lines))

    def pushes(ref, peers, sems, base):
        return [remote(ref, ref, sems[0].at[base + k], sems[1].at[base + k], p) for k, p in enumerate(peers)]

    def z_arrives(slot, sems):
        for b in zs:
            pltpu.make_async_copy(slot(b), slot(b), sems.at[b]).wait()

    sems0 = send0, recv0
    def first_slot(b):
        upper = b // 2
        return first_grid.at[upper, x + upper * (y - x), y + upper * (x - y), b % 2]

    spot = first_slot(z)
    first = [
        remote(padded.at[w], spot, send0.at[k], recv_z0.at[z], peer)
        for k, (w, peer) in enumerate(zip(zs, z_peers, strict=True))
    ]
    start(first)
    spot[...] = padded[z]
    z_arrives(first_slot, recv_z0)
    along_y = pushes(first_grid.at[0, x, y], y_peers, sems0, 3)
    along_x = pushes(first_grid.at[1, y, x], x_peers, sems0, 6)
    then_y = pushes(first_grid.at[1, y], y_peers, sems0, 9)
    start(along_y + along_x)
    for peer in hi_peers:
        pl.semaphore_signal(ready, inc=1, device_id=peer, device_id_type=MESH)

    def first_block(b, c, e):
        return first_grid[0, e, b, c] if c < 2 else first_grid[1, b, e, c - 2]

    @pl.when(y != 0)
    def _():
        then_x = pushes(first_grid.at[0, x], x_peers, sems0, 12)
        received(along_y)
        start(then_x)
        received(along_x)
        start(then_y)
        sent(first + along_y + along_x)
        received(then_x + then_y)
        compact(first_block, phi, range(8))
        phi_t[...] = phi[...].astype(F32).T.astype(BF16)
        sent(then_x + then_y)

    drain = []
    for s in range(STEPS):
        to_slab = [
            remote(theta.at[s, b], slab_theta.at[s, z], send.at[s, k], recv_z.at[s, 0, z], peer)
            for k, (b, peer) in enumerate(zip(zs, z_peers, strict=True))
        ]
        spots = [(k // SIDE, lax.rem(z + k % SIDE, SIDE)) for k in (10, 9, 11, 8, 6, 14, 5, 7, 13, 15, 4, 12, 2, 1, 3)]
        to_sums = [
            remote(parts.at[s, z], parts.at[s, z], bias_send.at[s, k], bias_recv.at[s, z], chol_id(b, c, x))
            for k, (b, c) in enumerate(spots)
        ]
        to_x = [
            remote(sums.at[s, x], sums.at[s, x], bias_send.at[s, 15 + k], bias_recv.at[s, 4 + k], peer)
            for k, peer in enumerate(x_peers)
        ]

        def part_arrives(which, s=s):
            pltpu.make_async_copy(parts.at[s, which], parts.at[s, which], bias_recv.at[s, which]).wait()

        @pl.when(y == 0)
        def _(s=s, drain=drain, led=led if s else []):
            if s == 0:
                early = pushes(first_grid.at[0, x, 0], x_peers, sems0, 15)
                then_x = pushes(first_grid.at[0, x, pl.ds(1, 3)], x_peers, sems0, 12)
                start(early)
                received(along_y)
                start(then_x)
                received(along_x)
                start(then_y)
                load.wait()
                trace[...] = diagonal(chol, z * SIDE + x)
                received(early)
                compact(first_block, phi, range(2))
                inv, size = inverse_of(phi[: phi.shape[1], :], *NEWTON[s])
                received(then_x + then_y)
                compact(first_block, phi, range(2, 8))
                phi_t[...] = phi[...].astype(F32).T.astype(BF16)
            else:
                top = phi_t[:, : phi_t.shape[0]].astype(F32).T.astype(BF16)
                inv, size = inverse_of(top, *NEWTON[s])
            theta[s] = theta_rows(inv, phi_t, x)
            start(to_slab)
            slab_theta[s, z] = theta[s, z]
            if s == 0:
                sent(first + along_y + along_x + early + then_x + then_y)
                pack_picks(picks, y, x)
            sent(drain + led)
            missed = jnp.where(size < MISS, 0.0, 1.0)
            mine = parts.at[s, z]
            mine[...] = jnp.zeros(mine.shape, F32)
            flags = index((SIDE, LANES), 0) == z
            mine[:, FLAGS:] = jnp.where(flags, missed, 0.0)
            z_arrives(lambda b: slab_theta.at[s, b], recv_z.at[s, 0])
            mine[:, : chol.shape[1]] = trace[...] + bias_rows(slab_theta[s].reshape(SIDE * PAD, chol.shape[2] - VIRT), chol)
            start(to_sums)
            for which in zs:
                part_arrives(which)

        @pl.when(y != 0)
        def _(s=s, drain=drain):
            sent(drain)
            if s == 0:
                load.wait()
                pack_picks(picks, y, x)
            for which in range(SIDE):
                part_arrives(which)

        sums[s, x] = sum(parts[s, which] for which in range(SIDE))
        start(to_x)
        received(to_x)
        total = sum(sums[s, which] for which in range(SIDE))
        flag = jnp.sum(jnp.where(index((SIDE, LANES), 0) == z, total[:, FLAGS:], 0.0), axis=0, keepdims=True)[:, :1]
        missed = flag if s == 0 else missed + flag
        total = SQRT_DT * total[:, : chol.shape[1]]
        field = (noise[s] - total).astype(BF16).astype(F32)

        sems = send.at[s, pl.ds(3, 18)], recv.at[s, pl.ds(3, 18)]
        firsts, alongs, thens = [], [], []
        for c, (u, v) in enumerate([(x, y), (y, x)]):
            blocks[s, c] = potential_chunk(field, chol, c)
            spot = grid.at[s, c, u, v, z]
            firsts.append([
                remote(blocks.at[s, c, w], spot, sems[0].at[9 * c + k], recv_z.at[s, 1 + c, z], peer)
                for k, (w, peer) in enumerate(zip(zs, z_peers, strict=True))
            ])
            start(firsts[c])
            spot[...] = blocks[s, c, z]
        for c, (u, v, peers) in enumerate([(x, y, y_peers), (y, x, x_peers)]):
            z_arrives(lambda b, c=c, u=u, v=v: grid.at[s, c, u, v, b], recv_z.at[s, 1 + c])
            alongs.append(pushes(grid.at[s, c, u, v], peers, sems, 9 * c + 3))
            start(alongs[c])
        for c, (u, peers) in enumerate([(x, x_peers), (y, y_peers)]):
            received(alongs[c])
            thens.append(pushes(grid.at[s, c, u], peers, sems, 9 * c + 6))
            start(thens[c])
        share = one_hot(index((chol.shape[1], 8), 0) == d * bias.shape[2] + index((chol.shape[1], 8), 1)).astype(F32)
        bias[s] = jnp.dot(total, share, precision=lax.Precision.HIGHEST, preferred_element_type=F32)[:, : bias.shape[2]]
        received(thens[0])
        compact_packed(lambda b, c, e, s=s: grid[s, 0, e, b, c], pot, 0)
        received(thens[1])
        compact_packed(lambda b, c, e, s=s: grid[s, 1, b, e, c], pot, 1)

        term = phi_t[...]
        sum_of = term.astype(F32)
        for order in range(1, ORDER + 1):
            term = (-dot_nt(term, pot[...]) / order).astype(BF16)
            sum_of = sum_of + term.astype(F32)
        phi_t[...] = sum_of.astype(BF16)
        drain = sum(firsts + alongs + thens, to_x)
        led = to_slab + to_sums

    pl.semaphore_wait(ready, len(hi_peers))
    pack_walker(phi_t, picks, packed, y, missed)
    spot = everyone.at[hi, core, z]
    to_ring = [
        remote(packed.at[b], spot, last_send.at[k], last_recv.at[k], peer)
        for k, ((_, b), peer) in enumerate(zip(ring, ring_peers, strict=True))
    ]
    start(to_ring)
    everyone[hi, core, z] = packed[z]
    sent(drain)

    @pl.when(y == 0)
    def _():
        sent(led)

    received(to_ring)
    mine = everyone.at[:, core]
    to_twin = [remote(mine, mine, last_send.at[15], last_recv.at[15], twin)]
    start(to_twin)
    sent(to_ring)
    received(to_twin)

    chosen = []
    for slot in range(SIDE):
        source = sources[slot]
        chosen.append(everyone[source // 8, source // 4 % 2, source % 4])
    whole = jnp.concatenate(chosen, axis=0)
    rest = out.shape[2] - LANES
    shape = (SIDE * PAD, SIDE * PAD)
    row, col = index(shape, 0), index(shape, 1)
    r = row % PAD
    back = one_hot(index((LANES, rest), 0) % rest == index((LANES, rest), 1))
    lane = index((SIDE * PAD, LANES), 1) // rest
    tail = jnp.zeros((SIDE * PAD, LANES), F32)
    for s in range(4):
        pick = one_hot((row // PAD == col // PAD) & (col % PAD == ROWS + r // 4) & (r % 4 == s) & (r < ROWS))
        tail = tail + jnp.where(lane == s, dot(pick, whole), 0.0)
    tail = dot(tail.astype(BF16), back)
    whole = jnp.concatenate([whole.astype(F32), tail], axis=1).reshape(SIDE, PAD, LANES + rest)
    out[...] = jnp.swapaxes(whole[:, :ROWS, :], 0, 1).astype(BF16)
    flags = everyone[...].reshape(8 * SIDE, PAD, LANES).astype(F32)
    bad = jnp.where((index(flags.shape, 1) == FLAG) & jnp.logical_not(flags == 0.0), 1.0, 0.0)
    missed_out[...] = jnp.max(jnp.max(bad, axis=0), axis=0, keepdims=True)
    sent(to_twin)


def propagate(walkers, chol, noise, sources):
    rows, vecs, orb = chol.shape
    occ = walkers.shape[2]
    dma = pltpu.SemaphoreType.DMA
    vmem = pl.BlockSpec(memory_space=VMEM)
    return pl.pallas_call(
        kernel,
        out_shape=(
            jax.ShapeDtypeStruct((rows, SIDE, occ), BF16),
            jax.ShapeDtypeStruct((STEPS, SIDE, vecs // SIDE**3), F32),
            jax.ShapeDtypeStruct((1, LANES), F32),
        ),
        in_specs=[vmem, pl.BlockSpec(memory_space=pl.ANY), vmem, pl.BlockSpec(memory_space=pltpu.SMEM)],
        out_specs=(vmem, vmem, vmem),
        scratch_shapes=[
            VMEM((rows, vecs, orb), BF16),
            VMEM((SIDE, PAD, occ), BF16),
            VMEM((2, SIDE, SIDE, 2, PAD, occ), BF16),
            VMEM((orb, occ), BF16),
            VMEM((occ, orb), BF16),
            VMEM((STEPS, SIDE, PAD, orb - VIRT), BF16),
            VMEM((STEPS, SIDE, PAD, orb - VIRT), BF16),
            VMEM((1, vecs), F32),
            VMEM((STEPS, SIDE, SIDE, FLAGS + LANES), F32),
            VMEM((STEPS, SIDE, SIDE, FLAGS + LANES), F32),
            VMEM((STEPS, 2, SIDE, PAD, HALF), BF16),
            VMEM((STEPS, 2, SIDE, SIDE, SIDE, PAD, HALF), BF16),
            VMEM((orb, orb), BF16),
            VMEM((5, SIDE * PAD, WINDOW), BF16),
            VMEM((SIDE, PAD, LANES), BF16),
            VMEM((SIDE, 2, SIDE, PAD, LANES), BF16),
            dma((18,)),
            dma((18,)),
            dma((SIDE,)),
            dma((STEPS, 21)),
            dma((STEPS, 21)),
            dma((STEPS, 3, SIDE)),
            dma((STEPS, 18)),
            dma((STEPS, 7)),
            dma((16,)),
            dma((16,)),
            dma,
            pltpu.SemaphoreType.REGULAR,
        ],
        compiler_params=pltpu.CompilerParams(collective_id=0, has_side_effects=True, vmem_limit_bytes=LIMIT),
        name="propagate",
    )(walkers, chol, noise, sources)


def solve_each(factor, target):
    return jax.scipy.linalg.cho_solve((factor, True), target)


def by_cholesky(walkers, chol_vectors, noise, sources):
    walk_count, row_count, occ_count = walkers.shape
    vec_count, _, orb_count = chol_vectors.shape
    first_row = lax.axis_index("chol") * row_count
    flat_chol = chol_vectors.reshape(vec_count, row_count * orb_count)
    current = walkers
    biases = []
    for step_index in range(STEPS):
        gathered = lax.all_gather(current, "chol", axis=1, tiled=True)
        phi = gathered.astype(F32)
        top_plain = gathered[:, :occ_count, :]
        gram = jnp.einsum("wai,waj->wij", top_plain, top_plain, preferred_element_type=F32)
        factor = jnp.linalg.cholesky(gram)
        inverse = jax.vmap(solve_each)(factor, jnp.swapaxes(phi[:, :occ_count, :], 1, 2))
        inverse_wide = jnp.pad(inverse, ((0, 0), (0, 0), (0, orb_count - occ_count)))
        inverse_cols = lax.dynamic_slice_in_dim(inverse_wide, first_row, row_count, 2)
        theta_slab = jnp.einsum("wja,wai->wji", phi, inverse_cols, precision=lax.Precision.HIGHEST).astype(BF16)
        green = jnp.swapaxes(theta_slab, 1, 2).reshape(walk_count, row_count * orb_count)
        partial_bias = lax.dot_general(green, flat_chol, (((1,), (1,)), ((), ())), preferred_element_type=F32)
        bias_now = SQRT_DT * lax.psum(partial_bias, "chol")
        biases.append(bias_now)
        field = (noise[step_index] - bias_now).astype(BF16)
        potential = SQRT_DT * jnp.dot(field, flat_chol, preferred_element_type=F32)
        potential = potential.reshape(walk_count, row_count, orb_count).astype(BF16)
        total = current.astype(F32)
        term = current
        for order in range(1, ORDER + 1):
            whole = gathered if order == 1 else lax.all_gather(term, "chol", axis=1, tiled=True)
            product = jnp.einsum("wij,wjb->wib", potential, whole, preferred_element_type=F32)
            term = (-product / order).astype(BF16)
            total = total + term.astype(F32)
        current = total.astype(BF16)
    everyone = lax.all_gather(current, "pop", axis=0, tiled=True)
    return everyone[sources], jnp.stack(biases)


def local(walkers, chol_vectors, noise, sources):
    vec_count = chol_vectors.shape[0]
    share = vec_count // lax.axis_size("chol")
    branched, bias, missed = propagate(
        jnp.transpose(walkers, (1, 0, 2)), jnp.transpose(chol_vectors, (1, 0, 2)), noise, sources
    )

    def by_share():
        branched, bias = by_cholesky(walkers, chol_vectors, noise, sources)
        return branched, lax.dynamic_slice_in_dim(bias, lax.axis_index("chol") * share, share, 2)

    return lax.cond(missed[0, 0] == 0.0, lambda: (jnp.transpose(branched, (1, 0, 2)), bias), by_share)


def solution(mesh):
    return jax.shard_map(
        local,
        mesh=mesh,
        in_specs=(P("pop", "chol", None), P(None, "chol", None), P(None, "pop", None), P("pop")),
        out_specs=(P("pop", "chol", None), P(None, "pop", "chol")),
        check_vma=False,
    )
```

```python
import jax
import jax.numpy as jnp
from jax import lax
from jax.experimental import pallas as pl
from jax.experimental.pallas import tpu as pltpu
from jax.sharding import PartitionSpec as P

STEPS = 2
ORDER = 4
SQRT_DT = 0.1
MESH = pl.DeviceIdType.MESH
F32 = jnp.float32
BF16 = jnp.bfloat16
VMEM = pltpu.VMEM
ROWS = 10
PAD = 16
SIDE = 4
HALF = 256
LANES = 128
VIRT = 128
WINDOW = 256
FLAGS = 384
FLAG = 15
NEWTON = ((0.05, 5), (0.001, 7))
CARRIED = 3
REFINE = 2
MISS = 1e-3
LIMIT = 60 * 1024 * 1024


def dot(a, b):
    return lax.dot_general(a, b, (((1,), (0,)), ((), ())), preferred_element_type=F32)


def dot_nt(a, b):
    return lax.dot_general(a, b, (((1,), (1,)), ((), ())), preferred_element_type=F32)


def split(a):
    head = a.astype(BF16)
    return head, (a - head.astype(F32)).astype(BF16)


def index(shape, axis):
    return lax.broadcasted_iota(jnp.int32, shape, axis)


def one_hot(mask):
    return jnp.where(mask, 1.0, 0.0).astype(BF16)


def chol_id(y, z, x):
    return {"chol": y * 16 + z * 4 + x}


def others(at):
    return [lax.rem(at + k, SIDE) for k in (2, 1, 3)]


def remote(src, dst, send, recv, peer):
    return pltpu.make_async_remote_copy(
        src_ref=src, dst_ref=dst, send_sem=send, recv_sem=recv, device_id=peer, device_id_type=MESH
    )


def start(copies):
    for copy in copies:
        copy.start()


def received(copies):
    for copy in copies:
        copy.wait_recv()


def sent(copies):
    for copy in copies:
        copy.wait_send()


def inverse_of(top, tuned, products):
    occ = top.shape[0]
    gram = dot_nt(top, top)
    scale = 0.999 / jnp.max(jnp.sum(jnp.abs(gram), axis=1, keepdims=True), axis=0, keepdims=True)
    inv, square = top.astype(F32) * scale, gram * scale
    least = tuned
    for turn in range(products):
        c = 2.0 / (1.0 + least)
        least = 1.0 - ((1.0 - least) / (1.0 + least)) ** 2
        near = inv.astype(BF16)
        if turn > CARRIED:
            square = dot_nt(near, top)
        held = square.astype(BF16)
        inv = (2.0 * c) * inv - (c * c) * dot(held, near)
        if turn < CARRIED:
            square = (2.0 * c) * square - (c * c) * dot(held, held)
    eye = jnp.where(index((occ, occ), 0) == index((occ, occ), 1), 1.0, 0.0)
    for _ in range(REFINE):
        head, rest = split(inv)
        miss = eye - (dot_nt(rest, top) + dot_nt(head, top))
        inv = inv + dot(miss.astype(BF16), head)
    return inv, jnp.sum(jnp.sum(miss * miss, axis=1, keepdims=True), axis=0, keepdims=True)


def theta_rows(inv, phi_t, x):
    occ, orb = phi_t.shape
    shape = (SIDE * PAD, occ)
    row, col = index(shape, 0), index(shape, 1)
    sel = one_hot((col == (row // PAD * SIDE + x) * ROWS + row % PAD) & (row % PAD < ROWS))
    head, rest = [dot(sel, part).astype(BF16) for part in split(inv)]
    theta = dot(rest, phi_t[:, VIRT:]) + dot(head, phi_t[:, VIRT:])
    theta = jnp.where(index(theta.shape, 1) >= occ - VIRT, theta, 0.0)
    return theta.astype(BF16).reshape(SIDE, PAD, orb - VIRT)


def eight(block, part):
    y, z = part // 2, 2 * (part % 2)
    return jnp.concatenate([block(y, z + k // SIDE, k % SIDE) for k in range(8)], axis=0)


def pick_rows():
    shape = (8 * ROWS, 8 * PAD)
    row, col = index(shape, 0), index(shape, 1)
    return row % ROWS, col % PAD, row // ROWS == col // PAD


def compact(block, out, these):
    row, col, same = pick_rows()
    pick = one_hot(same & (row == col))
    for part in these:
        out[8 * ROWS * part : 8 * ROWS * (part + 1), :] = dot(pick, eight(block, part)).astype(BF16)


def compact_packed(block, out, c):
    row, col, same = pick_rows()
    pick = one_hot(same & (row == col))
    rest = [one_hot(same & (col == ROWS + row // 4) & (row % 4 == 2 * c + e)) for e in range(2)]
    for part in range(8):
        piece = eight(block, part)
        rows = pl.ds(8 * ROWS * part, 8 * ROWS)
        out[rows, HALF * c : HALF * (c + 1)] = dot(pick, piece).astype(BF16)
        tail = sum(dot(rest[e], piece[:, LANES * e : LANES * (e + 1)]) for e in range(2))
        if c > 0:
            tail = tail + out[rows, 2 * HALF :].astype(F32)
        out[rows, 2 * HALF :] = tail.astype(BF16)


def diagonal(chol, slab):
    rows = chol.shape[0]
    shape = (PAD, WINDOW)
    row, col = index(shape, 0), index(shape, 1)
    acc = sum(dot_nt(one_hot((row == r) & (col == slab * ROWS + r)), chol[r, :, :WINDOW]) for r in range(rows))
    return jnp.sum(acc, axis=0, keepdims=True)


def bias_rows(green, chol):
    rows, vecs, _ = chol.shape
    row = index(green.shape, 0) % PAD
    acc = sum(dot_nt(jnp.where(row == r, green, jnp.zeros_like(green)), chol[r, :, VIRT:]) for r in range(rows))
    return jnp.sum(acc.reshape(SIDE, PAD, vecs), axis=1)


def potential_chunk(field, chol, c):
    rows, vecs, _ = chol.shape
    field = jnp.broadcast_to(field[:, None, :], (SIDE, PAD, vecs)).reshape(SIDE * PAD, vecs).astype(BF16)
    row = index(field.shape, 0) % PAD
    none = jnp.zeros_like(field)
    lanes = slice(HALF * c, HALF * (c + 1))
    main = sum(dot(jnp.where(row == r, field, none), chol[r, :, lanes]) for r in range(rows))
    tails = [
        sum(dot(jnp.where(row == ROWS + r // 4, field, none), chol[r, :, 2 * HALF :]) for r in range(2 * c + e, rows, 4))
        for e in range(2)
    ]
    whole = SQRT_DT * (main + jnp.concatenate(tails, axis=1))
    return whole.astype(BF16).reshape(SIDE, PAD, HALF)


def pack_picks(picks, y, x):
    shape = picks.shape[1:]
    row, col = index(shape, 0), index(shape, 1)
    base, r = (y * 16 + row // PAD * SIDE + x) * ROWS - LANES * y, row % PAD
    picks[0] = one_hot((col == base + r) & (r < ROWS))
    for s in range(4):
        at = 4 * (r - ROWS) + s
        picks[1 + s] = one_hot((col == base + at) & (at >= 0) & (at < ROWS))


def pack_walker(phi_w, picks, blocks, missed):
    rest = phi_w.shape[0] - LANES
    whole = dot_nt(picks[0], phi_w[:LANES, :])
    copies = jnp.concatenate([phi_w[LANES:, :]] * 4, axis=0)
    lane = index((SIDE * PAD, LANES), 1) // rest
    for s in range(4):
        whole = whole + jnp.where(lane == s, dot_nt(picks[1 + s], copies), 0.0)
    whole = jnp.where(index(whole.shape, 0) % PAD == FLAG, missed, whole)
    blocks[...] = whole.astype(BF16).reshape(SIDE, PAD, LANES)


def kernel(
    walkers, chol_hbm, noise, sources, out, bias, missed_out,
    chol, padded, first_grid, phi, phi_t, theta, slab_theta, trace, parts, sums, blocks, grid, pot, partial, picks, packed, everyone,
    send0, recv0, recv_z0, send, recv, recv_z, bias_send, bias_recv, last_send, last_recv, chol_sem, ready,
):
    d, pop = lax.axis_index("chol"), lax.axis_index("pop")
    y, z, x = d // 16, (d // 4) % 4, d % 4
    hi, core = pop // 2, pop % 2
    load = pltpu.make_async_copy(chol_hbm, chol, chol_sem)
    load.start()

    ys, xs = others(y), others(x)
    zs = [3 * (1 - z // 2), lax.rem(2 + 3 * z, 5)]
    zs.append(6 - z - zs[0] - zs[1])
    ring = []
    for k in sorted(range(1, 16), key=lambda k: abs(k - 8)):
        place = lax.rem(hi * 4 + z + k, 16)
        ring.append((place // 4, place % 4))
    twin = {"pop": hi * 2 + 1 - core}
    ring_peers = [{"chol": y * 16 + b * 4 + x, "pop": h * 2 + core} for h, b in ring]
    z_peers = [chol_id(y, b, x) for b in zs]
    y_peers = [chol_id(b, z, x) for b in ys]
    x_peers = [chol_id(y, z, b) for b in xs]
    barrier = pltpu.get_barrier_semaphore()

    def greet(peers):
        for peer in peers:
            pl.semaphore_signal(barrier, inc=1, device_id=peer, device_id_type=MESH)

    hi_peers = [{"pop": b * 2 + core} for b in others(hi)]
    lines = hi_peers + z_peers + x_peers + y_peers + [twin]
    greet(lines)
    padded[...] = jnp.zeros_like(padded)
    padded[:, :ROWS, :] = jnp.swapaxes(walkers[...].astype(F32), 0, 1).astype(BF16)

    pl.semaphore_wait(barrier, len(lines))

    def pushes(ref, peers, sems, base):
        return [remote(ref, ref, sems[0].at[base + k], sems[1].at[base + k], p) for k, p in enumerate(peers)]

    def z_arrives(slot, sems):
        for b in zs:
            pltpu.make_async_copy(slot(b), slot(b), sems.at[b]).wait()

    sems0 = send0, recv0
    def first_slot(b):
        upper = b // 2
        return first_grid.at[upper, x + upper * (y - x), y + upper * (x - y), b % 2]

    spot = first_slot(z)
    first = [
        remote(padded.at[w], spot, send0.at[k], recv_z0.at[z], peer)
        for k, (w, peer) in enumerate(zip(zs, z_peers, strict=True))
    ]
    start(first)
    spot[...] = padded[z]
    z_arrives(first_slot, recv_z0)
    along_y = pushes(first_grid.at[0, x, y], y_peers, sems0, 3)
    along_x = pushes(first_grid.at[1, y, x], x_peers, sems0, 6)
    then_y = pushes(first_grid.at[1, y], y_peers, sems0, 9)
    start(along_y + along_x)
    for peer in hi_peers:
        pl.semaphore_signal(ready, inc=1, device_id=peer, device_id_type=MESH)

    def first_block(b, c, e):
        return first_grid[0, e, b, c] if c < 2 else first_grid[1, b, e, c - 2]

    @pl.when(y != 0)
    def _():
        then_x = pushes(first_grid.at[0, x], x_peers, sems0, 12)
        received(along_y)
        start(then_x)
        received(along_x)
        start(then_y)
        sent(first + along_y + along_x)
        received(then_x + then_y)
        compact(first_block, phi, range(8))
        phi_t[...] = phi[...].astype(F32).T.astype(BF16)
        sent(then_x + then_y)

    drain = []
    for s in range(STEPS):
        to_slab = [
            remote(theta.at[s, b], slab_theta.at[s, z], send.at[s, k], recv_z.at[s, 0, z], peer)
            for k, (b, peer) in enumerate(zip(zs, z_peers, strict=True))
        ]
        spots = [(k // SIDE, lax.rem(z + k % SIDE, SIDE)) for k in (10, 9, 11, 8, 6, 14, 5, 7, 13, 15, 4, 12, 2, 1, 3)]
        to_sums = [
            remote(parts.at[s, z], parts.at[s, z], bias_send.at[s, k], bias_recv.at[s, z], chol_id(b, c, x))
            for k, (b, c) in enumerate(spots)
        ]
        to_x = [
            remote(sums.at[s, x], sums.at[s, x], bias_send.at[s, 15 + k], bias_recv.at[s, 4 + k], peer)
            for k, peer in enumerate(x_peers)
        ]

        def part_arrives(which, s=s):
            pltpu.make_async_copy(parts.at[s, which], parts.at[s, which], bias_recv.at[s, which]).wait()

        @pl.when(y == 0)
        def _(s=s, drain=drain, led=led if s else []):
            if s == 0:
                early = pushes(first_grid.at[0, x, 0], x_peers, sems0, 15)
                then_x = pushes(first_grid.at[0, x, pl.ds(1, 3)], x_peers, sems0, 12)
                start(early)
                received(along_y)
                start(then_x)
                received(along_x)
                start(then_y)
                load.wait()
                trace[...] = diagonal(chol, z * SIDE + x)
                received(early)
                compact(first_block, phi, range(2))
                inv, size = inverse_of(phi[: phi.shape[1], :], *NEWTON[s])
                received(then_x + then_y)
                compact(first_block, phi, range(2, 8))
                phi_t[...] = phi[...].astype(F32).T.astype(BF16)
            else:
                top = phi_t[:, : phi_t.shape[0]].astype(F32).T.astype(BF16)
                inv, size = inverse_of(top, *NEWTON[s])
            theta[s] = theta_rows(inv, phi_t, x)
            start(to_slab)
            slab_theta[s, z] = theta[s, z]
            if s == 0:
                sent(first + along_y + along_x + early + then_x + then_y)
                pack_picks(picks, y, x)
            sent(drain + led)
            missed = jnp.where(size < MISS, 0.0, 1.0)
            mine = parts.at[s, z]
            mine[...] = jnp.zeros(mine.shape, F32)
            flags = index((SIDE, LANES), 0) == z
            mine[:, FLAGS:] = jnp.where(flags, missed, 0.0)
            z_arrives(lambda b: slab_theta.at[s, b], recv_z.at[s, 0])
            mine[:, : chol.shape[1]] = trace[...] + bias_rows(slab_theta[s].reshape(SIDE * PAD, chol.shape[2] - VIRT), chol)
            start(to_sums)
            for which in zs:
                part_arrives(which)

        @pl.when(y != 0)
        def _(s=s, drain=drain):
            sent(drain)
            if s == 0:
                load.wait()
                pack_picks(picks, y, x)
            for which in range(SIDE):
                part_arrives(which)

        sums[s, x] = sum(parts[s, which] for which in range(SIDE))
        start(to_x)
        received(to_x)
        total = sum(sums[s, which] for which in range(SIDE))
        flag = jnp.sum(jnp.where(index((SIDE, LANES), 0) == z, total[:, FLAGS:], 0.0), axis=0, keepdims=True)[:, :1]
        missed = flag if s == 0 else missed + flag
        total = SQRT_DT * total[:, : chol.shape[1]]
        field = (noise[s] - total).astype(BF16).astype(F32)

        sems = send.at[s, pl.ds(3, 18)], recv.at[s, pl.ds(3, 18)]
        firsts, alongs, thens = [], [], []
        for c, (u, v) in enumerate([(x, y), (y, x)]):
            blocks[s, c] = potential_chunk(field, chol, c)
            spot = grid.at[s, c, u, v, z]
            firsts.append([
                remote(blocks.at[s, c, w], spot, sems[0].at[9 * c + k], recv_z.at[s, 1 + c, z], peer)
                for k, (w, peer) in enumerate(zip(zs, z_peers, strict=True))
            ])
            start(firsts[c])
            spot[...] = blocks[s, c, z]
        for c, (u, v, peers) in enumerate([(x, y, y_peers), (y, x, x_peers)]):
            z_arrives(lambda b, c=c, u=u, v=v: grid.at[s, c, u, v, b], recv_z.at[s, 1 + c])
            alongs.append(pushes(grid.at[s, c, u, v], peers, sems, 9 * c + 3))
            start(alongs[c])
        for c, (u, peers) in enumerate([(x, x_peers), (y, y_peers)]):
            received(alongs[c])
            thens.append(pushes(grid.at[s, c, u], peers, sems, 9 * c + 6))
            start(thens[c])
        share = one_hot(index((chol.shape[1], 8), 0) == d * bias.shape[2] + index((chol.shape[1], 8), 1)).astype(F32)
        bias[s] = jnp.dot(total, share, precision=lax.Precision.HIGHEST, preferred_element_type=F32)[:, : bias.shape[2]]
        received(thens[0])
        compact_packed(lambda b, c, e, s=s: grid[s, 0, e, b, c], pot, 0)
        received(thens[1])
        compact_packed(lambda b, c, e, s=s: grid[s, 1, b, e, c], pot, 1)

        term = phi_t[...]
        sum_of = term.astype(F32)
        for order in range(1, ORDER):
            term = (-dot_nt(term, pot[...]) / order).astype(BF16)
            sum_of = sum_of + term.astype(F32)
        if s < STEPS - 1:
            term = (-dot_nt(term, pot[...]) / ORDER).astype(BF16)
            phi_t[...] = (sum_of + term.astype(F32)).astype(BF16)
        else:
            partial[...] = sum_of
            window = pl.ds(pl.multiple_of(LANES * y, LANES), WINDOW)
            term = (-dot_nt(term, pot[window, :]) / ORDER).astype(BF16)
            phi_w = (partial[:, window] + term.astype(F32)).astype(BF16)
        drain = sum(firsts + alongs + thens, to_x)
        led = to_slab + to_sums

    pl.semaphore_wait(ready, len(hi_peers))
    pack_walker(phi_w, picks, packed, missed)
    spot = everyone.at[hi, core, z]
    to_ring = [
        remote(packed.at[b], spot, last_send.at[k], last_recv.at[k], peer)
        for k, ((_, b), peer) in enumerate(zip(ring, ring_peers, strict=True))
    ]
    start(to_ring)
    everyone[hi, core, z] = packed[z]
    sent(drain)

    @pl.when(y == 0)
    def _():
        sent(led)

    received(to_ring)
    mine = everyone.at[:, core]
    to_twin = [remote(mine, mine, last_send.at[15], last_recv.at[15], twin)]
    start(to_twin)
    sent(to_ring)
    received(to_twin)

    chosen = []
    for slot in range(SIDE):
        source = sources[slot]
        chosen.append(everyone[source // 8, source // 4 % 2, source % 4])
    whole = jnp.concatenate(chosen, axis=0)
    rest = out.shape[2] - LANES
    shape = (SIDE * PAD, SIDE * PAD)
    row, col = index(shape, 0), index(shape, 1)
    r = row % PAD
    back = one_hot(index((LANES, rest), 0) % rest == index((LANES, rest), 1))
    lane = index((SIDE * PAD, LANES), 1) // rest
    tail = jnp.zeros((SIDE * PAD, LANES), F32)
    for s in range(4):
        pick = one_hot((row // PAD == col // PAD) & (col % PAD == ROWS + r // 4) & (r % 4 == s) & (r < ROWS))
        tail = tail + jnp.where(lane == s, dot(pick, whole), 0.0)
    tail = dot(tail.astype(BF16), back)
    whole = jnp.concatenate([whole.astype(F32), tail], axis=1).reshape(SIDE, PAD, LANES + rest)
    out[...] = jnp.swapaxes(whole[:, :ROWS, :], 0, 1).astype(BF16)
    flags = everyone[...].reshape(8 * SIDE, PAD, LANES).astype(F32)
    bad = jnp.where((index(flags.shape, 1) == FLAG) & jnp.logical_not(flags == 0.0), 1.0, 0.0)
    missed_out[...] = jnp.max(jnp.max(bad, axis=0), axis=0, keepdims=True)
    sent(to_twin)


def propagate(walkers, chol, noise, sources):
    rows, vecs, orb = chol.shape
    occ = walkers.shape[2]
    dma = pltpu.SemaphoreType.DMA
    vmem = pl.BlockSpec(memory_space=VMEM)
    return pl.pallas_call(
        kernel,
        out_shape=(
            jax.ShapeDtypeStruct((rows, SIDE, occ), BF16),
            jax.ShapeDtypeStruct((STEPS, SIDE, vecs // SIDE**3), F32),
            jax.ShapeDtypeStruct((1, LANES), F32),
        ),
        in_specs=[vmem, pl.BlockSpec(memory_space=pl.ANY), vmem, pl.BlockSpec(memory_space=pltpu.SMEM)],
        out_specs=(vmem, vmem, vmem),
        scratch_shapes=[
            VMEM((rows, vecs, orb), BF16),
            VMEM((SIDE, PAD, occ), BF16),
            VMEM((2, SIDE, SIDE, 2, PAD, occ), BF16),
            VMEM((orb, occ), BF16),
            VMEM((occ, orb), BF16),
            VMEM((STEPS, SIDE, PAD, orb - VIRT), BF16),
            VMEM((STEPS, SIDE, PAD, orb - VIRT), BF16),
            VMEM((1, vecs), F32),
            VMEM((STEPS, SIDE, SIDE, FLAGS + LANES), F32),
            VMEM((STEPS, SIDE, SIDE, FLAGS + LANES), F32),
            VMEM((STEPS, 2, SIDE, PAD, HALF), BF16),
            VMEM((STEPS, 2, SIDE, SIDE, SIDE, PAD, HALF), BF16),
            VMEM((orb, orb), BF16),
            VMEM((occ, orb), F32),
            VMEM((5, SIDE * PAD, WINDOW), BF16),
            VMEM((SIDE, PAD, LANES), BF16),
            VMEM((SIDE, 2, SIDE, PAD, LANES), BF16),
            dma((18,)),
            dma((18,)),
            dma((SIDE,)),
            dma((STEPS, 21)),
            dma((STEPS, 21)),
            dma((STEPS, 3, SIDE)),
            dma((STEPS, 18)),
            dma((STEPS, 7)),
            dma((16,)),
            dma((16,)),
            dma,
            pltpu.SemaphoreType.REGULAR,
        ],
        compiler_params=pltpu.CompilerParams(collective_id=0, has_side_effects=True, vmem_limit_bytes=LIMIT),
        name="propagate",
    )(walkers, chol, noise, sources)


def solve_each(factor, target):
    return jax.scipy.linalg.cho_solve((factor, True), target)


def by_cholesky(walkers, chol_vectors, noise, sources):
    walk_count, row_count, occ_count = walkers.shape
    vec_count, _, orb_count = chol_vectors.shape
    first_row = lax.axis_index("chol") * row_count
    flat_chol = chol_vectors.reshape(vec_count, row_count * orb_count)
    current = walkers
    biases = []
    for step_index in range(STEPS):
        gathered = lax.all_gather(current, "chol", axis=1, tiled=True)
        phi = gathered.astype(F32)
        top_plain = gathered[:, :occ_count, :]
        gram = jnp.einsum("wai,waj->wij", top_plain, top_plain, preferred_element_type=F32)
        factor = jnp.linalg.cholesky(gram)
        inverse = jax.vmap(solve_each)(factor, jnp.swapaxes(phi[:, :occ_count, :], 1, 2))
        inverse_wide = jnp.pad(inverse, ((0, 0), (0, 0), (0, orb_count - occ_count)))
        inverse_cols = lax.dynamic_slice_in_dim(inverse_wide, first_row, row_count, 2)
        theta_slab = jnp.einsum("wja,wai->wji", phi, inverse_cols, precision=lax.Precision.HIGHEST).astype(BF16)
        green = jnp.swapaxes(theta_slab, 1, 2).reshape(walk_count, row_count * orb_count)
        partial_bias = lax.dot_general(green, flat_chol, (((1,), (1,)), ((), ())), preferred_element_type=F32)
        bias_now = SQRT_DT * lax.psum(partial_bias, "chol")
        biases.append(bias_now)
        field = (noise[step_index] - bias_now).astype(BF16)
        potential = SQRT_DT * jnp.dot(field, flat_chol, preferred_element_type=F32)
        potential = potential.reshape(walk_count, row_count, orb_count).astype(BF16)
        total = current.astype(F32)
        term = current
        for order in range(1, ORDER + 1):
            whole = gathered if order == 1 else lax.all_gather(term, "chol", axis=1, tiled=True)
            product = jnp.einsum("wij,wjb->wib", potential, whole, preferred_element_type=F32)
            term = (-product / order).astype(BF16)
            total = total + term.astype(F32)
        current = total.astype(BF16)
    everyone = lax.all_gather(current, "pop", axis=0, tiled=True)
    return everyone[sources], jnp.stack(biases)


def local(walkers, chol_vectors, noise, sources):
    vec_count = chol_vectors.shape[0]
    share = vec_count // lax.axis_size("chol")
    branched, bias, missed = propagate(
        jnp.transpose(walkers, (1, 0, 2)), jnp.transpose(chol_vectors, (1, 0, 2)), noise, sources
    )

    def by_share():
        branched, bias = by_cholesky(walkers, chol_vectors, noise, sources)
        return branched, lax.dynamic_slice_in_dim(bias, lax.axis_index("chol") * share, share, 2)

    return lax.cond(missed[0, 0] == 0.0, lambda: (jnp.transpose(branched, (1, 0, 2)), bias), by_share)


def solution(mesh):
    return jax.shard_map(
        local,
        mesh=mesh,
        in_specs=(P("pop", "chol", None), P(None, "chol", None), P(None, "pop", None), P("pop")),
        out_specs=(P("pop", "chol", None), P(None, "pop", "chol")),
        check_vma=False,
    )
```
